32 devices in a mesh: groups: 2 (over y), seq: 4 (over z), head: 4 (over x, core).
Axes of the slice: x: 2, y: 2, z: 4, core: 2. Of those that a mesh axis runs over, the one named last changes fastest.
Arguments:
- query_latent_rows: bfloat16 [640, 1536], P(('groups', 'seq')), parts along dimension 0, may hold values from -6 to 6
- key_value_latents: bfloat16 [640, 576], P(('groups', 'seq')), parts along dimension 0, may hold values from -500 to 500
- positions: int32 [640], P(('groups', 'seq')), parts along dimension 0, may hold values from 130752 to 131071, as said below
- query_up_weight: bfloat16 [1536, 12288], P('seq', 'head'), may hold values from -0.15625 to 0.15625
- adapter_down_factor: bfloat16 [3072, 64], P(('groups', 'seq')), parts along dimension 0, may hold values from -0.75 to 0.75
- adapter_up_factor: bfloat16 [128, 12288], P('groups', 'head'), parts along dimension 0, may hold values from -0.15625 to 0.15625
- head_key_up_weight: bfloat16 [64, 128, 512], P('head'), may hold values from -0.5 to 0.5
- head_value_up_weight: bfloat16 [64, 512, 128], P('head'), may hold values from -0.25 to 0.25
- output_projection_weight: bfloat16 [8192, 7168], P('head', 'seq'), may hold values from -0.0625 to 0.0625
Outputs:
- merged_weight: bfloat16 [3072, 12288], P(('groups', 'seq'), 'head'), parts along dimension 0
- mixed: bfloat16 [640, 7168], P(('groups', 'head'), 'seq'), parts along dimension 0
The draws below stay inside these ranges and needn't reach their ends.
There are 2 independent parts, one for each index of `groups`. The reference program is written for one: setup_inputs(seed, part) draws one part's arguments, and reference() takes and returns one part's arrays. A program takes and returns all parts, laid end to end along the dimension named above; an argument that names none is the same for every part. Nothing has to cross between parts.
Inputs may be any that keep to these rules, and one draw needn't show every extreme that they name: positions are distinct; each aligned block of 80 rows holds 80 consecutive positions in rising order, and the blocks together cover the last 320 positions of the prompt in an order drawn from the seed.
All inputs are finite; a program needn't handle non-finite values.
Results may differ from the reference program's by a relative error of at most 0.015.
The reference program's roundings to bfloat16 on the way count: a program that leaves them out, or rounds other values in their place, can miss the bound.
Values may be sent and summed in bfloat16 or wider, within the bound.
No kernel may reach another device: no remote copies, remote signals or barrier semaphores. Data moves between devices by JAX's collectives and lax.ppermute only.
A program may use at most 64 MiB of HBM per device.

```python
import math
import jax
import jax.numpy as jnp
from jax import lax

QUERY_LATENT = 1536
HEADS = 64
NOPE = 128
ROPE = 64
KVR = 512
VDIM = 128
D = 7168
ADAPTER_RANK = 64
TOK_DEV = 80
TOKENS = 320
QUERY_UP_COLUMNS = 12288


def draw_positions(key, part):
    order = jax.random.permutation(jax.random.fold_in(key, 11), TOKENS // TOK_DEV)
    begin = 131072 - TOKENS
    index = jnp.arange(TOKENS, dtype=jnp.int32)
    inner = index % TOK_DEV
    block = index // TOK_DEV
    return (begin + order[block] * TOK_DEV + inner).astype(jnp.int32)


def draw_key_value_latents(key, part):
    base = jax.random.normal(jax.random.fold_in(key, 21), (TOKENS, KVR + ROPE), jnp.float32)
    return base.astype(jnp.bfloat16)


def block_levels(own_key, shape, pieces, smallest, largest):
    def one(dim, parts):
        steps = jax.random.uniform(jax.random.fold_in(jax.random.fold_in(own_key, 6), dim), (parts,), jnp.float32, smallest / len(pieces), largest / len(pieces))
        return jnp.repeat(jnp.exp(steps), shape[dim] // parts).reshape((-1,) + (1,) * (len(shape) - dim - 1))

    level = one(*pieces[0])
    for cut in pieces[1:]:
        level = level * one(*cut)
    return level


def bell_draw(stream_key, extent, deviation, reach, cuts=(), kind=jnp.bfloat16):
    values = deviation * jax.random.normal(stream_key, extent, jnp.float32)
    if cuts:
        values = values * block_levels(stream_key, extent, cuts, -0.22, 0.18)
    return jnp.clip(values, -reach, reach).astype(kind)


def setup_inputs(seed: int = 0, part: int = 0) -> dict:
    seeds = jax.random.split(jax.random.key(seed), 10)
    part_keys = jax.random.split(jax.random.fold_in(seeds[9], part), 10)
    query_latent_rows = bell_draw(part_keys[0], (TOKENS, QUERY_LATENT), 1.0, 6.0, ((0, 4),))
    key_value_latents = draw_key_value_latents(jax.random.fold_in(jax.random.fold_in(seeds[9], part), 71), part)
    positions = draw_positions(jax.random.fold_in(jax.random.fold_in(seeds[9], part), 71), part)
    query_up_weight = bell_draw(seeds[3], (QUERY_LATENT, QUERY_UP_COLUMNS), QUERY_LATENT ** -0.5, 0.15625, ((0, 4), (1, 4)))
    adapter_down_factor = bell_draw(part_keys[4], (QUERY_LATENT, ADAPTER_RANK), ADAPTER_RANK ** -0.5, 0.75, ((0, 4),))
    adapter_up_factor = bell_draw(part_keys[5], (ADAPTER_RANK, QUERY_UP_COLUMNS), QUERY_LATENT ** -0.5, 0.15625, ((1, 4),))
    head_key_up_weight = bell_draw(seeds[6], (HEADS, NOPE, KVR), NOPE ** -0.5, 0.5, ((0, 4),))
    head_value_up_weight = bell_draw(seeds[7], (HEADS, KVR, VDIM), KVR ** -0.5, 0.25, ((0, 4),))
    output_projection_weight = bell_draw(seeds[8], (HEADS * VDIM, D), (HEADS * VDIM) ** -0.5, 0.0625, ((0, 4), (1, 4)))
    return dict(query_latent_rows=query_latent_rows, key_value_latents=key_value_latents, positions=positions, query_up_weight=query_up_weight, adapter_down_factor=adapter_down_factor, adapter_up_factor=adapter_up_factor, head_key_up_weight=head_key_up_weight, head_value_up_weight=head_value_up_weight, output_projection_weight=output_projection_weight)


def reference(query_latent_rows, key_value_latents, positions, query_up_weight, adapter_down_factor, adapter_up_factor, head_key_up_weight, head_value_up_weight, output_projection_weight):
    merged_query_weight = (query_up_weight.astype(jnp.float32) + jnp.dot(adapter_down_factor, adapter_up_factor, preferred_element_type=jnp.float32)).astype(jnp.bfloat16)
    queries = jnp.dot(query_latent_rows, merged_query_weight, preferred_element_type=jnp.float32).astype(jnp.bfloat16)
    queries = queries.reshape(TOKENS, HEADS, NOPE + ROPE)
    absorbed = jnp.einsum('thn,hnk->thk', queries[:, :, :NOPE].astype(jnp.float32), head_key_up_weight.astype(jnp.float32)).astype(jnp.bfloat16)
    full_query = jnp.concatenate([absorbed, queries[:, :, NOPE:]], axis=2)
    visible = positions[None, :] <= positions[:, None]
    values = key_value_latents[:, :KVR]
    score_scale = 1.0 / math.sqrt(NOPE + ROPE)

    def one_head(inputs):
        head_query, head_value = inputs
        scores = jnp.dot(head_query, key_value_latents.T, preferred_element_type=jnp.float32) * score_scale
        scores = jnp.where(visible, scores, jnp.float32(-1e+30))
        row_max = lax.optimization_barrier(jnp.max(scores, axis=1, keepdims=True))
        weights = jnp.where(visible, jnp.exp(scores - row_max), jnp.float32(0.0))
        row_sum = lax.optimization_barrier(jnp.sum(weights, axis=1))
        context_output = jnp.dot(weights.astype(jnp.bfloat16), values, preferred_element_type=jnp.float32) / row_sum[:, None]
        context_output = context_output.astype(jnp.bfloat16)
        return jnp.dot(context_output, head_value, preferred_element_type=jnp.float32).astype(jnp.bfloat16)
    per_head = lax.map(one_head, (jnp.transpose(full_query, (1, 0, 2)), head_value_up_weight))
    flattened = jnp.transpose(per_head, (1, 0, 2)).reshape(TOKENS, HEADS * VDIM)
    mixed = jnp.dot(flattened, output_projection_weight, preferred_element_type=jnp.float32).astype(jnp.bfloat16)
    return (merged_query_weight, mixed)
```

```python
import functools
import math

import jax
import jax.numpy as jnp
from jax import lax
from jax.experimental import pallas as pl
from jax.experimental.pallas import tpu as pltpu
from jax.sharding import PartitionSpec as P

CHUNKS = 2
VMEM_BYTES = 50 * 1024 * 1024


def on_device(
    query_latent_rows,
    key_value_latents,
    positions,
    query_up_weight,
    adapter_down_factor,
    adapter_up_factor,
    head_key_up_weight,
    head_value_up_weight,
    output_projection_weight,
):
    merged_query_weight = (
        query_up_weight.astype(jnp.float32)
        + jnp.dot(adapter_down_factor, adapter_up_factor, preferred_element_type=jnp.float32)
    ).astype(jnp.bfloat16)
    tok_rows = query_latent_rows.shape[0]
    queries = jnp.dot(
        query_latent_rows,
        lax.all_gather(merged_query_weight, "seq", axis=0, tiled=True),
        preferred_element_type=jnp.float32,
    )
    heads_dev = head_key_up_weight.shape[0]
    nope_dim = head_key_up_weight.shape[1]
    kv_rank = head_key_up_weight.shape[2]
    lat_width = key_value_latents.shape[1]
    score_scale = 1.0 / math.sqrt(nope_dim + lat_width - kv_rank)
    queries = queries.astype(jnp.bfloat16).reshape(tok_rows, heads_dev, -1)
    absorbed = jnp.einsum(
        "thn,hnk->thk",
        queries[:, :, :nope_dim],
        head_key_up_weight,
        preferred_element_type=jnp.float32,
    ).astype(jnp.bfloat16)
    full_query = jnp.concatenate([absorbed, queries[:, :, nope_dim:]], axis=2).reshape(
        tok_rows * heads_dev, lat_width
    )
    query_pos = jnp.repeat(positions, heads_dev)
    q_count = tok_rows * heads_dev
    row_max = jnp.full((q_count,), -1e30, jnp.float32)
    key_rows = lax.all_gather(key_value_latents, "seq", axis=0, tiled=True)
    key_pos = lax.all_gather(positions, "seq", axis=0, tiled=True)
    visible = key_pos[None, :] <= query_pos[:, None]
    scores = (
        lax.dot_general(
            full_query, key_rows, (((1,), (1,)), ((), ())), preferred_element_type=jnp.float32
        )
        * score_scale
    )
    scores = jnp.where(visible, scores, jnp.float32(-1e30))
    new_max = jnp.maximum(row_max, jnp.max(scores, axis=1))
    weights = jnp.where(visible, jnp.exp(scores - new_max[:, None]), jnp.float32(0.0))
    row_sum = jnp.sum(weights, axis=1)
    running = jnp.dot(
        weights.astype(jnp.bfloat16), key_rows[:, :kv_rank], preferred_element_type=jnp.float32
    )
    row_max, row_sum, running = (new_max, row_sum, running)
    context_output = (
        (running / row_sum[:, None]).astype(jnp.bfloat16).reshape(tok_rows, heads_dev, kv_rank)
    )
    heads_out = (
        jnp.einsum(
            "euw,uwz->euz", context_output, head_value_up_weight, preferred_element_type=jnp.float32
        )
        .astype(jnp.bfloat16)
        .reshape(tok_rows, -1)
    )
    partial_value = jnp.dot(
        lax.all_gather(heads_out, "seq", axis=0, tiled=True),
        output_projection_weight,
        preferred_element_type=jnp.float32,
    )
    mixed = lax.psum_scatter(
        partial_value.astype(jnp.bfloat16), "head", scatter_dimension=0, tiled=True
    )
    return (merged_query_weight, mixed)


def cyclic(n, k):
    return [(i, (i + k) % n) for i in range(n)]


def flipped(n, bit):
    return [(i, i ^ bit) for i in range(n)]


def call(body, outs, blocks, scalars, args, scratch=(), flops=0, moved=0):
    def whole(shape):
        return pl.BlockSpec(tuple(shape), lambda i, sc: (0,) * len(shape))

    return pl.pallas_call(
        body,
        out_shape=outs,
        grid_spec=pltpu.PrefetchScalarGridSpec(
            num_scalar_prefetch=1,
            grid=(1,),
            in_specs=[whole(a.shape) if b is None else b for a, b in zip(args, blocks)],
            out_specs=jax.tree.map(lambda o: whole(o.shape), outs),
            scratch_shapes=list(scratch),
        ),
        compiler_params=pltpu.CompilerParams(vmem_limit_bytes=VMEM_BYTES),
        cost_estimate=pl.CostEstimate(flops=flops, bytes_accessed=moved, transcendentals=0),
    )(scalars, *args)


def unpack_body(n, nh, tok, kq, vq, aq, sc, x_ref, kv_ref, a_ref, *rest):
    stacks, (xo, kvo, ao) = rest[:nh], rest[nh:]
    s, h = sc[0], sc[2]
    kvr = vq * nh
    depth = a_ref.shape[0]
    row = pl.multiple_of(s * tok, 16)
    xo[pl.ds(row, tok), :] = x_ref[...]
    kvo[pl.ds(row, tok), :] = kv_ref[...]
    ao[pl.ds(pl.multiple_of(s * depth, 16), depth), :] = a_ref[...]
    third = aq // 3
    unit = tok + third
    rope = kvo.shape[1] - kvr
    rank = ao.shape[1]
    for j in range(nh):
        hh = h ^ j
        ref = stacks[j]
        for k in range(1, n):
            src = lax.rem(s - k + n, n)
            row = pl.multiple_of(src * tok, 16)
            base = (k - 1) * unit
            xo[pl.ds(row, tok), pl.ds(pl.multiple_of(hh * kq, 128), kq)] = ref[base : base + tok, :kq]
            kvo[pl.ds(row, tok), pl.ds(pl.multiple_of(hh * vq, 128), vq)] = ref[base : base + tok, kq : kq + vq]
            for i in range(3):
                piece = ref[base + tok : base + unit, i * 128 : (i + 1) * 128]
                arow = pl.multiple_of(src * depth + hh * aq + i * third, 16)
                ao[pl.ds(arow, third), :] = piece[:, :rank]
                if j == 0:
                    rows = min(third, tok - i * third)
                    krow = pl.multiple_of(src * tok + i * third, 16)
                    kvo[pl.ds(krow, rows), kvr:] = piece[:rows, rank : rank + rope]


def attend_body(n, nope, scale, sc, x_ref, a_ref, b_ref, w_ref, kv_ref, pr_ref, pc_ref, ku_ref, vu_ref, *rest):
    moved, out, merged = rest[: 2 * (n - 1)], rest[-2], rest[-1]
    s, g = sc[0], sc[1]
    depth = w_ref.shape[0]
    half = depth // 2
    up = b_ref[...]

    def merge(w, begin):
        rows = w.shape[0]
        at = pl.ds(pl.multiple_of(begin, 16), rows)
        add = jnp.dot(a_ref[at, :], up, preferred_element_type=jnp.float32)
        merged[at, :] = (w.astype(jnp.float32) + add).astype(jnp.bfloat16)

    merge(w_ref[...], s * depth)
    for k in range(1, n):
        src = lax.rem(s - k + n, n)
        merge(moved[k - 1][...], src * depth + g * half)
        merge(moved[n - 2 + k][...], src * depth + (1 - g) * half)
    q = jnp.dot(x_ref[...], merged[...], preferred_element_type=jnp.float32)
    heads, kvr = vu_ref.shape[0], vu_ref.shape[1]
    vdim = vu_ref.shape[2]
    width = q.shape[1] // heads
    lat, rope_key = kv_ref[:, :kvr], kv_ref[:, kvr:]
    visible = pr_ref[...] <= pc_ref[...]
    nt = (((1,), (1,)), ((), ()))
    for j in range(heads):
        qn = q[:, j * width : j * width + nope].astype(jnp.bfloat16)
        qr = q[:, j * width + nope : (j + 1) * width].astype(jnp.bfloat16)
        absorbed = jnp.dot(qn, ku_ref[j], preferred_element_type=jnp.float32).astype(jnp.bfloat16)
        scores = lax.dot_general(absorbed, lat, nt, preferred_element_type=jnp.float32)
        scores = scores + lax.dot_general(qr, rope_key, nt, preferred_element_type=jnp.float32)
        scores = jnp.where(visible, scores * scale, jnp.float32(-1e30))
        top = jnp.max(scores, axis=1, keepdims=True)
        e = jnp.where(visible, jnp.exp(scores - top), jnp.float32(0.0))
        total = jnp.sum(e, axis=1, keepdims=True)
        ctx = jnp.dot(e.astype(jnp.bfloat16), lat, preferred_element_type=jnp.float32)
        ctx = (ctx / total).astype(jnp.bfloat16)
        ho = jnp.dot(ctx, vu_ref[j], preferred_element_type=jnp.float32)
        out[:, j * vdim : (j + 1) * vdim] = ho.astype(jnp.bfloat16)


def gather_slots(n, sc, slots, lhs):
    s = sc[0]
    width = slots[0].shape[1]
    for k in range(n):
        src = lax.rem(s - k + n, n)
        lhs[:, pl.ds(pl.multiple_of(src * width, 128), width)] = slots[k][...]


def first_body(n, sc, w_ref, *rest):
    slots, acc, lhs = rest[:n], rest[n], rest[n + 1]
    gather_slots(n, sc, slots, lhs)
    w = w_ref[...].reshape(lhs.shape[1], w_ref.shape[-1])
    acc[...] = jnp.dot(lhs[...], w, preferred_element_type=jnp.float32)


def last_body(n, nh, tok, sc, w_ref, acc, *rest):
    slots, (keep, send), lhs, tot = rest[:n], rest[n : n + 2], rest[n + 2], rest[n + 3]
    gather_slots(n, sc, slots, lhs)
    w = w_ref[...].reshape(lhs.shape[1], w_ref.shape[-1])
    tot[...] = acc[...] + jnp.dot(lhs[...], w, preferred_element_type=jnp.float32)
    core = sc[2] % 2
    for i in range(nh // 2):
        mine = pl.ds(pl.multiple_of((2 * i + core) * tok, 16), tok)
        theirs = pl.ds(pl.multiple_of((2 * i + 1 - core) * tok, 16), tok)
        keep[i * tok : (i + 1) * tok, :] = tot[mine, :]
        send[i * tok : (i + 1) * tok, :] = tot[theirs, :].astype(jnp.bfloat16)


def by_heads(x, kv, pos, wq, down, up, ku, vu, wo):
    n, nh = lax.axis_size("seq"), lax.axis_size("head")
    s, g, h = lax.axis_index("seq"), lax.axis_index("groups"), lax.axis_index("head")
    sc = jnp.stack([s, g, h]).astype(jnp.int32)
    tok, depth = x.shape
    heads, nope, kvr = ku.shape
    vdim = vu.shape[2]
    rope = kv.shape[1] - kvr
    rank = down.shape[1]
    rows, cols = wq.shape
    half = rows // 2
    tokens = n * tok
    mine = heads // n
    per = mine // CHUNKS
    wide = per * (cols // heads)
    bf = jnp.bfloat16

    kq, vq, aq = depth // nh, kvr // nh, rows // nh
    third = aq // 3
    xs = lax.dynamic_slice(x, (0, h * kq), (tok, kq))
    vs = lax.dynamic_slice(kv, (0, h * vq), (tok, vq))
    as_ = lax.dynamic_slice(down, (h * aq, 0), (aq, rank))
    tail = jnp.concatenate([as_, jnp.pad(kv[:, kvr:], ((0, aq - tok), (0, 0)))], axis=1)
    tail = jnp.concatenate([tail[i * third : (i + 1) * third] for i in range(3)], axis=1)
    tail = jnp.pad(tail, ((0, 0), (0, kq + vq - tail.shape[1])))
    pack = jnp.concatenate([jnp.concatenate([xs, vs], axis=1), tail], axis=0)
    packs = [lax.ppermute(pack, "seq", cyclic(n, k)) for k in range(1, n)]
    others = [lax.ppermute(pos, "seq", cyclic(n, k)) for k in range(1, n)]

    received = []
    for c in range(CHUNKS):
        got = []
        for k in range(1, n):
            at = lax.rem(s + k, n) * (mine * (cols // heads)) + c * wide
            piece = lax.dynamic_slice(wq, (g * half, at), (half, wide))
            got.append(lax.ppermute(piece, "seq", cyclic(n, k)))
        received.append(got)
    passed = [[lax.ppermute(p, "groups", cyclic(2, 1)) for p in got] for got in received]

    stack = jnp.concatenate(packs, axis=0)
    bit = 1
    stacks = [stack]
    across = lax.ppermute(stack, "head", flipped(nh, 2))
    stacks = [
        stack,
        lax.ppermute(stack, "head", flipped(nh, 1)),
        across,
        lax.ppermute(across, "head", flipped(nh, 1)),
    ]
    x_all, kv_all, a_all = call(
        functools.partial(unpack_body, n, nh, tok, kq, vq, aq),
        (
            jax.ShapeDtypeStruct((tokens, depth), bf),
            jax.ShapeDtypeStruct((tokens, kv.shape[1]), bf),
            jax.ShapeDtypeStruct((n * rows, rank), bf),
        ),
        [None] * (3 + nh),
        sc,
        [x, kv, down] + stacks,
        moved=4 * x.size * n * 2,
    )
    around = jnp.concatenate([o for o in others[::-1]] + [pos] + [o for o in others[::-1]] + [pos])
    pos_all = lax.dynamic_slice(around, ((n - 1 - s) * tok,), (tokens,))
    pr, pc = pos_all[None, :], pos_all[:, None]

    merged = (
        wq.astype(jnp.float32) + jnp.dot(down, up, preferred_element_type=jnp.float32)
    ).astype(bf)

    scale = 1.0 / math.sqrt(nope + rope)
    slots = []
    for c in range(CHUNKS):
        def column(i, sc, c=c):
            return (0, sc[0] * CHUNKS + c)

        def leading(i, sc, c=c):
            return (sc[0] * CHUNKS + c, 0, 0)

        args = [x_all, a_all, up, wq, kv_all, pr, pc, ku, vu] + received[c] + passed[c]
        blocks = [None] * len(args)
        blocks[2] = pl.BlockSpec((rank, wide), column)
        blocks[3] = pl.BlockSpec((rows, wide), column)
        blocks[7] = pl.BlockSpec((per, nope, kvr), leading)
        blocks[8] = pl.BlockSpec((per, kvr, vdim), leading)
        ho = call(
            functools.partial(attend_body, n, nope, scale),
            jax.ShapeDtypeStruct((tokens, per * vdim), bf),
            blocks,
            sc,
            args,
            scratch=[pltpu.VMEM((n * rows, wide), bf)],
            flops=2 * tokens * per * (depth * wide // per + 2 * nope * kvr + 2 * tokens * kvr),
            moved=4 * n * rows * wide,
        )
        slots.append([ho] + [lax.ppermute(ho, "seq", cyclic(n, k)) for k in range(1, n)])

    w4 = wo.reshape(n, CHUNKS, per * vdim, wo.shape[1])
    wide_out = wo.shape[1]
    acc = None
    for c in range(CHUNKS):
        spec = pl.BlockSpec((n, None, per * vdim, wide_out), lambda i, sc, c=c: (0, c, 0, 0))
        lhs = pltpu.VMEM((tokens, n * per * vdim), bf)
        cost = dict(flops=2 * tokens * n * per * vdim * wide_out, moved=w4.size * 2 // CHUNKS)
        if c < CHUNKS - 1:
            acc = call(
                functools.partial(first_body, n),
                jax.ShapeDtypeStruct((tokens, wide_out), jnp.float32),
                [spec] + [None] * n,
                sc,
                [w4] + slots[c],
                scratch=[lhs],
                **cost,
            )
        else:
            keep, send = call(
                functools.partial(last_body, n, nh, tok),
                (
                    jax.ShapeDtypeStruct((nh // 2 * tok, wide_out), jnp.float32),
                    jax.ShapeDtypeStruct((nh // 2 * tok, wide_out), bf),
                ),
                [spec] + [None] * (n + 1),
                sc,
                [w4, acc] + slots[c],
                scratch=[lhs, pltpu.VMEM((tokens, wide_out), jnp.float32)],
                **cost,
            )
    got = lax.ppermute(send, "head", flipped(nh, 1))
    pair = (keep + got.astype(jnp.float32)).reshape(nh // 2, tok, wide_out)
    side = h // 2
    out = lax.dynamic_index_in_dim(pair, side, 0, keepdims=False)
    away = lax.dynamic_index_in_dim(pair, 1 - side, 0, keepdims=False).astype(bf)
    out = out + lax.ppermute(away, "head", flipped(nh, 2)).astype(jnp.float32)
    return merged, out.astype(bf)


def fits(mesh, heads, tok):
    n, nh = mesh.shape["seq"], mesh.shape["head"]
    return mesh.shape["groups"] == 2 and nh == 4 and heads % (nh * n * CHUNKS) == 0 and tok % 16 == 0


def solution(mesh):
    placed = (
        P(("groups", "seq"), None),
        P(("groups", "seq"), None),
        P(("groups", "seq")),
        P("seq", "head"),
        P(("groups", "seq"), None),
        P("groups", "head"),
        P("head", None, None),
        P("head", None, None),
        P("head", "seq"),
    )

    def local(*args):
        heads = args[6].shape[0] * mesh.shape["head"]
        return (by_heads if fits(mesh, heads, args[0].shape[0]) else on_device)(*args)

    return jax.shard_map(
        local,
        mesh=mesh,
        in_specs=placed,
        out_specs=(P(("groups", "seq"), "head"), P(("groups", "head"), "seq")),
        check_vma=False,
    )
```

```python
import functools
import math

import jax
import jax.numpy as jnp
from jax import lax
from jax.experimental import pallas as pl
from jax.experimental.pallas import tpu as pltpu
from jax.sharding import PartitionSpec as P

CHUNKS = 2
VMEM_BYTES = 50 * 1024 * 1024


def on_device(
    query_latent_rows,
    key_value_latents,
    positions,
    query_up_weight,
    adapter_down_factor,
    adapter_up_factor,
    head_key_up_weight,
    head_value_up_weight,
    output_projection_weight,
):
    merged_query_weight = (
        query_up_weight.astype(jnp.float32)
        + jnp.dot(adapter_down_factor, adapter_up_factor, preferred_element_type=jnp.float32)
    ).astype(jnp.bfloat16)
    tok_rows = query_latent_rows.shape[0]
    queries = jnp.dot(
        query_latent_rows,
        lax.all_gather(merged_query_weight, "seq", axis=0, tiled=True),
        preferred_element_type=jnp.float32,
    )
    heads_dev = head_key_up_weight.shape[0]
    nope_dim = head_key_up_weight.shape[1]
    kv_rank = head_key_up_weight.shape[2]
    lat_width = key_value_latents.shape[1]
    score_scale = 1.0 / math.sqrt(nope_dim + lat_width - kv_rank)
    queries = queries.astype(jnp.bfloat16).reshape(tok_rows, heads_dev, -1)
    absorbed = jnp.einsum(
        "thn,hnk->thk",
        queries[:, :, :nope_dim],
        head_key_up_weight,
        preferred_element_type=jnp.float32,
    ).astype(jnp.bfloat16)
    full_query = jnp.concatenate([absorbed, queries[:, :, nope_dim:]], axis=2).reshape(
        tok_rows * heads_dev, lat_width
    )
    query_pos = jnp.repeat(positions, heads_dev)
    q_count = tok_rows * heads_dev
    row_max = jnp.full((q_count,), -1e30, jnp.float32)
    key_rows = lax.all_gather(key_value_latents, "seq", axis=0, tiled=True)
    key_pos = lax.all_gather(positions, "seq", axis=0, tiled=True)
    visible = key_pos[None, :] <= query_pos[:, None]
    scores = (
        lax.dot_general(
            full_query, key_rows, (((1,), (1,)), ((), ())), preferred_element_type=jnp.float32
        )
        * score_scale
    )
    scores = jnp.where(visible, scores, jnp.float32(-1e30))
    new_max = jnp.maximum(row_max, jnp.max(scores, axis=1))
    weights = jnp.where(visible, jnp.exp(scores - new_max[:, None]), jnp.float32(0.0))
    row_sum = jnp.sum(weights, axis=1)
    running = jnp.dot(
        weights.astype(jnp.bfloat16), key_rows[:, :kv_rank], preferred_element_type=jnp.float32
    )
    row_max, row_sum, running = (new_max, row_sum, running)
    context_output = (
        (running / row_sum[:, None]).astype(jnp.bfloat16).reshape(tok_rows, heads_dev, kv_rank)
    )
    heads_out = (
        jnp.einsum(
            "euw,uwz->euz", context_output, head_value_up_weight, preferred_element_type=jnp.float32
        )
        .astype(jnp.bfloat16)
        .reshape(tok_rows, -1)
    )
    partial_value = jnp.dot(
        lax.all_gather(heads_out, "seq", axis=0, tiled=True),
        output_projection_weight,
        preferred_element_type=jnp.float32,
    )
    mixed = lax.psum_scatter(
        partial_value.astype(jnp.bfloat16), "head", scatter_dimension=0, tiled=True
    )
    return (merged_query_weight, mixed)


def cyclic(n, k):
    return [(i, (i + k) % n) for i in range(n)]


def flipped(n, bit):
    return [(i, i ^ bit) for i in range(n)]


def call(body, outs, args, blocks=None, out_blocks=None, steps=1, scratch=(), flops=0, moved=0):
    whole = pl.BlockSpec(memory_space=pltpu.VMEM)
    blocks = blocks or {}
    return pl.pallas_call(
        body,
        out_shape=outs,
        grid_spec=pltpu.PrefetchScalarGridSpec(
            num_scalar_prefetch=1,
            grid=(steps,),
            in_specs=[blocks.get(i, whole) for i in range(len(args) - 1)],
            out_specs=out_blocks if out_blocks is not None else jax.tree.map(lambda o: whole, outs),
            scratch_shapes=list(scratch),
        ),
        compiler_params=pltpu.CompilerParams(vmem_limit_bytes=VMEM_BYTES),
        cost_estimate=pl.CostEstimate(flops=flops, bytes_accessed=moved, transcendentals=0),
    )(*args)


def three_terms(p):
    out = []
    for _ in range(3):
        t = p.astype(jnp.bfloat16).astype(jnp.float32)
        out.append(t)
        p = p - t
    return out


def pack_body(n, kq, vq, aq, wide, kvr, sc, x_ref, kv_ref, at_ref, pos_ref, w_ref, first, *rest):
    others, turn, turned = rest[:-2], rest[-2], rest[-1]
    h = sc[2]
    tok = x_ref.shape[0]
    rope = kv_ref.shape[1] - kvr
    half = w_ref.shape[0]
    pieces = 1 + len(others)
    turn[...] = jnp.zeros_like(turn)
    turn[:tok, :rope] = kv_ref[:, kvr:].astype(jnp.float32)
    start = pos_ref[0:1, 0:1].astype(jnp.float32)
    for i, t in enumerate(three_terms(start)):
        turn[tok + i : tok + i + 1, :] = jnp.broadcast_to(t, (1, turn.shape[1]))
    turned[...] = turn[...].T
    xs = x_ref[:, pl.ds(pl.multiple_of(h * kq, 128), kq)]
    ats = at_ref[pl.ds(pl.multiple_of(h * aq, 16), aq), :]
    keys = kv_ref[:, pl.ds(pl.multiple_of(h * vq, 128), vq)]
    ropes = turned[pl.ds(pl.multiple_of(h * aq, 16), aq), :].astype(jnp.bfloat16)
    third = (tok + aq) // 3
    tail = jnp.concatenate([keys, ropes], axis=0)
    for j in range(n):
        at = j * pieces * wide
        first[j, :half, :] = w_ref[:, at : at + wide]
        first[j, half : half + tok, :] = xs
        first[j, half + tok : half + tok + aq, :] = ats
        for i in range(3):
            first[j, half + tok + aq :, i * vq : (i + 1) * vq] = tail[i * third : (i + 1) * third]
        for c, other in enumerate(others):
            at = (j * pieces + c + 1) * wide
            other[j] = w_ref[:, at : at + wide]


def split_body(n, half, sc, u_ref, *outs):
    for k in range(1, n):
        src = lax.rem(sc[0] - k + n, n)
        outs[0][k - 1] = u_ref[src, :half]
        if len(outs) > 1:
            outs[1][k - 1] = u_ref[src, half:]


def unpack_body(n, nh, kq, vq, aq, kvr, sc, x_ref, kv_ref, at_ref, pos_ref, *rest):
    stacks, (xo, kvo, ao, bias), turn = rest[:nh], rest[nh : nh + 4], rest[nh + 4]
    s, h = sc[0], sc[2]
    tok, depth = x_ref.shape[0], at_ref.shape[1]
    rope = kv_ref.shape[1] - kvr
    third = (tok + aq) // 3
    tokens = bias.shape[0]
    row = pl.multiple_of(s * tok, 16)
    xo[pl.ds(row, tok), :] = x_ref[...]
    kvo[pl.ds(row, tok), :] = kv_ref[...]
    ao[:, pl.ds(pl.multiple_of(s * depth, 128), depth)] = at_ref[...]
    starts = [(s, pos_ref[0:1, 0:1].astype(jnp.float32))]
    turn[...] = jnp.zeros_like(turn)
    for k in range(1, n):
        src = lax.rem(s - k + n, n)
        rows = pl.ds(pl.multiple_of(src * tok, 16), tok)
        for j in range(nh):
            hh = h ^ j
            got = stacks[j].at[k - 1]
            xo[rows, pl.ds(pl.multiple_of(hh * kq, 128), kq)] = got[:tok, :]
            arow = pl.ds(pl.multiple_of(hh * aq, 16), aq)
            ao[arow, pl.ds(pl.multiple_of(src * depth, 128), depth)] = got[tok : tok + aq, :]
            tail = jnp.concatenate([got[tok + aq :, i * vq : (i + 1) * vq] for i in range(3)], axis=0)
            kvo[rows, pl.ds(pl.multiple_of(hh * vq, 128), vq)] = tail[:tok]
            turn[arow, :] = tail[tok:].astype(jnp.float32)
        turned = turn[...].T
        kvo[rows, kvr:] = turned[:tok, :rope].astype(jnp.bfloat16)
        starts.append((src, turned[tok : tok + 1, :1] + turned[tok + 1 : tok + 2, :1] + turned[tok + 2 : tok + 3, :1]))

    def places(shape, dim):
        index = lax.broadcasted_iota(jnp.int32, shape, dim)
        block = index // tok
        out = (index - block * tok).astype(jnp.float32)
        for src, start in starts:
            out = out + jnp.where(block == src, start, 0.0)
        return out

    seen = places((1, tokens), 1) <= places((tokens, 1), 0)
    bias[...] = jnp.where(seen, 0.0, -1e30)


def attend_body(n, nope, scale, sc, x_ref, at_ref, b_ref, w_ref, kv_ref, bias_ref, ku_ref, vu_ref, u_ref, y_ref, out, raw):
    s, g = sc[0], sc[1]
    depth = w_ref.shape[0]
    half = depth // 2
    raw[pl.ds(pl.multiple_of(s * depth, 16), depth), :] = w_ref[...]
    for k in range(1, n):
        src = lax.rem(s - k + n, n)
        raw[pl.ds(pl.multiple_of(src * depth + g * half, 16), half), :] = u_ref[src, :half]
        raw[pl.ds(pl.multiple_of(src * depth + (1 - g) * half, 16), half), :] = y_ref[k - 1]
    add = lax.dot_general(
        at_ref[...], b_ref[...], (((0,), (0,)), ((), ())), preferred_element_type=jnp.float32
    )
    merged = (raw[...].astype(jnp.float32) + add).astype(jnp.bfloat16)
    q = jnp.dot(x_ref[...], merged, preferred_element_type=jnp.float32)
    heads, kvr, vdim = vu_ref.shape
    width = q.shape[1] // heads
    lat, rope_key = kv_ref[:, :kvr], kv_ref[:, kvr:]
    bias = bias_ref[...]
    nt = (((1,), (1,)), ((), ()))
    for j in range(heads):
        qn = q[:, j * width : j * width + nope].astype(jnp.bfloat16)
        qr = q[:, j * width + nope : (j + 1) * width].astype(jnp.bfloat16)
        absorbed = jnp.dot(qn, ku_ref[j], preferred_element_type=jnp.float32).astype(jnp.bfloat16)
        scores = lax.dot_general(absorbed, lat, nt, preferred_element_type=jnp.float32)
        scores = scores + lax.dot_general(qr, rope_key, nt, preferred_element_type=jnp.float32)
        scores = scores * scale + bias
        top = jnp.max(scores, axis=1, keepdims=True)
        e = jnp.exp(scores - top)
        total = jnp.sum(e, axis=1, keepdims=True)
        ctx = jnp.dot(e.astype(jnp.bfloat16), lat, preferred_element_type=jnp.float32)
        ctx = (ctx / total).astype(jnp.bfloat16)
        ho = jnp.dot(ctx, vu_ref[j], preferred_element_type=jnp.float32)
        out[:, j * vdim : (j + 1) * vdim] = ho.astype(jnp.bfloat16)


def gather_line(x):
    left = lax.ppermute(x, "seq", [(0, 1), (1, 2), (2, 3)])
    right = lax.ppermute(x, "seq", [(1, 0), (2, 1), (3, 2)])
    two = lax.ppermute(x, "seq", cyclic(4, 2))
    three = lax.ppermute(two, "seq", [(2, 3), (1, 0)])
    return [x, left, right, two, three]


def place_line(s, slots, lhs):
    own, left, right, two, three = slots
    width = own.shape[1]

    def put(src, ref):
        lhs[:, pl.ds(pl.multiple_of(src * width, 128), width)] = ref[...]

    put(s, own)
    put(lax.rem(s + 2, 4), two)

    @pl.when(s > 0)
    def _():
        put(s - 1, left)

    @pl.when(s < 3)
    def _():
        put(s + 1, right)

    @pl.when((s == 0) | (s == 3))
    def _():
        put(3 - s, three)


def first_body(sc, w_ref, *rest):
    slots, acc, lhs = rest[:5], rest[5], rest[6]

    @pl.when(pl.program_id(0) == 0)
    def _():
        place_line(sc[0], slots, lhs)

    w = w_ref[...].reshape(lhs.shape[1], w_ref.shape[-1])
    acc[...] = jnp.dot(lhs[...], w, preferred_element_type=jnp.float32)


def last_body(nh, tok, sc, w_ref, acc, *rest):
    slots, (keep, send), lhs, tot = rest[:5], rest[5:7], rest[7], rest[8]

    @pl.when(pl.program_id(0) == 0)
    def _():
        place_line(sc[0], slots, lhs)

    w = w_ref[...].reshape(lhs.shape[1], w_ref.shape[-1])
    tot[...] = acc[...] + jnp.dot(lhs[...], w, preferred_element_type=jnp.float32)
    core = sc[2] % 2
    for i in range(nh // 2):
        mine = pl.ds(pl.multiple_of((2 * i + core) * tok, 16), tok)
        theirs = pl.ds(pl.multiple_of((2 * i + 1 - core) * tok, 16), tok)
        keep[i * tok : (i + 1) * tok, :] = tot[mine, :]
        send[i * tok : (i + 1) * tok, :] = tot[theirs, :].astype(jnp.bfloat16)


def by_heads(x, kv, pos, wq, down, up, ku, vu, wo):
    n, nh = lax.axis_size("seq"), lax.axis_size("head")
    s, g, h = lax.axis_index("seq"), lax.axis_index("groups"), lax.axis_index("head")
    sc = jnp.stack([s, g, h]).astype(jnp.int32)
    bf, f32 = jnp.bfloat16, jnp.float32
    tok, depth = x.shape
    heads, nope, kvr = ku.shape
    vdim = vu.shape[2]
    rope = kv.shape[1] - kvr
    rank = down.shape[1]
    rows, cols = wq.shape
    half = rows // 2
    tokens = n * tok
    per = heads // n // CHUNKS
    wide = per * (cols // heads)
    kq, vq, aq = depth // nh, kvr // nh, rank // nh
    extra = tok + aq + (tok + aq) // 3
    at = down.T
    pos2 = pos[None, :]

    def like(*shape, dtype=bf):
        return jax.ShapeDtypeStruct(shape, dtype)

    units = call(
        functools.partial(pack_body, n, kq, vq, aq, wide, kvr),
        tuple([like(n, half + extra, wide)] + [like(n, half, wide)] * (CHUNKS - 1)),
        [sc, x, kv, at, pos2, wq],
        blocks={4: pl.BlockSpec((half, cols), lambda i, sc: (sc[1], 0))},
        scratch=[pltpu.VMEM((128, 128), f32)] * 2,
        moved=4 * half * cols,
    )
    moved, passed, stack = [], [], None
    for c in range(CHUNKS):
        unit = units[c]
        if c:
            unit, _ = lax.optimization_barrier((unit, moved[c - 1]))
        got = lax.all_to_all(unit, "seq", 0, 0, tiled=True)
        moved.append(got)
        outs = [like(n - 1, half, wide)] + ([] if c else [like(n - 1, extra, wide)])
        outs = call(
            functools.partial(split_body, n, half),
            tuple(outs),
            [sc, got],
            moved=4 * got.size,
        )
        passed.append(lax.ppermute(outs[0], "groups", cyclic(2, 1)))
        if c == 0:
            stack = outs[1]
    across = lax.ppermute(stack, "head", flipped(nh, 2))
    stacks = [
        stack,
        lax.ppermute(stack, "head", flipped(nh, 1)),
        across,
        lax.ppermute(across, "head", flipped(nh, 1)),
    ]
    x_all, kv_all, at_all, bias = call(
        functools.partial(unpack_body, n, nh, kq, vq, aq, kvr),
        (
            like(tokens, depth),
            like(tokens, kvr + rope),
            like(rank, n * rows),
            like(tokens, tokens, dtype=f32),
        ),
        [sc, x, kv, at, pos2] + stacks,
        scratch=[pltpu.VMEM((128, 128), f32)],
        moved=4 * tokens * depth,
    )

    merged = (wq.astype(f32) + jnp.dot(down, up, preferred_element_type=f32)).astype(bf)

    scale = 1.0 / math.sqrt(nope + rope)
    slots = []
    for c in range(CHUNKS):
        def column(i, sc, c=c):
            return (0, sc[0] * CHUNKS + c)

        def leading(i, sc, c=c):
            return (sc[0] * CHUNKS + c, 0, 0)

        ho = call(
            functools.partial(attend_body, n, nope, scale),
            like(tokens, per * vdim),
            [sc, x_all, at_all, up, wq, kv_all, bias, ku, vu, moved[c], passed[c]],
            blocks={
                2: pl.BlockSpec((rank, wide), column),
                3: pl.BlockSpec((rows, wide), column),
                6: pl.BlockSpec((per, nope, kvr), leading),
                7: pl.BlockSpec((per, kvr, vdim), leading),
            },
            scratch=[pltpu.VMEM((n * rows, wide), bf)],
            flops=2 * tokens * per * (depth * wide // per + 2 * nope * kvr + 2 * tokens * kvr),
            moved=4 * n * rows * wide,
        )
        slots.append(gather_line(ho))

    w4 = wo.reshape(n, CHUNKS, per * vdim, wo.shape[1])
    total = wo.shape[1]
    tile = 256
    tiles = total // tile
    lhs = pltpu.VMEM((tokens, n * per * vdim), bf)

    def weights(c, begin):
        return pl.BlockSpec((n, None, per * vdim, tile), lambda i, sc: (0, c, 0, i + begin))

    def band(count, begin=0):
        return pl.BlockSpec((count, tile), lambda i, sc: (0, i + begin))

    cost = dict(flops=2 * tokens * n * per * vdim * total, moved=w4.size * 2 // CHUNKS)
    acc = call(
        first_body,
        like(tokens, total, dtype=f32),
        [sc, w4] + slots[0],
        blocks={0: weights(0, 0)},
        out_blocks=band(tokens),
        steps=tiles,
        scratch=[lhs],
        **cost,
    )
    side = h // 2
    bands = []
    cut = (tiles + 1) // 2
    for begin, count in ((0, cut), (cut, tiles - cut)):
        keep, send = call(
            functools.partial(last_body, nh, tok),
            (
                like(nh // 2 * tok, count * tile, dtype=f32),
                like(nh // 2 * tok, count * tile),
            ),
            [sc, w4, acc] + slots[1],
            blocks={0: weights(1, begin), 1: band(tokens, begin)},
            out_blocks=(band(nh // 2 * tok), band(nh // 2 * tok)),
            steps=count,
            scratch=[lhs, pltpu.VMEM((tokens, tile), f32)],
            flops=cost["flops"] * count // tiles,
            moved=cost["moved"] * count // tiles,
        )
        got = lax.ppermute(send, "head", flipped(nh, 1))
        pair = (keep + got.astype(f32)).reshape(nh // 2, tok, count * tile)
        out = lax.dynamic_index_in_dim(pair, side, 0, keepdims=False)
        away = lax.dynamic_index_in_dim(pair, 1 - side, 0, keepdims=False).astype(bf)
        out = out + lax.ppermute(away, "head", flipped(nh, 2)).astype(f32)
        bands.append(out.astype(bf))
    return merged, jnp.concatenate(bands, axis=1)


def fits(mesh, shapes):
    n, nh = mesh.shape["seq"], mesh.shape["head"]
    x, kv, _, wq, down, _, ku, vu, wo = shapes
    tok, kvr, rank = x[0], ku[2], down[1]
    if mesh.shape["groups"] != 2 or n != 4 or nh != 4 or CHUNKS != 2 or ku[0] % (n * CHUNKS):
        return False
    wide = wq[1] // n // CHUNKS
    return (
        (tok + rank // nh) % 48 == 0
        and tok % 16 == 0
        and tok + 3 <= 128
        and rank <= 128
        and rank // nh % 16 == 0
        and kv[1] - kvr == rank
        and kvr // nh == 128
        and x[1] // nh == wide
        and down[0] == wide
        and wide == 3 * 128
        and wo[1] % 256 == 0
    )


def solution(mesh):
    placed = (
        P(("groups", "seq"), None),
        P(("groups", "seq"), None),
        P(("groups", "seq")),
        P("seq", "head"),
        P(("groups", "seq"), None),
        P("groups", "head"),
        P("head", None, None),
        P("head", None, None),
        P("head", "seq"),
    )

    def local(*args):
        chosen = by_heads if fits(mesh, [a.shape for a in args]) else on_device
        return chosen(*args)

    return jax.shard_map(
        local,
        mesh=mesh,
        in_specs=placed,
        out_specs=(P(("groups", "seq"), "head"), P(("groups", "head"), "seq")),
        check_vma=False,
    )
```

```python
import functools
import math

import jax
import jax.numpy as jnp
from jax import lax
from jax.experimental import pallas as pl
from jax.experimental.pallas import tpu as pltpu
from jax.sharding import PartitionSpec as P

CHUNKS = 2
VMEM_BYTES = 20 * 1024 * 1024
TILE = 512


def on_device(
    query_latent_rows,
    key_value_latents,
    positions,
    query_up_weight,
    adapter_down_factor,
    adapter_up_factor,
    head_key_up_weight,
    head_value_up_weight,
    output_projection_weight,
):
    merged_query_weight = (
        query_up_weight.astype(jnp.float32)
        + jnp.dot(adapter_down_factor, adapter_up_factor, preferred_element_type=jnp.float32)
    ).astype(jnp.bfloat16)
    tok_rows = query_latent_rows.shape[0]
    queries = jnp.dot(
        query_latent_rows,
        lax.all_gather(merged_query_weight, "seq", axis=0, tiled=True),
        preferred_element_type=jnp.float32,
    )
    heads_dev = head_key_up_weight.shape[0]
    nope_dim = head_key_up_weight.shape[1]
    kv_rank = head_key_up_weight.shape[2]
    lat_width = key_value_latents.shape[1]
    score_scale = 1.0 / math.sqrt(nope_dim + lat_width - kv_rank)
    queries = queries.astype(jnp.bfloat16).reshape(tok_rows, heads_dev, -1)
    absorbed = jnp.einsum(
        "thn,hnk->thk",
        queries[:, :, :nope_dim],
        head_key_up_weight,
        preferred_element_type=jnp.float32,
    ).astype(jnp.bfloat16)
    full_query = jnp.concatenate([absorbed, queries[:, :, nope_dim:]], axis=2).reshape(
        tok_rows * heads_dev, lat_width
    )
    query_pos = jnp.repeat(positions, heads_dev)
    q_count = tok_rows * heads_dev
    row_max = jnp.full((q_count,), -1e30, jnp.float32)
    key_rows = lax.all_gather(key_value_latents, "seq", axis=0, tiled=True)
    key_pos = lax.all_gather(positions, "seq", axis=0, tiled=True)
    visible = key_pos[None, :] <= query_pos[:, None]
    scores = (
        lax.dot_general(
            full_query, key_rows, (((1,), (1,)), ((), ())), preferred_element_type=jnp.float32
        )
        * score_scale
    )
    scores = jnp.where(visible, scores, jnp.float32(-1e30))
    new_max = jnp.maximum(row_max, jnp.max(scores, axis=1))
    weights = jnp.where(visible, jnp.exp(scores - new_max[:, None]), jnp.float32(0.0))
    row_sum = jnp.sum(weights, axis=1)
    running = jnp.dot(
        weights.astype(jnp.bfloat16), key_rows[:, :kv_rank], preferred_element_type=jnp.float32
    )
    row_max, row_sum, running = (new_max, row_sum, running)
    context_output = (
        (running / row_sum[:, None]).astype(jnp.bfloat16).reshape(tok_rows, heads_dev, kv_rank)
    )
    heads_out = (
        jnp.einsum(
            "euw,uwz->euz", context_output, head_value_up_weight, preferred_element_type=jnp.float32
        )
        .astype(jnp.bfloat16)
        .reshape(tok_rows, -1)
    )
    partial_value = jnp.dot(
        lax.all_gather(heads_out, "seq", axis=0, tiled=True),
        output_projection_weight,
        preferred_element_type=jnp.float32,
    )
    mixed = lax.psum_scatter(
        partial_value.astype(jnp.bfloat16), "head", scatter_dimension=0, tiled=True
    )
    return (merged_query_weight, mixed)


def cyclic(n, k):
    return [(i, (i + k) % n) for i in range(n)]


def flipped(n, bit):
    return [(i, i ^ bit) for i in range(n)]


def call(body, outs, args, hbm=(), scratch=(), flops=0, moved=0):
    vmem = pl.BlockSpec(memory_space=pltpu.VMEM)
    far = pl.BlockSpec(memory_space=pl.ANY)
    args = [pltpu.with_memory_space_constraint(a, pltpu.HBM) if i in hbm else a for i, a in enumerate(args)]
    return pl.pallas_call(
        body,
        out_shape=outs,
        grid_spec=pltpu.PrefetchScalarGridSpec(
            num_scalar_prefetch=1,
            grid=(1,),
            in_specs=[far if i in hbm else vmem for i in range(1, len(args))],
            out_specs=jax.tree.map(lambda o: vmem, outs),
            scratch_shapes=list(scratch),
        ),
        compiler_params=pltpu.CompilerParams(vmem_limit_bytes=VMEM_BYTES),
        cost_estimate=pl.CostEstimate(flops=flops, bytes_accessed=moved, transcendentals=0),
    )(*args)


def fetch(pairs, sems):
    copies = [pltpu.make_async_copy(a, b, sems.at[i]) for i, (a, b) in enumerate(pairs)]
    for copy in copies:
        copy.start()
    return copies


def three_terms(p):
    out = []
    for _ in range(3):
        t = p.astype(jnp.bfloat16).astype(jnp.float32)
        out.append(t)
        p = p - t
    return out


def pack_body(n, kq, vq, aq, wide, kvr, sc, x_ref, kv_ref, at_ref, pos_ref, w_ref, *rest):
    outs, (xs, kvs, ats, ps, turn, turned, sems) = rest[:CHUNKS], rest[CHUNKS:]
    g, h = sc[1], sc[2]
    tok = x_ref.shape[0]
    rope = kv_ref.shape[1] - kvr
    half = outs[1].shape[1]
    small = [
        (x_ref.at[:, pl.ds(pl.multiple_of(h * kq, 128), kq)], xs),
        (kv_ref, kvs),
        (at_ref.at[pl.ds(pl.multiple_of(h * aq, 16), aq), :], ats),
        (pos_ref, ps),
    ]
    mine = pl.ds(pl.multiple_of(g * half, 16), half)
    large = []
    for c in range(CHUNKS):
        for j in range(n):
            at = (j * CHUNKS + c) * wide
            large.append((w_ref.at[mine, at : at + wide], outs[c].at[j, :half]))
    copies = fetch(small + large, sems)
    turn[...] = jnp.zeros_like(turn)
    for copy in copies[: len(small)]:
        copy.wait()
    turn[:tok, :rope] = kvs[:, kvr:].astype(jnp.float32)
    start = ps[0:1, 0:1].astype(jnp.float32)
    for i, t in enumerate(three_terms(start)):
        turn[tok + i : tok + i + 1, :] = jnp.broadcast_to(t, (1, turn.shape[1]))
    turned[...] = turn[...].T
    keys = kvs[:, pl.ds(pl.multiple_of(h * vq, 128), vq)]
    ropes = turned[pl.ds(pl.multiple_of(h * aq, 16), aq), :].astype(jnp.bfloat16)
    third = (tok + aq) // 3
    tail = jnp.concatenate([keys, ropes], axis=0)
    for j in range(n):
        first = outs[0].at[j]
        first[half : half + tok, :] = xs[...]
        first[half + tok : half + tok + aq, :] = ats[...]
        for i in range(3):
            first[half + tok + aq :, i * vq : (i + 1) * vq] = tail[i * third : (i + 1) * third]
    for copy in copies[len(small) :]:
        copy.wait()


def split_body(n, half, sc, u_ref, *outs):
    for k in range(1, n):
        src = lax.rem(sc[0] - k + n, n)
        outs[0][k - 1] = u_ref[src, :half]
        if len(outs) > 1:
            outs[1][k - 1] = u_ref[src, half:]


def unpack_body(n, nh, kq, vq, aq, kvr, sc, x_ref, kv_ref, at_ref, pos_ref, *rest):
    stacks, (xo, kvo, ao, bias), turn = rest[:nh], rest[nh : nh + 4], rest[nh + 4]
    s, h = sc[0], sc[2]
    tok, depth = x_ref.shape[0], at_ref.shape[1]
    rope = kv_ref.shape[1] - kvr
    third = (tok + aq) // 3
    tokens = bias.shape[0]
    row = pl.multiple_of(s * tok, 16)
    xo[pl.ds(row, tok), :] = x_ref[...]
    kvo[pl.ds(row, tok), :] = kv_ref[...]
    ao[:, pl.ds(pl.multiple_of(s * depth, 128), depth)] = at_ref[...]
    starts = [(s, pos_ref[0:1, 0:1].astype(jnp.float32))]
    turn[...] = jnp.zeros_like(turn)
    for k in range(1, n):
        src = lax.rem(s - k + n, n)
        rows = pl.ds(pl.multiple_of(src * tok, 16), tok)
        for j in range(nh):
            hh = h ^ j
            got = stacks[j].at[k - 1]
            xo[rows, pl.ds(pl.multiple_of(hh * kq, 128), kq)] = got[:tok, :]
            arow = pl.ds(pl.multiple_of(hh * aq, 16), aq)
            ao[arow, pl.ds(pl.multiple_of(src * depth, 128), depth)] = got[tok : tok + aq, :]
            tail = jnp.concatenate([got[tok + aq :, i * vq : (i + 1) * vq] for i in range(3)], axis=0)
            kvo[rows, pl.ds(pl.multiple_of(hh * vq, 128), vq)] = tail[:tok]
            turn[arow, :] = tail[tok:].astype(jnp.float32)
        turned = turn[...].T
        kvo[rows, kvr:] = turned[:tok, :rope].astype(jnp.bfloat16)
        starts.append((src, turned[tok : tok + 1, :1] + turned[tok + 1 : tok + 2, :1] + turned[tok + 2 : tok + 3, :1]))

    def places(shape, dim):
        index = lax.broadcasted_iota(jnp.int32, shape, dim)
        block = index // tok
        out = (index - block * tok).astype(jnp.float32)
        for src, start in starts:
            out = out + jnp.where(block == src, start, 0.0)
        return out

    seen = places((1, tokens), 1) <= places((tokens, 1), 0)
    bias[...] = jnp.where(seen, 0.0, -1e30)


def attend_body(n, nope, scale, c, sc, x_ref, at_ref, kv_ref, bias_ref, u_ref, y_ref, b_ref, w_ref, ku_ref, vu_ref, *rest):
    out, raw, b_own, ku, vu, sems = rest
    s, g = sc[0], sc[1]
    depth = w_ref.shape[0]
    half = depth // 2
    wide = raw.shape[1]
    heads, kvr, vdim = vu.shape
    chunk = s * CHUNKS + c
    columns = pl.ds(pl.multiple_of(chunk * wide, 128), wide)
    copies = fetch(
        [
            (b_ref.at[:, columns], b_own),
            (w_ref.at[:, columns], raw.at[pl.ds(pl.multiple_of(s * depth, 16), depth), :]),
            (ku_ref.at[pl.ds(chunk * heads, heads)], ku),
            (vu_ref.at[pl.ds(chunk * heads, heads)], vu),
        ],
        sems,
    )
    for k in range(1, n):
        src = lax.rem(s - k + n, n)
        raw[pl.ds(pl.multiple_of(src * depth + g * half, 16), half), :] = u_ref[src, :half]
        raw[pl.ds(pl.multiple_of(src * depth + (1 - g) * half, 16), half), :] = y_ref[k - 1]
    for copy in copies:
        copy.wait()
    add = lax.dot_general(
        at_ref[...], b_own[...], (((0,), (0,)), ((), ())), preferred_element_type=jnp.float32
    )
    merged = (raw[...].astype(jnp.float32) + add).astype(jnp.bfloat16)
    q = jnp.dot(x_ref[...], merged, preferred_element_type=jnp.float32)
    width = wide // heads
    lat, rope_key = kv_ref[:, :kvr], kv_ref[:, kvr:]
    bias = bias_ref[...]
    nt = (((1,), (1,)), ((), ()))
    for j in range(heads):
        qn = q[:, j * width : j * width + nope].astype(jnp.bfloat16)
        qr = q[:, j * width + nope : (j + 1) * width].astype(jnp.bfloat16)
        absorbed = jnp.dot(qn, ku[j], preferred_element_type=jnp.float32).astype(jnp.bfloat16)
        scores = lax.dot_general(absorbed, lat, nt, preferred_element_type=jnp.float32)
        scores = scores + lax.dot_general(qr, rope_key, nt, preferred_element_type=jnp.float32)
        scores = scores * scale + bias
        top = jnp.max(scores, axis=1, keepdims=True)
        e = jnp.exp(scores - top)
        total = jnp.sum(e, axis=1, keepdims=True)
        ctx = jnp.dot(e.astype(jnp.bfloat16), lat, preferred_element_type=jnp.float32)
        ctx = (ctx / total).astype(jnp.bfloat16)
        ho = jnp.dot(ctx, vu[j], preferred_element_type=jnp.float32)
        out[:, j * vdim : (j + 1) * vdim] = ho.astype(jnp.bfloat16)


def gather_line(x):
    left = lax.ppermute(x, "seq", [(0, 1), (1, 2), (2, 3)])
    right = lax.ppermute(x, "seq", [(1, 0), (2, 1), (3, 2)])
    two = lax.ppermute(x, "seq", cyclic(4, 2))
    three = lax.ppermute(two, "seq", [(2, 3), (1, 0)])
    return [x, left, right, two, three]


def place_line(s, slots, lhs):
    own, left, right, two, three = slots
    width = own.shape[1]

    def put(src, ref):
        lhs[:, pl.ds(pl.multiple_of(src * width, 128), width)] = ref[...]

    put(s, own)
    put(lax.rem(s + 2, 4), two)

    @pl.when(s > 0)
    def _():
        put(s - 1, left)

    @pl.when(s < 3)
    def _():
        put(s + 1, right)

    @pl.when((s == 0) | (s == 3))
    def _():
        put(3 - s, three)


def first_body(n, sc, *rest):
    slots, (w_ref, acc, kept, lhs, w, sems) = rest[:5], rest[5:]
    width = lhs.shape[1] // n
    pairs = [(w_ref.at[j, 0], w.at[j]) for j in range(n)]
    copies = fetch(pairs + [(w_ref.at[j, 1], kept.at[j]) for j in range(n)], sems)
    place_line(sc[0], slots, lhs)
    total = acc.shape[1]
    for j in range(n):
        copies[j].wait()
    for at in range(0, total, TILE):
        band = slice(at, min(at + TILE, total))
        tile = w[:, :, band]
        tile = tile.reshape(lhs.shape[1], tile.shape[-1])
        acc[:, band] = jnp.dot(lhs[...], tile, preferred_element_type=jnp.float32)
    for copy in copies[n:]:
        copy.wait()


def last_body(nh, tok, begin, sc, w_ref, acc, *rest):
    slots, (keep, send), lhs, tot = rest[:5], rest[5:7], rest[7], rest[8]
    place_line(sc[0], slots, lhs)
    total = keep.shape[1]
    for at in range(0, total, TILE):
        end = min(at + TILE, total)
        w = w_ref[:, :, begin + at : begin + end]
        w = w.reshape(lhs.shape[1], w.shape[-1])
        tot[:, at:end] = acc[:, begin + at : begin + end] + jnp.dot(
            lhs[...], w, preferred_element_type=jnp.float32
        )
    core = sc[2] % 2
    for i in range(nh // 2):
        mine = pl.ds(pl.multiple_of((2 * i + core) * tok, 16), tok)
        theirs = pl.ds(pl.multiple_of((2 * i + 1 - core) * tok, 16), tok)
        keep[i * tok : (i + 1) * tok, :] = tot[mine, :]
        send[i * tok : (i + 1) * tok, :] = tot[theirs, :].astype(jnp.bfloat16)


def by_heads(x, kv, pos, wq, down, up, ku, vu, wo):
    n, nh = lax.axis_size("seq"), lax.axis_size("head")
    s, g, h = lax.axis_index("seq"), lax.axis_index("groups"), lax.axis_index("head")
    sc = jnp.stack([s, g, h]).astype(jnp.int32)
    bf, f32 = jnp.bfloat16, jnp.float32
    tok, depth = x.shape
    heads, nope, kvr = ku.shape
    vdim = vu.shape[2]
    rope = kv.shape[1] - kvr
    rank = down.shape[1]
    rows, cols = wq.shape
    half = rows // 2
    tokens = n * tok
    per = heads // n // CHUNKS
    wide = per * (cols // heads)
    kq, vq, aq = depth // nh, kvr // nh, rank // nh
    extra = tok + aq + (tok + aq) // 3
    at = down.T
    pos2 = pos[None, :]

    def like(*shape, dtype=bf):
        return jax.ShapeDtypeStruct(shape, dtype)

    units = call(
        functools.partial(pack_body, n, kq, vq, aq, wide, kvr),
        tuple([like(n, half + extra, wide)] + [like(n, half, wide)] * (CHUNKS - 1)),
        [sc, x, kv, at, pos2, wq],
        hbm=range(1, 6),
        scratch=[
            pltpu.VMEM((tok, kq), bf),
            pltpu.VMEM(kv.shape, bf),
            pltpu.VMEM((aq, rows), bf),
            pltpu.VMEM(pos2.shape, jnp.int32),
            pltpu.VMEM((128, 128), f32),
            pltpu.VMEM((128, 128), f32),
            pltpu.SemaphoreType.DMA((4 + n * CHUNKS,)),
        ],
        moved=4 * half * cols,
    )
    def exchange(unit):
        return lax.all_to_all(unit, "seq", 0, 0, tiled=True)

    def split(got, *sizes):
        outs = tuple(like(n - 1, size, wide) for size in sizes)
        return call(functools.partial(split_body, n, half), outs, [sc, got], moved=4 * got.size)

    merged = (wq.astype(f32) + jnp.dot(down, up, preferred_element_type=f32)).astype(bf)
    moved = [exchange(units[0])]
    moved[0], merged = lax.optimization_barrier((moved[0], merged))
    later, _ = lax.optimization_barrier((units[1], moved[0]))
    moved.append(exchange(later))
    share, stack = split(moved[0], half, extra)
    passed = [lax.ppermute(share, "groups", cyclic(2, 1))]
    across = lax.ppermute(stack, "head", flipped(nh, 2))
    stacks = [
        stack,
        lax.ppermute(stack, "head", flipped(nh, 1)),
        across,
        lax.ppermute(across, "head", flipped(nh, 1)),
    ]
    moved[1], passed[0], *stacks = lax.optimization_barrier((moved[1], passed[0], *stacks))
    x_all, kv_all, at_all, bias = call(
        functools.partial(unpack_body, n, nh, kq, vq, aq, kvr),
        (
            like(tokens, depth),
            like(tokens, kvr + rope),
            like(rank, n * rows),
            like(tokens, tokens, dtype=f32),
        ),
        [sc, x, kv, at, pos2] + stacks,
        scratch=[pltpu.VMEM((128, 128), f32)],
        moved=4 * tokens * depth,
    )
    (share,) = split(moved[1], half)
    passed.append(lax.ppermute(share, "groups", cyclic(2, 1)))

    scale = 1.0 / math.sqrt(nope + rope)
    slots = []
    for c in range(CHUNKS):
        ho = call(
            functools.partial(attend_body, n, nope, scale, c),
            like(tokens, per * vdim),
            [sc, x_all, at_all, kv_all, bias, moved[c], passed[c], up, wq, ku, vu],
            hbm=range(7, 11),
            scratch=[
                pltpu.VMEM((n * rows, wide), bf),
                pltpu.VMEM((rank, wide), bf),
                pltpu.VMEM((per, nope, kvr), bf),
                pltpu.VMEM((per, kvr, vdim), bf),
                pltpu.SemaphoreType.DMA((4,)),
            ],
            flops=2 * tokens * per * (depth * wide // per + 2 * nope * kvr + 2 * tokens * kvr),
            moved=4 * n * rows * wide,
        )
        slots.append(gather_line(ho))

    w4 = wo.reshape(n, CHUNKS, per * vdim, wo.shape[1])
    total = wo.shape[1]
    lhs = pltpu.VMEM((tokens, n * per * vdim), bf)
    flops = 2 * tokens * n * per * vdim * total
    acc, w_last = call(
        functools.partial(first_body, n),
        (like(tokens, total, dtype=f32), like(n, per * vdim, total)),
        [sc] + slots[0] + [w4],
        hbm=(6,),
        scratch=[
            lhs,
            pltpu.VMEM((n, per * vdim, total), bf),
            pltpu.SemaphoreType.DMA((2 * n,)),
        ],
        flops=flops,
        moved=w4.size,
    )
    side = h // 2
    bands = []
    cut = (total // 128 + 1) // 2 * 128
    for begin, end in ((0, cut), (cut, total)):
        size = end - begin
        keep, send = call(
            functools.partial(last_body, nh, tok, begin),
            (like(nh // 2 * tok, size, dtype=f32), like(nh // 2 * tok, size)),
            [sc, w_last, acc] + slots[1],
            scratch=[lhs, pltpu.VMEM((tokens, size), f32)],
            flops=flops * size // total,
            moved=w4.size * size // total,
        )
        got = lax.ppermute(send, "head", flipped(nh, 1))
        pair = (keep + got.astype(f32)).reshape(nh // 2, tok, size)
        out = lax.dynamic_index_in_dim(pair, side, 0, keepdims=False)
        away = lax.dynamic_index_in_dim(pair, 1 - side, 0, keepdims=False).astype(bf)
        out = out + lax.ppermute(away, "head", flipped(nh, 2)).astype(f32)
        bands.append(out.astype(bf))
    return merged, jnp.concatenate(bands, axis=1)


def fits(mesh, shapes):
    n, nh = mesh.shape["seq"], mesh.shape["head"]
    x, kv, _, wq, down, _, ku, vu, wo = shapes
    tok, kvr, rank = x[0], ku[2], down[1]
    if mesh.shape["groups"] != 2 or n != 4 or nh != 4 or CHUNKS != 2 or ku[0] % (n * CHUNKS):
        return False
    wide = wq[1] // n // CHUNKS
    return (
        (tok + rank // nh) % 48 == 0
        and tok % 16 == 0
        and tok + 3 <= 128
        and rank <= 128
        and rank // nh % 16 == 0
        and kv[1] - kvr == rank
        and kvr // nh == 128
        and x[1] // nh == wide
        and down[0] == wide
        and wide == 3 * 128
        and wo[1] % 128 == 0
    )


def solution(mesh):
    placed = (
        P(("groups", "seq"), None),
        P(("groups", "seq"), None),
        P(("groups", "seq")),
        P("seq", "head"),
        P(("groups", "seq"), None),
        P("groups", "head"),
        P("head", None, None),
        P("head", None, None),
        P("head", "seq"),
    )

    def local(*args):
        chosen = by_heads if fits(mesh, [a.shape for a in args]) else on_device
        return chosen(*args)

    return jax.shard_map(
        local,
        mesh=mesh,
        in_specs=placed,
        out_specs=(P(("groups", "seq"), "head"), P(("groups", "head"), "seq")),
        check_vma=False,
    )
```

```python
import functools
import math

import jax
import jax.numpy as jnp
from jax import lax
from jax.experimental import pallas as pl
from jax.experimental.pallas import tpu as pltpu
from jax.sharding import PartitionSpec as P

CHUNKS = 2
VMEM_BYTES = 20 * 1024 * 1024
TILE = 512
W_PARTS = 4
HEAD_PARTS = 2
PACK_PARTS = 4


def on_device(
    query_latent_rows,
    key_value_latents,
    positions,
    query_up_weight,
    adapter_down_factor,
    adapter_up_factor,
    head_key_up_weight,
    head_value_up_weight,
    output_projection_weight,
):
    merged_query_weight = (
        query_up_weight.astype(jnp.float32)
        + jnp.dot(adapter_down_factor, adapter_up_factor, preferred_element_type=jnp.float32)
    ).astype(jnp.bfloat16)
    tok_rows = query_latent_rows.shape[0]
    queries = jnp.dot(
        query_latent_rows,
        lax.all_gather(merged_query_weight, "seq", axis=0, tiled=True),
        preferred_element_type=jnp.float32,
    )
    heads_dev = head_key_up_weight.shape[0]
    nope_dim = head_key_up_weight.shape[1]
    kv_rank = head_key_up_weight.shape[2]
    lat_width = key_value_latents.shape[1]
    score_scale = 1.0 / math.sqrt(nope_dim + lat_width - kv_rank)
    queries = queries.astype(jnp.bfloat16).reshape(tok_rows, heads_dev, -1)
    absorbed = jnp.einsum(
        "thn,hnk->thk",
        queries[:, :, :nope_dim],
        head_key_up_weight,
        preferred_element_type=jnp.float32,
    ).astype(jnp.bfloat16)
    full_query = jnp.concatenate([absorbed, queries[:, :, nope_dim:]], axis=2).reshape(
        tok_rows * heads_dev, lat_width
    )
    query_pos = jnp.repeat(positions, heads_dev)
    q_count = tok_rows * heads_dev
    row_max = jnp.full((q_count,), -1e30, jnp.float32)
    key_rows = lax.all_gather(key_value_latents, "seq", axis=0, tiled=True)
    key_pos = lax.all_gather(positions, "seq", axis=0, tiled=True)
    visible = key_pos[None, :] <= query_pos[:, None]
    scores = (
        lax.dot_general(
            full_query, key_rows, (((1,), (1,)), ((), ())), preferred_element_type=jnp.float32
        )
        * score_scale
    )
    scores = jnp.where(visible, scores, jnp.float32(-1e30))
    new_max = jnp.maximum(row_max, jnp.max(scores, axis=1))
    weights = jnp.where(visible, jnp.exp(scores - new_max[:, None]), jnp.float32(0.0))
    row_sum = jnp.sum(weights, axis=1)
    running = jnp.dot(
        weights.astype(jnp.bfloat16), key_rows[:, :kv_rank], preferred_element_type=jnp.float32
    )
    row_max, row_sum, running = (new_max, row_sum, running)
    context_output = (
        (running / row_sum[:, None]).astype(jnp.bfloat16).reshape(tok_rows, heads_dev, kv_rank)
    )
    heads_out = (
        jnp.einsum(
            "euw,uwz->euz", context_output, head_value_up_weight, preferred_element_type=jnp.float32
        )
        .astype(jnp.bfloat16)
        .reshape(tok_rows, -1)
    )
    partial_value = jnp.dot(
        lax.all_gather(heads_out, "seq", axis=0, tiled=True),
        output_projection_weight,
        preferred_element_type=jnp.float32,
    )
    mixed = lax.psum_scatter(
        partial_value.astype(jnp.bfloat16), "head", scatter_dimension=0, tiled=True
    )
    return (merged_query_weight, mixed)


def cyclic(n, k):
    return [(i, (i + k) % n) for i in range(n)]


def flipped(n, bit):
    return [(i, i ^ bit) for i in range(n)]


def call(body, outs, args, hbm=(), scratch=(), alias=None, flops=0, moved=0):
    vmem = pl.BlockSpec(memory_space=pltpu.VMEM)
    far = pl.BlockSpec(memory_space=pl.ANY)
    args = [pltpu.with_memory_space_constraint(a, pltpu.HBM) if i in hbm else a for i, a in enumerate(args)]
    return pl.pallas_call(
        body,
        out_shape=outs,
        grid_spec=pltpu.PrefetchScalarGridSpec(
            num_scalar_prefetch=1,
            grid=(1,),
            in_specs=[far if i in hbm else vmem for i in range(1, len(args))],
            out_specs=jax.tree.map(lambda o: vmem, outs),
            scratch_shapes=list(scratch),
        ),
        input_output_aliases=alias or {},
        compiler_params=pltpu.CompilerParams(vmem_limit_bytes=VMEM_BYTES),
        cost_estimate=pl.CostEstimate(flops=flops, bytes_accessed=moved, transcendentals=0),
    )(*args)


def fetch(pairs, sems):
    copies = [pltpu.make_async_copy(a, b, sems.at[i]) for i, (a, b) in enumerate(pairs)]
    for copy in copies:
        copy.start()
    return copies


def three_terms(p):
    out = []
    for _ in range(3):
        t = p.astype(jnp.bfloat16).astype(jnp.float32)
        out.append(t)
        p = p - t
    return out


def pack_body(n, kq, vq, aq, wide, kvr, sc, x_ref, kv_ref, at_ref, pos_ref, w_ref, *rest):
    count = CHUNKS * (n - 1)
    outs, (xs, kvs, ats, ps, turn, turned, sems) = rest[:count], rest[count:]
    s, g, h = sc[0], sc[1], sc[2]
    tok = x_ref.shape[0]
    rope = kv_ref.shape[1] - kvr
    half = outs[-1].shape[0]
    small = [
        (x_ref.at[:, pl.ds(pl.multiple_of(h * kq, 128), kq)], xs),
        (kv_ref, kvs),
        (at_ref.at[pl.ds(pl.multiple_of(h * aq, 16), aq), :], ats),
        (pos_ref, ps),
    ]
    mine = pl.ds(pl.multiple_of(g * half, 16), half)
    large = []
    for c in range(CHUNKS):
        for k in range(1, n):
            chunk = lax.rem(s + k, n) * CHUNKS + c
            columns = pl.ds(pl.multiple_of(chunk * wide, 128), wide)
            large.append((w_ref.at[mine, columns], outs[c * (n - 1) + k - 1].at[:half]))
    copies = fetch(small + large, sems)
    turn[...] = jnp.zeros_like(turn)
    for copy in copies[: len(small)]:
        copy.wait()
    turn[:tok, :rope] = kvs[:, kvr:].astype(jnp.float32)
    start = ps[0:1, 0:1].astype(jnp.float32)
    for i, t in enumerate(three_terms(start)):
        turn[tok + i : tok + i + 1, :] = jnp.broadcast_to(t, (1, turn.shape[1]))
    turned[...] = turn[...].T
    keys = kvs[:, pl.ds(pl.multiple_of(h * vq, 128), vq)]
    ropes = turned[pl.ds(pl.multiple_of(h * aq, 16), aq), :].astype(jnp.bfloat16)
    third = (tok + aq) // 3
    tail = jnp.concatenate([keys, ropes], axis=0)
    for first in outs[: n - 1]:
        first[half : half + tok, :] = xs[...]
        first[half + tok : half + tok + aq, :] = ats[...]
        for i in range(3):
            first[half + tok + aq :, i * vq : (i + 1) * vq] = tail[i * third : (i + 1) * third]
    for copy in copies[len(small) :]:
        copy.wait()


def split_body(n, half, sc, *refs):
    outs = refs[n - 1 :]
    for k in range(n - 1):
        outs[0][k] = refs[k][:half]
        if len(outs) > 1:
            outs[1][k] = refs[k][half:]


def unpack(n, nh, kq, vq, aq, sc, own, units, stacks, outs, turn):
    (x_ref, kv_ref, at_ref, pos_ref), (xo, kvo, ao, bias) = own, outs
    s, h = sc[0], sc[2]
    tok, depth = x_ref.shape[0], at_ref.shape[1]
    kvr = vq * nh
    rope = kv_ref.shape[1] - kvr
    half = units[0].shape[0] - stacks[0].shape[1]
    third = (tok + aq) // 3
    tokens = bias.shape[0]
    row = pl.multiple_of(s * tok, 16)
    xo[pl.ds(row, tok), :] = x_ref[...]
    kvo[pl.ds(row, tok), :] = kv_ref[...]
    ao[:, pl.ds(pl.multiple_of(s * depth, 128), depth)] = at_ref[...]
    starts = [(s, pos_ref[0:1, 0:1].astype(jnp.float32))]
    turn[...] = jnp.zeros_like(turn)
    for k in range(1, n):
        src = lax.rem(s - k + n, n)
        rows = pl.ds(pl.multiple_of(src * tok, 16), tok)
        for j in range(nh):
            hh = h ^ j
            got = stacks[j - 1].at[k - 1] if j else units[k - 1].at[half:]
            xo[rows, pl.ds(pl.multiple_of(hh * kq, 128), kq)] = got[:tok, :]
            arow = pl.ds(pl.multiple_of(hh * aq, 16), aq)
            ao[arow, pl.ds(pl.multiple_of(src * depth, 128), depth)] = got[tok : tok + aq, :]
            tail = jnp.concatenate([got[tok + aq :, i * vq : (i + 1) * vq] for i in range(3)], axis=0)
            kvo[rows, pl.ds(pl.multiple_of(hh * vq, 128), vq)] = tail[:tok]
            turn[arow, :] = tail[tok:].astype(jnp.float32)
        turned = turn[...].T
        kvo[rows, kvr:] = turned[:tok, :rope].astype(jnp.bfloat16)
        terms = [turned[tok + i : tok + i + 1, :1] for i in range(3)]
        starts.append((src, terms[0] + terms[1] + terms[2]))

    def places(shape, dim):
        index = lax.broadcasted_iota(jnp.int32, shape, dim)
        block = index // tok
        out = (index - block * tok).astype(jnp.float32)
        for src, start in starts:
            out = out + jnp.where(block == src, start, 0.0)
        return out

    seen = places((1, tokens), 1) <= places((tokens, 1), 0)
    bias[...] = jnp.where(seen, 0.0, -1e30)


def attend(n, nope, scale, c, sc, shared, units, y_ref, weights, out, scratch, before=None):
    x_ref, kv_ref, at_ref, bias_ref = shared
    b_ref, w_ref, ku_ref, vu_ref = weights
    raw, b_own, ku, vu, sems = scratch
    s, g = sc[0], sc[1]
    depth = w_ref.shape[0]
    half = depth // 2
    wide = raw.shape[1]
    heads, kvr, vdim = vu.shape
    chunk = s * CHUNKS + c
    columns = pl.ds(pl.multiple_of(chunk * wide, 128), wide)
    mine = pl.ds(pl.multiple_of(s * depth, 128), depth)
    b_copy, w_copy, ku_copy, vu_copy = fetch(
        [
            (b_ref.at[:, columns], b_own),
            (w_ref.at[:, columns], raw.at[mine, :]),
            (ku_ref.at[pl.ds(chunk * heads, heads)], ku),
            (vu_ref.at[pl.ds(chunk * heads, heads)], vu),
        ],
        sems,
    )
    if before is not None:
        before()
    for k in range(1, n):
        src = lax.rem(s - k + n, n)
        raw[pl.ds(pl.multiple_of(src * depth + g * half, 16), half), :] = units[k - 1][:half]
        raw[pl.ds(pl.multiple_of(src * depth + (1 - g) * half, 16), half), :] = y_ref[k - 1]
    b_copy.wait()
    w_copy.wait()

    def merge(rows):
        add = lax.dot_general(
            at_ref[:, rows], b_own[...], (((0,), (0,)), ((), ())), preferred_element_type=jnp.float32
        )
        raw[rows, :] = (raw[rows, :].astype(jnp.float32) + add).astype(jnp.bfloat16)

    for src in range(n):
        merge(slice(src * depth, (src + 1) * depth))
    q = jnp.dot(x_ref[...], raw[...], preferred_element_type=jnp.float32)
    ku_copy.wait()
    vu_copy.wait()
    width = wide // heads
    lat, rope_key = kv_ref[:, :kvr], kv_ref[:, kvr:]
    bias = bias_ref[...]
    nt = (((1,), (1,)), ((), ()))
    for j in range(heads):
        qn = q[:, j * width : j * width + nope].astype(jnp.bfloat16)
        qr = q[:, j * width + nope : (j + 1) * width].astype(jnp.bfloat16)
        absorbed = jnp.dot(qn, ku[j], preferred_element_type=jnp.float32).astype(jnp.bfloat16)
        scores = lax.dot_general(absorbed, lat, nt, preferred_element_type=jnp.float32)
        scores = scores + lax.dot_general(qr, rope_key, nt, preferred_element_type=jnp.float32)
        scores = scores * scale + bias
        top = jnp.max(scores, axis=1, keepdims=True)
        e = jnp.exp(scores - top)
        total = jnp.sum(e, axis=1, keepdims=True)
        ctx = jnp.dot(e.astype(jnp.bfloat16), lat, preferred_element_type=jnp.float32)
        ctx = (ctx / total).astype(jnp.bfloat16)
        ho = jnp.dot(ctx, vu[j], preferred_element_type=jnp.float32)
        out[:, j * vdim : (j + 1) * vdim] = ho.astype(jnp.bfloat16)


def attend_first(n, nh, kq, vq, aq, nope, scale, sc, *refs):
    own, units, y_ref, stacks = refs[:4], refs[4 : 3 + n], refs[3 + n], refs[4 + n : 3 + n + nh]
    refs = refs[3 + n + nh :]
    weights, out, shared, turn, scratch = refs[:4], refs[4], refs[5:9], refs[9], refs[10:]

    def before():
        unpack(n, nh, kq, vq, aq, sc, own, units, stacks, shared, turn)

    attend(n, nope, scale, 0, sc, shared, units, y_ref, weights, out, scratch, before)


def attend_next(n, nope, scale, sc, *refs):
    shared, units, refs = refs[:4], refs[4 : 3 + n], refs[3 + n :]
    attend(n, nope, scale, CHUNKS - 1, sc, shared, units, refs[0], refs[1:5], refs[5], refs[6:])


def gather_line(x):
    left = lax.ppermute(x, "seq", [(0, 1), (1, 2), (2, 3)])
    right = lax.ppermute(x, "seq", [(1, 0), (2, 1), (3, 2)])
    two = lax.ppermute(x, "seq", cyclic(4, 2))
    three = lax.ppermute(two, "seq", [(2, 3), (1, 0)])
    return [x, left, right, two, three]


def place_line(s, slots, lhs):
    own, left, right, two, three = slots
    width = own.shape[1]

    def put(src, ref):
        lhs[:, pl.ds(pl.multiple_of(src * width, 128), width)] = ref[...]

    put(s, own)
    put(lax.rem(s + 2, 4), two)

    @pl.when(s > 0)
    def _():
        put(s - 1, left)

    @pl.when(s < 3)
    def _():
        put(s + 1, right)

    @pl.when((s == 0) | (s == 3))
    def _():
        put(3 - s, three)


def columns_dot(lhs, w, begin, end, put):
    for at in range(begin, end, TILE):
        stop = min(at + TILE, end)
        tile = w[:, :, at:stop]
        tile = tile.reshape(lhs.shape[1], tile.shape[-1])
        put(slice(at, stop), jnp.dot(lhs[...], tile, preferred_element_type=jnp.float32))


def first_body(n, cut, sc, *refs):
    slots, (w_ref, acc, later, lhs, w, sems) = refs[:5], refs[5:]
    copies = fetch(
        [(w_ref.at[j, 0], w.at[j]) for j in range(n)]
        + [(w_ref.at[j, 1, :, :cut], later.at[j]) for j in range(n)],
        sems,
    )
    place_line(sc[0], slots, lhs)
    for copy in copies[:n]:
        copy.wait()

    def put(band, value):
        acc[:, band] = value

    columns_dot(lhs, w, 0, acc.shape[1], put)
    for copy in copies[n:]:
        copy.wait()


def last_body(nh, tok, begin, sc, w, acc, slots, keep, send, lhs, tot):
    place_line(sc[0], slots, lhs)

    def put(band, value):
        tot[:, band] = acc[:, begin + band.start : begin + band.stop] + value

    columns_dot(lhs, w, 0, keep.shape[1], put)
    core = sc[2] % 2
    for i in range(nh // 2):
        mine = pl.ds(pl.multiple_of((2 * i + core) * tok, 16), tok)
        theirs = pl.ds(pl.multiple_of((2 * i + 1 - core) * tok, 16), tok)
        keep[i * tok : (i + 1) * tok, :] = tot[mine, :]
        send[i * tok : (i + 1) * tok, :] = tot[theirs, :].astype(jnp.bfloat16)


def last_left(n, nh, tok, sc, *refs):
    slots, (w, acc, w_ref, keep, send, later, lhs, tot, sems) = refs[:5], refs[5:]
    cut = keep.shape[1]
    copies = fetch([(w_ref.at[j, 1, :, cut:], later.at[j]) for j in range(n)], sems)
    last_body(nh, tok, 0, sc, w, acc, slots, keep, send, lhs, tot)
    for copy in copies:
        copy.wait()


def last_right(nh, tok, sc, *refs):
    slots, (w, acc, held, keep, send, passed, lhs, tot) = refs[:5], refs[5:]
    del held, passed
    last_body(nh, tok, acc.shape[1] - keep.shape[1], sc, w, acc, slots, keep, send, lhs, tot)


def by_heads(x, kv, pos, wq, down, up, ku, vu, wo):
    n, nh = lax.axis_size("seq"), lax.axis_size("head")
    s, g, h = lax.axis_index("seq"), lax.axis_index("groups"), lax.axis_index("head")
    sc = jnp.stack([s, g, h]).astype(jnp.int32)
    bf, f32 = jnp.bfloat16, jnp.float32
    tok, depth = x.shape
    heads, nope, kvr = ku.shape
    vdim = vu.shape[2]
    rope = kv.shape[1] - kvr
    rank = down.shape[1]
    rows, cols = wq.shape
    half = rows // 2
    tokens = n * tok
    per = heads // n // CHUNKS
    wide = per * (cols // heads)
    kq, vq, aq = depth // nh, kvr // nh, rank // nh
    extra = tok + aq + (tok + aq) // 3
    at = down.T
    pos2 = pos[None, :]

    def like(*shape, dtype=bf):
        return jax.ShapeDtypeStruct(shape, dtype)

    units = call(
        functools.partial(pack_body, n, kq, vq, aq, wide, kvr),
        tuple([like(half + extra, wide)] * (n - 1) + [like(half, wide)] * (n - 1) * (CHUNKS - 1)),
        [sc, x, kv, at, pos2, wq],
        hbm=range(1, 6),
        scratch=[
            pltpu.VMEM((tok, kq), bf),
            pltpu.VMEM(kv.shape, bf),
            pltpu.VMEM((aq, rows), bf),
            pltpu.VMEM(pos2.shape, jnp.int32),
            pltpu.VMEM((128, 128), f32),
            pltpu.VMEM((128, 128), f32),
            pltpu.SemaphoreType.DMA((4 + (n - 1) * CHUNKS,)),
        ],
        moved=4 * half * cols,
    )
    def exchange(parts):
        return [lax.ppermute(p, "seq", cyclic(n, k)) for p, k in zip(parts, range(1, n))]

    def split(got, *sizes):
        outs = tuple(like(n - 1, size, wide) for size in sizes)
        return call(functools.partial(split_body, n, half), outs, [sc] + got, moved=4 * 3 * got[0].size)

    merged = (wq.astype(f32) + jnp.dot(down, up, preferred_element_type=f32)).astype(bf)
    moved = [exchange(units[: n - 1])]
    *moved[0], merged = lax.optimization_barrier((*moved[0], merged))
    later = lax.optimization_barrier((*units[n - 1 :], moved[0][0]))
    moved.append(exchange(later[: n - 1]))
    share, stack = split(moved[0], half, extra)
    passed = [lax.ppermute(share, "groups", cyclic(2, 1))]
    across = lax.ppermute(stack, "head", flipped(nh, 2))
    across, *moved[1] = lax.optimization_barrier((across, *moved[1]))
    stacks = [
        lax.ppermute(stack, "head", flipped(nh, 1)),
        across,
        lax.ppermute(across, "head", flipped(nh, 1)),
    ]
    (share,) = split(moved[1], half)
    passed.append(lax.ppermute(share, "groups", cyclic(2, 1)))

    scale = 1.0 / math.sqrt(nope + rope)
    scratch = [
        pltpu.VMEM((n * rows, wide), bf),
        pltpu.VMEM((rank, wide), bf),
        pltpu.VMEM((per, nope, kvr), bf),
        pltpu.VMEM((per, kvr, vdim), bf),
        pltpu.SemaphoreType.DMA((4,)),
    ]
    cost = dict(
        flops=2 * tokens * per * (depth * wide // per + 2 * nope * kvr + 2 * tokens * kvr),
        moved=4 * n * rows * wide,
    )
    ho, *shared = call(
        functools.partial(attend_first, n, nh, kq, vq, aq, nope, scale),
        (
            like(tokens, per * vdim),
            like(tokens, depth),
            like(tokens, kvr + rope),
            like(rank, n * rows),
            like(tokens, tokens, dtype=f32),
        ),
        [sc, x, kv, at, pos2] + moved[0] + [passed[0]] + stacks + [up, wq, ku, vu],
        hbm=range(4 + n + nh, 8 + n + nh),
        scratch=[pltpu.VMEM((128, 128), f32)] + scratch,
        **cost,
    )
    slots = [gather_line(ho)]
    ho = call(
        functools.partial(attend_next, n, nope, scale),
        like(tokens, per * vdim),
        [sc] + shared + moved[1] + [passed[1], up, wq, ku, vu],
        hbm=range(5 + n, 9 + n),
        scratch=scratch,
        **cost,
    )
    slots.append(gather_line(ho))

    w4 = wo.reshape(n, CHUNKS, per * vdim, wo.shape[1])
    total = wo.shape[1]
    lhs = pltpu.VMEM((tokens, n * per * vdim), bf)
    flops = 2 * tokens * n * per * vdim * total
    cut = (total // 128 + 1) // 2 * 128
    acc, w_left = call(
        functools.partial(first_body, n, cut),
        (like(tokens, total, dtype=f32), like(n, per * vdim, cut)),
        [sc] + slots[0] + [w4],
        hbm=(6,),
        scratch=[
            lhs,
            pltpu.VMEM((n, per * vdim, total), bf),
            pltpu.SemaphoreType.DMA((2 * n,)),
        ],
        flops=flops,
        moved=w4.size,
    )
    pair_rows = nh // 2 * tok

    def partial_sums(size):
        return (like(pair_rows, size, dtype=f32), like(pair_rows, size))

    keep, send, w_right = call(
        functools.partial(last_left, n, nh, tok),
        partial_sums(cut) + (like(n, per * vdim, total - cut),),
        [sc] + slots[1] + [w_left, acc, w4],
        hbm=(8,),
        scratch=[lhs, pltpu.VMEM((tokens, cut), f32), pltpu.SemaphoreType.DMA((n,))],
        flops=flops // 2,
        moved=w4.size // 2,
    )
    left = send
    keep_right, right, keep = call(
        functools.partial(last_right, nh, tok),
        partial_sums(total - cut) + (like(pair_rows, cut, dtype=f32),),
        [sc] + slots[1] + [w_right, acc, keep],
        scratch=[lhs, pltpu.VMEM((tokens, total - cut), f32)],
        alias={8: 2},
        flops=flops // 2,
        moved=w4.size // 2,
    )
    side = h // 2
    bands = []
    for keep, send in ((keep, left), (keep_right, right)):
        got = lax.ppermute(send, "head", flipped(nh, 1))
        pair = (keep + got.astype(f32)).reshape(nh // 2, tok, keep.shape[1])
        out = lax.dynamic_index_in_dim(pair, side, 0, keepdims=False)
        away = lax.dynamic_index_in_dim(pair, 1 - side, 0, keepdims=False).astype(bf)
        out = out + lax.ppermute(away, "head", flipped(nh, 2)).astype(f32)
        bands.append(out.astype(bf))
    return merged, jnp.concatenate(bands, axis=1)


def fits(mesh, shapes):
    n, nh = mesh.shape["seq"], mesh.shape["head"]
    x, kv, _, wq, down, _, ku, vu, wo = shapes
    tok, kvr, rank = x[0], ku[2], down[1]
    if mesh.shape["groups"] != 2 or n != 4 or nh != 4 or CHUNKS != 2 or ku[0] % (n * CHUNKS):
        return False
    wide = wq[1] // n // CHUNKS
    return (
        (tok + rank // nh) % 48 == 0
        and tok % 16 == 0
        and tok + 3 <= 128
        and rank <= 128
        and rank // nh % 16 == 0
        and kv[1] - kvr == rank
        and kvr // nh == 128
        and x[1] // nh == wide
        and down[0] == wide
        and wide == 3 * 128
        and wo[1] % 128 == 0
    )


def solution(mesh):
    placed = (
        P(("groups", "seq"), None),
        P(("groups", "seq"), None),
        P(("groups", "seq")),
        P("seq", "head"),
        P(("groups", "seq"), None),
        P("groups", "head"),
        P("head", None, None),
        P("head", None, None),
        P("head", "seq"),
    )

    def local(*args):
        chosen = by_heads if fits(mesh, [a.shape for a in args]) else on_device
        return chosen(*args)

    return jax.shard_map(
        local,
        mesh=mesh,
        in_specs=placed,
        out_specs=(P(("groups", "seq"), "head"), P(("groups", "head"), "seq")),
        check_vma=False,
    )
```

```python
import functools
import math

import jax
import jax.numpy as jnp
from jax import lax
from jax.experimental import pallas as pl
from jax.experimental.pallas import tpu as pltpu
from jax.sharding import PartitionSpec as P

CHUNKS = 2
VMEM_BYTES = 20 * 1024 * 1024
TILE = 512
W_PARTS = 4
HEAD_PARTS = 2
PACK_PARTS = 4


def on_device(
    query_latent_rows,
    key_value_latents,
    positions,
    query_up_weight,
    adapter_down_factor,
    adapter_up_factor,
    head_key_up_weight,
    head_value_up_weight,
    output_projection_weight,
):
    merged_query_weight = (
        query_up_weight.astype(jnp.float32)
        + jnp.dot(adapter_down_factor, adapter_up_factor, preferred_element_type=jnp.float32)
    ).astype(jnp.bfloat16)
    tok_rows = query_latent_rows.shape[0]
    queries = jnp.dot(
        query_latent_rows,
        lax.all_gather(merged_query_weight, "seq", axis=0, tiled=True),
        preferred_element_type=jnp.float32,
    )
    heads_dev = head_key_up_weight.shape[0]
    nope_dim = head_key_up_weight.shape[1]
    kv_rank = head_key_up_weight.shape[2]
    lat_width = key_value_latents.shape[1]
    score_scale = 1.0 / math.sqrt(nope_dim + lat_width - kv_rank)
    queries = queries.astype(jnp.bfloat16).reshape(tok_rows, heads_dev, -1)
    absorbed = jnp.einsum(
        "thn,hnk->thk",
        queries[:, :, :nope_dim],
        head_key_up_weight,
        preferred_element_type=jnp.float32,
    ).astype(jnp.bfloat16)
    full_query = jnp.concatenate([absorbed, queries[:, :, nope_dim:]], axis=2).reshape(
        tok_rows * heads_dev, lat_width
    )
    query_pos = jnp.repeat(positions, heads_dev)
    q_count = tok_rows * heads_dev
    row_max = jnp.full((q_count,), -1e30, jnp.float32)
    key_rows = lax.all_gather(key_value_latents, "seq", axis=0, tiled=True)
    key_pos = lax.all_gather(positions, "seq", axis=0, tiled=True)
    visible = key_pos[None, :] <= query_pos[:, None]
    scores = (
        lax.dot_general(
            full_query, key_rows, (((1,), (1,)), ((), ())), preferred_element_type=jnp.float32
        )
        * score_scale
    )
    scores = jnp.where(visible, scores, jnp.float32(-1e30))
    new_max = jnp.maximum(row_max, jnp.max(scores, axis=1))
    weights = jnp.where(visible, jnp.exp(scores - new_max[:, None]), jnp.float32(0.0))
    row_sum = jnp.sum(weights, axis=1)
    running = jnp.dot(
        weights.astype(jnp.bfloat16), key_rows[:, :kv_rank], preferred_element_type=jnp.float32
    )
    row_max, row_sum, running = (new_max, row_sum, running)
    context_output = (
        (running / row_sum[:, None]).astype(jnp.bfloat16).reshape(tok_rows, heads_dev, kv_rank)
    )
    heads_out = (
        jnp.einsum(
            "euw,uwz->euz", context_output, head_value_up_weight, preferred_element_type=jnp.float32
        )
        .astype(jnp.bfloat16)
        .reshape(tok_rows, -1)
    )
    partial_value = jnp.dot(
        lax.all_gather(heads_out, "seq", axis=0, tiled=True),
        output_projection_weight,
        preferred_element_type=jnp.float32,
    )
    mixed = lax.psum_scatter(
        partial_value.astype(jnp.bfloat16), "head", scatter_dimension=0, tiled=True
    )
    return (merged_query_weight, mixed)


def flipped(n, bit):
    return [(i, i ^ bit) for i in range(n)]


def partners(n):
    return [b for b in range(2, n)] + [1]


def call(body, outs, args, hbm=(), scratch=(), alias=None, flops=0, moved=0):
    vmem = pl.BlockSpec(memory_space=pltpu.VMEM)
    far = pl.BlockSpec(memory_space=pl.ANY)
    args = [pltpu.with_memory_space_constraint(a, pltpu.HBM) if i in hbm else a for i, a in enumerate(args)]
    return pl.pallas_call(
        body,
        out_shape=outs,
        grid_spec=pltpu.PrefetchScalarGridSpec(
            num_scalar_prefetch=1,
            grid=(1,),
            in_specs=[far if i in hbm else vmem for i in range(1, len(args))],
            out_specs=jax.tree.map(lambda o: vmem, outs),
            scratch_shapes=list(scratch),
        ),
        input_output_aliases=alias or {},
        compiler_params=pltpu.CompilerParams(vmem_limit_bytes=VMEM_BYTES),
        cost_estimate=pl.CostEstimate(flops=flops, bytes_accessed=moved, transcendentals=0),
    )(*args)


def fetch(pairs, sems):
    copies = [pltpu.make_async_copy(a, b, sems.at[i]) for i, (a, b) in enumerate(pairs)]
    for copy in copies:
        copy.start()
    return copies


def three_terms(p):
    out = []
    for _ in range(3):
        t = p.astype(jnp.bfloat16).astype(jnp.float32)
        out.append(t)
        p = p - t
    return out


def pack_body(n, kq, vq, aq, wide, kvr, sc, x_ref, kv_ref, at_ref, pos_ref, w_ref, *rest):
    count = CHUNKS * (n - 1)
    outs, (xs, kvs, ats, ps, turn, turned, sems) = rest[:count], rest[count:]
    s, g, h = sc[0], sc[1], sc[2]
    tok = x_ref.shape[0]
    rope = kv_ref.shape[1] - kvr
    half = outs[-1].shape[0]
    small = [
        (x_ref.at[:, pl.ds(pl.multiple_of(h * kq, 128), kq)], xs),
        (kv_ref, kvs),
        (at_ref.at[pl.ds(pl.multiple_of(h * aq, 16), aq), :], ats),
        (pos_ref, ps),
    ]
    mine = pl.ds(pl.multiple_of(g * half, 16), half)
    large = []
    for c in range(CHUNKS):
        for k, bits in enumerate(partners(n)):
            chunk = (s ^ bits) * CHUNKS + c
            columns = pl.ds(pl.multiple_of(chunk * wide, 128), wide)
            large.append((w_ref.at[mine, columns], outs[c * (n - 1) + k].at[:half]))
    copies = fetch(small + large, sems)
    turn[...] = jnp.zeros_like(turn)
    for copy in copies[: len(small)]:
        copy.wait()
    turn[:tok, :rope] = kvs[:, kvr:].astype(jnp.float32)
    start = ps[0:1, 0:1].astype(jnp.float32)
    for i, t in enumerate(three_terms(start)):
        turn[tok + i : tok + i + 1, :] = jnp.broadcast_to(t, (1, turn.shape[1]))
    turned[...] = turn[...].T
    keys = kvs[:, pl.ds(pl.multiple_of(h * vq, 128), vq)]
    ropes = turned[pl.ds(pl.multiple_of(h * aq, 16), aq), :].astype(jnp.bfloat16)
    third = (tok + aq) // 3
    tail = jnp.concatenate([keys, ropes], axis=0)
    for first in outs[: n - 1]:
        first[half : half + tok, :] = xs[...]
        first[half + tok : half + tok + aq, :] = ats[...]
        for i in range(3):
            first[half + tok + aq :, i * vq : (i + 1) * vq] = tail[i * third : (i + 1) * third]
    for copy in copies[len(small) :]:
        copy.wait()


def split_body(n, half, sc, *refs):
    outs = refs[n - 1 :]
    for k in range(n - 1):
        outs[0][k] = refs[k][:half]
        if len(outs) > 1:
            outs[1][k] = refs[k][half:]


def unpack(n, nh, kq, vq, aq, sc, own, units, stacks, outs, turn):
    (x_ref, kv_ref, at_ref, pos_ref), (xo, kvo, ao, bias) = own, outs
    s, h = sc[0], sc[2]
    tok, depth = x_ref.shape[0], at_ref.shape[1]
    kvr = vq * nh
    rope = kv_ref.shape[1] - kvr
    half = units[0].shape[0] - stacks[0].shape[1]
    third = (tok + aq) // 3
    tokens = bias.shape[0]
    row = pl.multiple_of(s * tok, 16)
    xo[pl.ds(row, tok), :] = x_ref[...]
    kvo[pl.ds(row, tok), :] = kv_ref[...]
    ao[:, pl.ds(pl.multiple_of(s * depth, 128), depth)] = at_ref[...]
    starts = [(s, pos_ref[0:1, 0:1].astype(jnp.float32))]
    turn[...] = jnp.zeros_like(turn)
    for k, bits in enumerate(partners(n)):
        src = s ^ bits
        rows = pl.ds(pl.multiple_of(src * tok, 16), tok)
        for j in range(nh):
            hh = h ^ j
            got = stacks[j - 1].at[k] if j else units[k].at[half:]
            xo[rows, pl.ds(pl.multiple_of(hh * kq, 128), kq)] = got[:tok, :]
            arow = pl.ds(pl.multiple_of(hh * aq, 16), aq)
            ao[arow, pl.ds(pl.multiple_of(src * depth, 128), depth)] = got[tok : tok + aq, :]
            tail = jnp.concatenate([got[tok + aq :, i * vq : (i + 1) * vq] for i in range(3)], axis=0)
            kvo[rows, pl.ds(pl.multiple_of(hh * vq, 128), vq)] = tail[:tok]
            turn[arow, :] = tail[tok:].astype(jnp.float32)
        turned = turn[...].T
        kvo[rows, kvr:] = turned[:tok, :rope].astype(jnp.bfloat16)
        terms = [turned[tok + i : tok + i + 1, :1] for i in range(3)]
        starts.append((src, terms[0] + terms[1] + terms[2]))

    def places(shape, dim):
        index = lax.broadcasted_iota(jnp.int32, shape, dim)
        block = index // tok
        out = (index - block * tok).astype(jnp.float32)
        for src, start in starts:
            out = out + jnp.where(block == src, start, 0.0)
        return out

    seen = places((1, tokens), 1) <= places((tokens, 1), 0)
    bias[...] = jnp.where(seen, 0.0, -1e30)


def attend(n, nope, scale, c, sc, shared, units, y_ref, weights, out, scratch, before=None):
    x_ref, kv_ref, at_ref, bias_ref = shared
    b_ref, w_ref, ku_ref, vu_ref = weights
    raw, b_own, ku, vu, sems = scratch
    s, g = sc[0], sc[1]
    depth = w_ref.shape[0]
    half = depth // 2
    wide = raw.shape[1]
    heads, kvr, vdim = vu.shape
    chunk = s * CHUNKS + c
    columns = pl.ds(pl.multiple_of(chunk * wide, 128), wide)
    mine = pl.ds(pl.multiple_of(s * depth, 128), depth)
    b_copy, w_copy, ku_copy, vu_copy = fetch(
        [
            (b_ref.at[:, columns], b_own),
            (w_ref.at[:, columns], raw.at[mine, :]),
            (ku_ref.at[pl.ds(chunk * heads, heads)], ku),
            (vu_ref.at[pl.ds(chunk * heads, heads)], vu),
        ],
        sems,
    )
    if before is not None:
        before()
    for k, bits in enumerate(partners(n)):
        src = s ^ bits
        raw[pl.ds(pl.multiple_of(src * depth + g * half, 16), half), :] = units[k][:half]
        raw[pl.ds(pl.multiple_of(src * depth + (1 - g) * half, 16), half), :] = y_ref[k]
    b_copy.wait()
    w_copy.wait()

    def merge(rows):
        add = lax.dot_general(
            at_ref[:, rows], b_own[...], (((0,), (0,)), ((), ())), preferred_element_type=jnp.float32
        )
        raw[rows, :] = (raw[rows, :].astype(jnp.float32) + add).astype(jnp.bfloat16)

    for src in range(n):
        merge(slice(src * depth, (src + 1) * depth))
    q = jnp.dot(x_ref[...], raw[...], preferred_element_type=jnp.float32)
    ku_copy.wait()
    vu_copy.wait()
    width = wide // heads
    lat, rope_key = kv_ref[:, :kvr], kv_ref[:, kvr:]
    bias = bias_ref[...]
    nt = (((1,), (1,)), ((), ()))
    for j in range(heads):
        qn = q[:, j * width : j * width + nope].astype(jnp.bfloat16)
        qr = q[:, j * width + nope : (j + 1) * width].astype(jnp.bfloat16)
        absorbed = jnp.dot(qn, ku[j], preferred_element_type=jnp.float32).astype(jnp.bfloat16)
        scores = lax.dot_general(absorbed, lat, nt, preferred_element_type=jnp.float32)
        scores = scores + lax.dot_general(qr, rope_key, nt, preferred_element_type=jnp.float32)
        scores = scores * scale + bias
        top = jnp.max(scores, axis=1, keepdims=True)
        e = jnp.exp(scores - top)
        total = jnp.sum(e, axis=1, keepdims=True)
        ctx = jnp.dot(e.astype(jnp.bfloat16), lat, preferred_element_type=jnp.float32)
        ctx = (ctx / total).astype(jnp.bfloat16)
        ho = jnp.dot(ctx, vu[j], preferred_element_type=jnp.float32)
        out[:, j * vdim : (j + 1) * vdim] = ho.astype(jnp.bfloat16)


def attend_first(n, nh, kq, vq, aq, nope, scale, sc, *refs):
    own, units, y_ref, stacks = refs[:4], refs[4 : 3 + n], refs[3 + n], refs[4 + n : 3 + n + nh]
    refs = refs[3 + n + nh :]
    weights, out, shared, turn, scratch = refs[:4], refs[4], refs[5:9], refs[9], refs[10:]

    def before():
        unpack(n, nh, kq, vq, aq, sc, own, units, stacks, shared, turn)

    attend(n, nope, scale, 0, sc, shared, units, y_ref, weights, out, scratch, before)


def attend_next(n, nope, scale, sc, *refs):
    shared, units, refs = refs[:4], refs[4 : 3 + n], refs[3 + n :]
    attend(n, nope, scale, CHUNKS - 1, sc, shared, units, refs[0], refs[1:5], refs[5], refs[6:])


def gather_line(x):
    two = lax.ppermute(x, "seq", flipped(4, 2))
    one = lax.ppermute(x, "seq", flipped(4, 1))
    two, one = lax.optimization_barrier((two, one))
    return [x, one, two, lax.ppermute(two, "seq", flipped(4, 1))]


EARLY = ((0, 0), (1, 0), (2, 0), (0, 1))
LATE = ((3, 0), (1, 1), (2, 1), (3, 1))


def place(slots, lhs):
    for i, ref in enumerate(slots):
        width = ref.shape[1]
        lhs[:, i * width : (i + 1) * width] = ref[...]


def slabs(sc, w_ref, pieces, columns, out):
    return [(w_ref.at[sc[0] ^ bits, c, :, columns], out.at[i]) for i, (bits, c) in enumerate(pieces)]


def columns_dot(lhs, w, begin, end, put):
    for at in range(begin, end, TILE):
        stop = min(at + TILE, end)
        tile = w[:, :, at:stop]
        tile = tile.reshape(lhs.shape[1], tile.shape[-1])
        put(slice(at, stop), jnp.dot(lhs[...], tile, preferred_element_type=jnp.float32))


def first_body(cut, sc, *refs):
    count = len(EARLY)
    slots, (w_ref, acc, left, right, lhs, w, sems) = refs[:count], refs[count:]
    copies = fetch(
        slabs(sc, w_ref, EARLY, slice(None), w)
        + slabs(sc, w_ref, LATE, slice(0, cut), left)
        + slabs(sc, w_ref, LATE, slice(cut, acc.shape[1]), right),
        sems,
    )
    place(slots, lhs)
    for copy in copies[:count]:
        copy.wait()

    def put(band, value):
        acc[:, band] = value

    columns_dot(lhs, w, 0, acc.shape[1], put)
    for copy in copies[count:]:
        copy.wait()


def last_body(nh, tok, begin, sc, w, acc, slots, keep, send, lhs, tot):
    place(slots, lhs)

    def put(band, value):
        tot[:, band] = acc[:, begin + band.start : begin + band.stop] + value

    columns_dot(lhs, w, 0, keep.shape[1], put)
    core = sc[2] % 2
    for i in range(nh // 2):
        mine = pl.ds(pl.multiple_of((2 * i + core) * tok, 16), tok)
        theirs = pl.ds(pl.multiple_of((2 * i + 1 - core) * tok, 16), tok)
        keep[i * tok : (i + 1) * tok, :] = tot[mine, :]
        send[i * tok : (i + 1) * tok, :] = tot[theirs, :].astype(jnp.bfloat16)


def last_left(nh, tok, sc, *refs):
    count = len(LATE)
    slots, (w, acc, held, keep, send, passed, lhs, tot) = refs[:count], refs[count:]
    del held, passed
    last_body(nh, tok, 0, sc, w, acc, slots, keep, send, lhs, tot)


def last_right(nh, tok, sc, *refs):
    count = len(LATE)
    slots, (w, acc, held, keep, send, passed, lhs, tot) = refs[:count], refs[count:]
    del held, passed
    last_body(nh, tok, acc.shape[1] - keep.shape[1], sc, w, acc, slots, keep, send, lhs, tot)


def by_heads(x, kv, pos, wq, down, up, ku, vu, wo):
    n, nh = lax.axis_size("seq"), lax.axis_size("head")
    s, g, h = lax.axis_index("seq"), lax.axis_index("groups"), lax.axis_index("head")
    sc = jnp.stack([s, g, h]).astype(jnp.int32)
    bf, f32 = jnp.bfloat16, jnp.float32
    tok, depth = x.shape
    heads, nope, kvr = ku.shape
    vdim = vu.shape[2]
    rope = kv.shape[1] - kvr
    rank = down.shape[1]
    rows, cols = wq.shape
    half = rows // 2
    tokens = n * tok
    per = heads // n // CHUNKS
    wide = per * (cols // heads)
    kq, vq, aq = depth // nh, kvr // nh, rank // nh
    extra = tok + aq + (tok + aq) // 3
    at = down.T
    pos2 = pos[None, :]

    def like(*shape, dtype=bf):
        return jax.ShapeDtypeStruct(shape, dtype)

    units = call(
        functools.partial(pack_body, n, kq, vq, aq, wide, kvr),
        tuple([like(half + extra, wide)] * (n - 1) + [like(half, wide)] * (n - 1) * (CHUNKS - 1)),
        [sc, x, kv, at, pos2, wq],
        hbm=range(1, 6),
        scratch=[
            pltpu.VMEM((tok, kq), bf),
            pltpu.VMEM(kv.shape, bf),
            pltpu.VMEM((aq, rows), bf),
            pltpu.VMEM(pos2.shape, jnp.int32),
            pltpu.VMEM((128, 128), f32),
            pltpu.VMEM((128, 128), f32),
            pltpu.SemaphoreType.DMA((4 + (n - 1) * CHUNKS,)),
        ],
        moved=4 * half * cols,
    )
    def exchange(parts):
        return [lax.ppermute(p, "seq", flipped(n, bits)) for p, bits in zip(parts, partners(n))]

    def split(got, *sizes):
        outs = tuple(like(n - 1, size, wide) for size in sizes)
        return call(functools.partial(split_body, n, half), outs, [sc] + got, moved=4 * 3 * got[0].size)

    merged = (wq.astype(f32) + jnp.dot(down, up, preferred_element_type=f32)).astype(bf)
    moved = [exchange(units[: n - 1])]
    *moved[0], merged = lax.optimization_barrier((*moved[0], merged))
    later = lax.optimization_barrier((*units[n - 1 :], moved[0][0]))
    moved.append(exchange(later[: n - 1]))
    share, stack = split(moved[0], half, extra)
    passed = [lax.ppermute(share, "groups", flipped(2, 1))]
    across = lax.ppermute(stack, "head", flipped(nh, 2))
    across, *moved[1] = lax.optimization_barrier((across, *moved[1]))
    stacks = [
        lax.ppermute(stack, "head", flipped(nh, 1)),
        across,
        lax.ppermute(across, "head", flipped(nh, 1)),
    ]
    (share,) = split(moved[1], half)
    passed.append(lax.ppermute(share, "groups", flipped(2, 1)))

    scale = 1.0 / math.sqrt(nope + rope)
    scratch = [
        pltpu.VMEM((n * rows, wide), bf),
        pltpu.VMEM((rank, wide), bf),
        pltpu.VMEM((per, nope, kvr), bf),
        pltpu.VMEM((per, kvr, vdim), bf),
        pltpu.SemaphoreType.DMA((4,)),
    ]
    cost = dict(
        flops=2 * tokens * per * (depth * wide // per + 2 * nope * kvr + 2 * tokens * kvr),
        moved=4 * n * rows * wide,
    )
    ho, *shared = call(
        functools.partial(attend_first, n, nh, kq, vq, aq, nope, scale),
        (
            like(tokens, per * vdim),
            like(tokens, depth),
            like(tokens, kvr + rope),
            like(rank, n * rows),
            like(tokens, tokens, dtype=f32),
        ),
        [sc, x, kv, at, pos2] + moved[0] + [passed[0]] + stacks + [up, wq, ku, vu],
        hbm=range(4 + n + nh, 8 + n + nh),
        scratch=[pltpu.VMEM((128, 128), f32)] + scratch,
        **cost,
    )
    slots = [gather_line(ho)]
    ho = call(
        functools.partial(attend_next, n, nope, scale),
        like(tokens, per * vdim),
        [sc] + shared + moved[1] + [passed[1], up, wq, ku, vu],
        hbm=range(5 + n, 9 + n),
        scratch=scratch,
        **cost,
    )
    slots.append(gather_line(ho))

    w4 = wo.reshape(n, CHUNKS, per * vdim, wo.shape[1])
    total = wo.shape[1]
    early, late = ([slots[c][bits] for bits, c in pieces] for pieces in (EARLY, LATE))
    lhs = pltpu.VMEM((tokens, n * per * vdim), bf)
    flops = 2 * tokens * n * per * vdim * total
    cut = (total // 128 + 1) // 2 * 128
    acc, w_left, w_right = call(
        functools.partial(first_body, cut),
        (
            like(tokens, total, dtype=f32),
            like(n, per * vdim, cut),
            like(n, per * vdim, total - cut),
        ),
        [sc] + early + [w4],
        hbm=(5,),
        scratch=[
            lhs,
            pltpu.VMEM((n, per * vdim, total), bf),
            pltpu.SemaphoreType.DMA((3 * n,)),
        ],
        flops=flops,
        moved=w4.size,
    )
    pair_rows = nh // 2 * tok

    def partial_sums(size):
        return (like(pair_rows, size, dtype=f32), like(pair_rows, size))

    keep, send, w_right = call(
        functools.partial(last_left, nh, tok),
        partial_sums(cut) + (like(n, per * vdim, total - cut),),
        [sc] + late + [w_left, acc, w_right],
        scratch=[lhs, pltpu.VMEM((tokens, cut), f32)],
        alias={7: 2},
        flops=flops // 2,
        moved=w4.size // 2,
    )
    left = send
    keep_right, right, keep = call(
        functools.partial(last_right, nh, tok),
        partial_sums(total - cut) + (like(pair_rows, cut, dtype=f32),),
        [sc] + late + [w_right, acc, keep],
        scratch=[lhs, pltpu.VMEM((tokens, total - cut), f32)],
        alias={7: 2},
        flops=flops // 2,
        moved=w4.size // 2,
    )
    side = h // 2
    bands = []
    for keep, send in ((keep, left), (keep_right, right)):
        got = lax.ppermute(send, "head", flipped(nh, 1))
        pair = (keep + got.astype(f32)).reshape(nh // 2, tok, keep.shape[1])
        out = lax.dynamic_index_in_dim(pair, side, 0, keepdims=False)
        away = lax.dynamic_index_in_dim(pair, 1 - side, 0, keepdims=False).astype(bf)
        out = out + lax.ppermute(away, "head", flipped(nh, 2)).astype(f32)
        bands.append(out.astype(bf))
    return merged, jnp.concatenate(bands, axis=1)


def fits(mesh, shapes):
    n, nh = mesh.shape["seq"], mesh.shape["head"]
    x, kv, _, wq, down, _, ku, vu, wo = shapes
    tok, kvr, rank = x[0], ku[2], down[1]
    if mesh.shape["groups"] != 2 or n != 4 or nh != 4 or CHUNKS != 2 or ku[0] % (n * CHUNKS):
        return False
    wide = wq[1] // n // CHUNKS
    return (
        (tok + rank // nh) % 48 == 0
        and tok % 16 == 0
        and tok + 3 <= 128
        and rank <= 128
        and rank // nh % 16 == 0
        and kv[1] - kvr == rank
        and kvr // nh == 128
        and x[1] // nh == wide
        and down[0] == wide
        and wide == 3 * 128
        and wo[1] % 128 == 0
    )


def solution(mesh):
    placed = (
        P(("groups", "seq"), None),
        P(("groups", "seq"), None),
        P(("groups", "seq")),
        P("seq", "head"),
        P(("groups", "seq"), None),
        P("groups", "head"),
        P("head", None, None),
        P("head", None, None),
        P("head", "seq"),
    )

    def local(*args):
        chosen = by_heads if fits(mesh, [a.shape for a in args]) else on_device
        return chosen(*args)

    return jax.shard_map(
        local,
        mesh=mesh,
        in_specs=placed,
        out_specs=(P(("groups", "seq"), "head"), P(("groups", "head"), "seq")),
        check_vma=False,
    )
```

```python
import functools
import math

import jax
import jax.numpy as jnp
from jax import lax
from jax.experimental import pallas as pl
from jax.experimental.pallas import tpu as pltpu
from jax.sharding import PartitionSpec as P

CHUNKS = 2
VMEM_BYTES = 20 * 1024 * 1024
TILE = 512
W_PARTS = 4
HEAD_PARTS = 2
PACK_PARTS = 4


def on_device(
    query_latent_rows,
    key_value_latents,
    positions,
    query_up_weight,
    adapter_down_factor,
    adapter_up_factor,
    head_key_up_weight,
    head_value_up_weight,
    output_projection_weight,
):
    merged_query_weight = (
        query_up_weight.astype(jnp.float32)
        + jnp.dot(adapter_down_factor, adapter_up_factor, preferred_element_type=jnp.float32)
    ).astype(jnp.bfloat16)
    tok_rows = query_latent_rows.shape[0]
    queries = jnp.dot(
        query_latent_rows,
        lax.all_gather(merged_query_weight, "seq", axis=0, tiled=True),
        preferred_element_type=jnp.float32,
    )
    heads_dev = head_key_up_weight.shape[0]
    nope_dim = head_key_up_weight.shape[1]
    kv_rank = head_key_up_weight.shape[2]
    lat_width = key_value_latents.shape[1]
    score_scale = 1.0 / math.sqrt(nope_dim + lat_width - kv_rank)
    queries = queries.astype(jnp.bfloat16).reshape(tok_rows, heads_dev, -1)
    absorbed = jnp.einsum(
        "thn,hnk->thk",
        queries[:, :, :nope_dim],
        head_key_up_weight,
        preferred_element_type=jnp.float32,
    ).astype(jnp.bfloat16)
    full_query = jnp.concatenate([absorbed, queries[:, :, nope_dim:]], axis=2).reshape(
        tok_rows * heads_dev, lat_width
    )
    query_pos = jnp.repeat(positions, heads_dev)
    q_count = tok_rows * heads_dev
    row_max = jnp.full((q_count,), -1e30, jnp.float32)
    key_rows = lax.all_gather(key_value_latents, "seq", axis=0, tiled=True)
    key_pos = lax.all_gather(positions, "seq", axis=0, tiled=True)
    visible = key_pos[None, :] <= query_pos[:, None]
    scores = (
        lax.dot_general(
            full_query, key_rows, (((1,), (1,)), ((), ())), preferred_element_type=jnp.float32
        )
        * score_scale
    )
    scores = jnp.where(visible, scores, jnp.float32(-1e30))
    new_max = jnp.maximum(row_max, jnp.max(scores, axis=1))
    weights = jnp.where(visible, jnp.exp(scores - new_max[:, None]), jnp.float32(0.0))
    row_sum = jnp.sum(weights, axis=1)
    running = jnp.dot(
        weights.astype(jnp.bfloat16), key_rows[:, :kv_rank], preferred_element_type=jnp.float32
    )
    row_max, row_sum, running = (new_max, row_sum, running)
    context_output = (
        (running / row_sum[:, None]).astype(jnp.bfloat16).reshape(tok_rows, heads_dev, kv_rank)
    )
    heads_out = (
        jnp.einsum(
            "euw,uwz->euz", context_output, head_value_up_weight, preferred_element_type=jnp.float32
        )
        .astype(jnp.bfloat16)
        .reshape(tok_rows, -1)
    )
    partial_value = jnp.dot(
        lax.all_gather(heads_out, "seq", axis=0, tiled=True),
        output_projection_weight,
        preferred_element_type=jnp.float32,
    )
    mixed = lax.psum_scatter(
        partial_value.astype(jnp.bfloat16), "head", scatter_dimension=0, tiled=True
    )
    return (merged_query_weight, mixed)


def flipped(n, bit):
    return [(i, i ^ bit) for i in range(n)]


def partners(n):
    return [b for b in range(2, n)] + [1]


def call(body, outs, args, hbm=(), scratch=(), alias=None, flops=0, moved=0):
    vmem = pl.BlockSpec(memory_space=pltpu.VMEM)
    far = pl.BlockSpec(memory_space=pl.ANY)
    args = [pltpu.with_memory_space_constraint(a, pltpu.HBM) if i in hbm else a for i, a in enumerate(args)]
    return pl.pallas_call(
        body,
        out_shape=outs,
        grid_spec=pltpu.PrefetchScalarGridSpec(
            num_scalar_prefetch=1,
            grid=(1,),
            in_specs=[far if i in hbm else vmem for i in range(1, len(args))],
            out_specs=jax.tree.map(lambda o: vmem, outs),
            scratch_shapes=list(scratch),
        ),
        input_output_aliases=alias or {},
        compiler_params=pltpu.CompilerParams(vmem_limit_bytes=VMEM_BYTES),
        cost_estimate=pl.CostEstimate(flops=flops, bytes_accessed=moved, transcendentals=0),
    )(*args)


def fetch(pairs, sems):
    copies = [pltpu.make_async_copy(a, b, sems.at[i]) for i, (a, b) in enumerate(pairs)]
    for copy in copies:
        copy.start()
    return copies


def three_terms(p):
    out = []
    for _ in range(3):
        t = p.astype(jnp.bfloat16).astype(jnp.float32)
        out.append(t)
        p = p - t
    return out


def pack_body(n, kq, vq, aq, wide, kvr, sc, x_ref, kv_ref, at_ref, pos_ref, w_ref, *rest):
    count = CHUNKS * (n - 1)
    outs, (xs, kvs, ats, ps, turn, turned, sems) = rest[:count], rest[count:]
    s, g, h = sc[0], sc[1], sc[2]
    tok = x_ref.shape[0]
    rope = kv_ref.shape[1] - kvr
    half = outs[-1].shape[0]
    small = [
        (x_ref.at[:, pl.ds(pl.multiple_of(h * kq, 128), kq)], xs),
        (kv_ref, kvs),
        (at_ref.at[pl.ds(pl.multiple_of(h * aq, 16), aq), :], ats),
        (pos_ref, ps),
    ]
    mine = pl.ds(pl.multiple_of(g * half, 16), half)
    large = []
    for c in range(CHUNKS):
        for k, bits in enumerate(partners(n)):
            chunk = (s ^ bits) * CHUNKS + c
            columns = pl.ds(pl.multiple_of(chunk * wide, 128), wide)
            large.append((w_ref.at[mine, columns], outs[c * (n - 1) + k].at[:half]))
    copies = fetch(small + large, sems)
    turn[...] = jnp.zeros_like(turn)
    for copy in copies[: len(small)]:
        copy.wait()
    turn[:tok, :rope] = kvs[:, kvr:].astype(jnp.float32)
    start = ps[0:1, 0:1].astype(jnp.float32)
    for i, t in enumerate(three_terms(start)):
        turn[tok + i : tok + i + 1, :] = jnp.broadcast_to(t, (1, turn.shape[1]))
    turned[...] = turn[...].T
    keys = kvs[:, pl.ds(pl.multiple_of(h * vq, 128), vq)]
    ropes = turned[pl.ds(pl.multiple_of(h * aq, 16), aq), :].astype(jnp.bfloat16)
    third = (tok + aq) // 3
    tail = jnp.concatenate([keys, ropes], axis=0)
    for first in outs[: n - 1]:
        first[half : half + tok, :] = xs[...]
        first[half + tok : half + tok + aq, :] = ats[...]
        for i in range(3):
            first[half + tok + aq :, i * vq : (i + 1) * vq] = tail[i * third : (i + 1) * third]
    for copy in copies[len(small) :]:
        copy.wait()


def split_body(n, half, sc, *refs):
    outs = refs[n - 1 :]
    for k in range(n - 1):
        outs[0][k] = refs[k][:half]
        if len(outs) > 1:
            outs[1][k] = refs[k][half:]


def unpack(n, nh, kq, vq, aq, sc, own, units, stacks, outs, turn):
    (x_ref, kv_ref, at_ref, pos_ref), (xo, kvo, ao, bias) = own, outs
    s, h = sc[0], sc[2]
    tok, depth = x_ref.shape[0], at_ref.shape[1]
    kvr = vq * nh
    rope = kv_ref.shape[1] - kvr
    half = units[0].shape[0] - stacks[0].shape[1]
    third = (tok + aq) // 3
    tokens = bias.shape[0]
    row = pl.multiple_of(s * tok, 16)
    xo[pl.ds(row, tok), :] = x_ref[...]
    kvo[pl.ds(row, tok), :] = kv_ref[...]
    ao[:, pl.ds(pl.multiple_of(s * depth, 128), depth)] = at_ref[...]
    starts = [(s, pos_ref[0:1, 0:1].astype(jnp.float32))]
    turn[...] = jnp.zeros_like(turn)
    for k, bits in enumerate(partners(n)):
        src = s ^ bits
        rows = pl.ds(pl.multiple_of(src * tok, 16), tok)
        for j in range(nh):
            hh = h ^ j
            got = stacks[j - 1].at[k] if j else units[k].at[half:]
            xo[rows, pl.ds(pl.multiple_of(hh * kq, 128), kq)] = got[:tok, :]
            arow = pl.ds(pl.multiple_of(hh * aq, 16), aq)
            ao[arow, pl.ds(pl.multiple_of(src * depth, 128), depth)] = got[tok : tok + aq, :]
            tail = jnp.concatenate([got[tok + aq :, i * vq : (i + 1) * vq] for i in range(3)], axis=0)
            kvo[rows, pl.ds(pl.multiple_of(hh * vq, 128), vq)] = tail[:tok]
            turn[arow, :] = tail[tok:].astype(jnp.float32)
        turned = turn[...].T
        kvo[rows, kvr:] = turned[:tok, :rope].astype(jnp.bfloat16)
        terms = [turned[tok + i : tok + i + 1, :1] for i in range(3)]
        starts.append((src, terms[0] + terms[1] + terms[2]))

    def places(shape, dim):
        index = lax.broadcasted_iota(jnp.int32, shape, dim)
        block = index // tok
        out = (index - block * tok).astype(jnp.float32)
        for src, start in starts:
            out = out + jnp.where(block == src, start, 0.0)
        return out

    seen = places((1, tokens), 1) <= places((tokens, 1), 0)
    bias[...] = jnp.where(seen, 0.0, -1e30)


def own_weights(sc, c, weights, outs):
    b_ref, w_ref, ku_ref, vu_ref = weights
    b, w, ku, vu = outs
    wide, heads = w.shape[1], ku.shape[0]
    chunk = sc[0] * CHUNKS + c
    columns = pl.ds(pl.multiple_of(chunk * wide, 128), wide)
    return [
        (b_ref.at[:, columns], b),
        (w_ref.at[:, columns], w),
        (ku_ref.at[pl.ds(chunk * heads, heads)], ku),
        (vu_ref.at[pl.ds(chunk * heads, heads)], vu),
    ]


def attend(n, nope, scale, sc, shared, units, ys, weights, out, raw, before=None, copies=()):
    x_ref, kv_ref, at_ref, bias_ref = shared
    b_own, w_own, ku, vu = weights
    s, g = sc[0], sc[1]
    depth, wide = w_own.shape
    half = depth // 2
    heads, kvr, vdim = vu.shape
    if before is not None:
        before()
    for k, bits in enumerate(partners(n)):
        src = s ^ bits
        raw[pl.ds(pl.multiple_of(src * depth + g * half, 16), half), :] = units[k][:half]
        raw[pl.ds(pl.multiple_of(src * depth + (1 - g) * half, 16), half), :] = ys[k][...]
    for copy in copies[:2]:
        copy.wait()
    raw[pl.ds(pl.multiple_of(s * depth, 16), depth), :] = w_own[...]

    def merge(rows):
        add = lax.dot_general(
            at_ref[:, rows], b_own[...], (((0,), (0,)), ((), ())), preferred_element_type=jnp.float32
        )
        raw[rows, :] = (raw[rows, :].astype(jnp.float32) + add).astype(jnp.bfloat16)

    for src in range(n):
        merge(slice(src * depth, (src + 1) * depth))
    q = jnp.dot(x_ref[...], raw[...], preferred_element_type=jnp.float32)
    for copy in copies[2:]:
        copy.wait()
    width = wide // heads
    lat, rope_key = kv_ref[:, :kvr], kv_ref[:, kvr:]
    bias = bias_ref[...]
    nt = (((1,), (1,)), ((), ()))
    for j in range(heads):
        qn = q[:, j * width : j * width + nope].astype(jnp.bfloat16)
        qr = q[:, j * width + nope : (j + 1) * width].astype(jnp.bfloat16)
        absorbed = jnp.dot(qn, ku[j], preferred_element_type=jnp.float32).astype(jnp.bfloat16)
        scores = lax.dot_general(absorbed, lat, nt, preferred_element_type=jnp.float32)
        scores = scores + lax.dot_general(qr, rope_key, nt, preferred_element_type=jnp.float32)
        scores = scores * scale + bias
        top = jnp.max(scores, axis=1, keepdims=True)
        e = jnp.exp(scores - top)
        total = jnp.sum(e, axis=1, keepdims=True)
        ctx = jnp.dot(e.astype(jnp.bfloat16), lat, preferred_element_type=jnp.float32)
        ctx = (ctx / total).astype(jnp.bfloat16)
        ho = jnp.dot(ctx, vu[j], preferred_element_type=jnp.float32)
        out[:, j * vdim : (j + 1) * vdim] = ho.astype(jnp.bfloat16)


def attend_first(n, nh, kq, vq, aq, nope, scale, sc, *refs):
    own, units, y_ref, stacks = refs[:4], refs[4 : 3 + n], refs[3 + n], refs[4 + n : 3 + n + nh]
    refs = refs[3 + n + nh :]
    far, out, shared, later = refs[:4], refs[4], refs[5:9], refs[9:13]
    turn, raw, weights, sems = refs[13], refs[14], refs[15:19], refs[19]
    copies = fetch(own_weights(sc, 0, far, weights) + own_weights(sc, CHUNKS - 1, far, later), sems)

    def before():
        unpack(n, nh, kq, vq, aq, sc, own, units, stacks, shared, turn)

    ys = [y_ref.at[k] for k in range(n - 1)]
    attend(n, nope, scale, sc, shared, units, ys, weights, out, raw, before, copies[:4])
    for copy in copies[4:]:
        copy.wait()


def attend_next(n, nope, scale, sc, *refs):
    shared, units, ys, refs = refs[:4], refs[4 : 3 + n], refs[3 + n : 2 + 2 * n], refs[2 + 2 * n :]
    attend(n, nope, scale, sc, shared, units, ys, refs[:4], refs[4], refs[5])


def gather_line(x, *held):
    two = lax.ppermute(x, "seq", flipped(4, 2))
    one = lax.ppermute(x, "seq", flipped(4, 1))
    two, one, *held = lax.optimization_barrier((two, one) + held)
    return [x, one, two, lax.ppermute(two, "seq", flipped(4, 1))] + held


EARLY = ((0, 0), (1, 0), (2, 0), (0, 1))
MIDDLE = ((3, 0), (1, 1), (2, 1))
LATE = ((3, 1),)


def place(slots, lhs):
    for i, ref in enumerate(slots):
        width = ref.shape[1]
        lhs[:, i * width : (i + 1) * width] = ref[...]


def slabs(sc, w_ref, pieces, columns, out):
    return [(w_ref.at[sc[0] ^ bits, c, :, columns], out.at[i]) for i, (bits, c) in enumerate(pieces)]


def columns_dot(lhs, w, begin, end, put):
    for at in range(begin, end, TILE):
        stop = min(at + TILE, end)
        tile = w[:, :, at:stop]
        tile = tile.reshape(-1, tile.shape[-1])
        put(slice(at, stop), jnp.dot(lhs[...], tile, preferred_element_type=jnp.float32))


def early_body(sc, *refs):
    count = len(EARLY)
    slots, (w_ref, acc, token, lhs, w, sems) = refs[:count], refs[count:]
    copies = fetch(slabs(sc, w_ref, EARLY, slice(None), w), sems)
    place(slots, lhs)
    token[...] = jnp.zeros_like(token)
    for copy in copies:
        copy.wait()

    def put(band, value):
        acc[:, band] = value

    columns_dot(lhs, w, 0, acc.shape[1], put)


def middle_body(sc, *refs):
    count = len(MIDDLE)
    slots, (w_ref, before, token, acc, last, lhs, w, sems) = refs[:count], refs[count:]
    del before, token
    total = acc.shape[1]
    copies = fetch(
        slabs(sc, w_ref, MIDDLE, slice(None), w) + slabs(sc, w_ref, LATE, slice(None), last), sems
    )
    place(slots, lhs)
    for copy in copies[:count]:
        copy.wait()

    def add(band, value):
        acc[:, band] += value

    columns_dot(lhs, w, 0, total, add)
    for copy in copies[count:]:
        copy.wait()


def last_body(nh, tok, sc, *refs):
    slots, (w, acc, keep, send, lhs, tot) = refs[: len(LATE)], refs[len(LATE) :]
    place(slots, lhs)

    def put(band, value):
        tot[:, band] = acc[:, band] + value

    columns_dot(lhs, w, 0, keep.shape[1], put)
    core = sc[2] % 2
    for i in range(nh // 2):
        mine = pl.ds(pl.multiple_of((2 * i + core) * tok, 16), tok)
        theirs = pl.ds(pl.multiple_of((2 * i + 1 - core) * tok, 16), tok)
        keep[i * tok : (i + 1) * tok, :] = tot[mine, :]
        send[i * tok : (i + 1) * tok, :] = tot[theirs, :].astype(jnp.bfloat16)


def by_heads(x, kv, pos, wq, down, up, ku, vu, wo):
    n, nh = lax.axis_size("seq"), lax.axis_size("head")
    s, g, h = lax.axis_index("seq"), lax.axis_index("groups"), lax.axis_index("head")
    sc = jnp.stack([s, g, h]).astype(jnp.int32)
    bf, f32 = jnp.bfloat16, jnp.float32
    tok, depth = x.shape
    heads, nope, kvr = ku.shape
    vdim = vu.shape[2]
    rope = kv.shape[1] - kvr
    rank = down.shape[1]
    rows, cols = wq.shape
    half = rows // 2
    tokens = n * tok
    per = heads // n // CHUNKS
    wide = per * (cols // heads)
    kq, vq, aq = depth // nh, kvr // nh, rank // nh
    extra = tok + aq + (tok + aq) // 3
    at = down.T
    pos2 = pos[None, :]

    def like(*shape, dtype=bf):
        return jax.ShapeDtypeStruct(shape, dtype)

    units = call(
        functools.partial(pack_body, n, kq, vq, aq, wide, kvr),
        tuple([like(half + extra, wide)] * (n - 1) + [like(half, wide)] * (n - 1) * (CHUNKS - 1)),
        [sc, x, kv, at, pos2, wq],
        hbm=range(1, 6),
        scratch=[
            pltpu.VMEM((tok, kq), bf),
            pltpu.VMEM(kv.shape, bf),
            pltpu.VMEM((aq, rows), bf),
            pltpu.VMEM(pos2.shape, jnp.int32),
            pltpu.VMEM((128, 128), f32),
            pltpu.VMEM((128, 128), f32),
            pltpu.SemaphoreType.DMA((4 + (n - 1) * CHUNKS,)),
        ],
        moved=4 * half * cols,
    )
    def exchange(parts):
        return [lax.ppermute(p, "seq", flipped(n, bits)) for p, bits in zip(parts, partners(n))]

    def split(got, *sizes):
        outs = tuple(like(n - 1, size, wide) for size in sizes)
        return call(functools.partial(split_body, n, half), outs, [sc] + got, moved=4 * 3 * got[0].size)

    merged = (wq.astype(f32) + jnp.dot(down, up, preferred_element_type=f32)).astype(bf)
    moved = [exchange(units[: n - 1])]
    *moved[0], merged = lax.optimization_barrier((*moved[0], merged))
    later = lax.optimization_barrier((*units[n - 1 :], moved[0][0]))
    moved.append(exchange(later[: n - 1]))
    share, stack = split(moved[0], half, extra)
    passed = [[lax.ppermute(share, "groups", flipped(2, 1))]]
    across = lax.ppermute(stack, "head", flipped(nh, 2))
    across, *moved[1] = lax.optimization_barrier((across, *moved[1]))
    stacks = [
        lax.ppermute(stack, "head", flipped(nh, 1)),
        across,
        lax.ppermute(across, "head", flipped(nh, 1)),
    ]
    passed.append([lax.ppermute(p, "groups", flipped(2, 1)) for p in moved[1]])

    scale = 1.0 / math.sqrt(nope + rope)
    shapes = ((rank, wide), (rows, wide), (per, nope, kvr), (per, kvr, vdim))
    raw = pltpu.VMEM((n * rows, wide), bf)
    cost = dict(
        flops=2 * tokens * per * (depth * wide // per + 2 * nope * kvr + 2 * tokens * kvr),
        moved=4 * n * rows * wide,
    )
    ho, *kept = call(
        functools.partial(attend_first, n, nh, kq, vq, aq, nope, scale),
        (
            like(tokens, per * vdim),
            like(tokens, depth),
            like(tokens, kvr + rope),
            like(rank, n * rows),
            like(tokens, tokens, dtype=f32),
            *(like(*shape) for shape in shapes),
        ),
        [sc, x, kv, at, pos2] + moved[0] + passed[0] + stacks + [up, wq, ku, vu],
        hbm=range(4 + n + nh, 8 + n + nh),
        scratch=[pltpu.VMEM((128, 128), f32), raw]
        + [pltpu.VMEM(shape, bf) for shape in shapes]
        + [pltpu.SemaphoreType.DMA((8,))],
        **cost,
    )
    slots = [gather_line(ho)]
    ho = call(
        functools.partial(attend_next, n, nope, scale),
        like(tokens, per * vdim),
        [sc] + kept[:4] + moved[1] + passed[1] + kept[4:],
        scratch=[raw],
        **cost,
    )
    w4 = wo.reshape(n, CHUNKS, per * vdim, wo.shape[1])
    total = wo.shape[1]
    width = per * vdim

    def room(pieces):
        return [
            pltpu.VMEM((tokens, len(pieces) * width), bf),
            pltpu.VMEM((len(pieces), width, total), bf),
        ]

    def work(pieces):
        rows = len(pieces) * width
        return dict(flops=2 * tokens * rows * total, moved=2 * rows * total)

    def pick(pieces):
        return [slots[c][bits] for bits, c in pieces]

    slots.append([ho])
    acc, token = call(
        early_body,
        (like(tokens, total, dtype=f32), like(8, 128, dtype=f32)),
        [sc] + pick(EARLY) + [w4],
        hbm=(1 + len(EARLY),),
        scratch=room(EARLY) + [pltpu.SemaphoreType.DMA((len(EARLY),))],
        **work(EARLY),
    )
    *slots[1], token = gather_line(ho, token)
    late = pick(LATE)
    acc, w_last = call(
        middle_body,
        (like(tokens, total, dtype=f32), like(len(LATE), width, total)),
        [sc] + pick(MIDDLE) + [w4, acc, token],
        hbm=(1 + len(MIDDLE),),
        scratch=room(MIDDLE) + [pltpu.SemaphoreType.DMA((len(MIDDLE) + len(LATE),))],
        alias={2 + len(MIDDLE): 0},
        **work(MIDDLE),
    )
    keep, send = call(
        functools.partial(last_body, nh, tok),
        (like(nh // 2 * tok, total, dtype=f32), like(nh // 2 * tok, total)),
        [sc] + late + [w_last, acc],
        scratch=[room(LATE)[0], pltpu.VMEM((tokens, total), f32)],
        **work(LATE),
    )
    got = lax.ppermute(send, "head", flipped(nh, 1))
    pair = (keep + got.astype(f32)).reshape(nh // 2, tok, total)
    side = h // 2
    out = lax.dynamic_index_in_dim(pair, side, 0, keepdims=False)
    away = lax.dynamic_index_in_dim(pair, 1 - side, 0, keepdims=False).astype(bf)
    out = out + lax.ppermute(away, "head", flipped(nh, 2)).astype(f32)
    return merged, out.astype(bf)


def fits(mesh, shapes):
    n, nh = mesh.shape["seq"], mesh.shape["head"]
    x, kv, _, wq, down, _, ku, vu, wo = shapes
    tok, kvr, rank = x[0], ku[2], down[1]
    if mesh.shape["groups"] != 2 or n != 4 or nh != 4 or CHUNKS != 2 or ku[0] % (n * CHUNKS):
        return False
    wide = wq[1] // n // CHUNKS
    return (
        (tok + rank // nh) % 48 == 0
        and tok % 16 == 0
        and tok + 3 <= 128
        and rank <= 128
        and rank // nh % 16 == 0
        and kv[1] - kvr == rank
        and kvr // nh == 128
        and x[1] // nh == wide
        and down[0] == wide
        and wide == 3 * 128
        and wo[1] % 128 == 0
    )


def solution(mesh):
    placed = (
        P(("groups", "seq"), None),
        P(("groups", "seq"), None),
        P(("groups", "seq")),
        P("seq", "head"),
        P(("groups", "seq"), None),
        P("groups", "head"),
        P("head", None, None),
        P("head", None, None),
        P("head", "seq"),
    )

    def local(*args):
        chosen = by_heads if fits(mesh, [a.shape for a in args]) else on_device
        return chosen(*args)

    return jax.shard_map(
        local,
        mesh=mesh,
        in_specs=placed,
        out_specs=(P(("groups", "seq"), "head"), P(("groups", "head"), "seq")),
        check_vma=False,
    )
```

```python
import functools
import math

import jax
import jax.numpy as jnp
from jax import lax
from jax.experimental import pallas as pl
from jax.experimental.pallas import tpu as pltpu
from jax.sharding import PartitionSpec as P

CHUNKS = 2
VMEM_BYTES = 20 * 1024 * 1024
TILE = 512
W_PARTS = 4
HEAD_PARTS = 2
PACK_PARTS = 4


def on_device(
    query_latent_rows,
    key_value_latents,
    positions,
    query_up_weight,
    adapter_down_factor,
    adapter_up_factor,
    head_key_up_weight,
    head_value_up_weight,
    output_projection_weight,
):
    merged_query_weight = (
        query_up_weight.astype(jnp.float32)
        + jnp.dot(adapter_down_factor, adapter_up_factor, preferred_element_type=jnp.float32)
    ).astype(jnp.bfloat16)
    tok_rows = query_latent_rows.shape[0]
    queries = jnp.dot(
        query_latent_rows,
        lax.all_gather(merged_query_weight, "seq", axis=0, tiled=True),
        preferred_element_type=jnp.float32,
    )
    heads_dev = head_key_up_weight.shape[0]
    nope_dim = head_key_up_weight.shape[1]
    kv_rank = head_key_up_weight.shape[2]
    lat_width = key_value_latents.shape[1]
    score_scale = 1.0 / math.sqrt(nope_dim + lat_width - kv_rank)
    queries = queries.astype(jnp.bfloat16).reshape(tok_rows, heads_dev, -1)
    absorbed = jnp.einsum(
        "thn,hnk->thk",
        queries[:, :, :nope_dim],
        head_key_up_weight,
        preferred_element_type=jnp.float32,
    ).astype(jnp.bfloat16)
    full_query = jnp.concatenate([absorbed, queries[:, :, nope_dim:]], axis=2).reshape(
        tok_rows * heads_dev, lat_width
    )
    query_pos = jnp.repeat(positions, heads_dev)
    q_count = tok_rows * heads_dev
    row_max = jnp.full((q_count,), -1e30, jnp.float32)
    key_rows = lax.all_gather(key_value_latents, "seq", axis=0, tiled=True)
    key_pos = lax.all_gather(positions, "seq", axis=0, tiled=True)
    visible = key_pos[None, :] <= query_pos[:, None]
    scores = (
        lax.dot_general(
            full_query, key_rows, (((1,), (1,)), ((), ())), preferred_element_type=jnp.float32
        )
        * score_scale
    )
    scores = jnp.where(visible, scores, jnp.float32(-1e30))
    new_max = jnp.maximum(row_max, jnp.max(scores, axis=1))
    weights = jnp.where(visible, jnp.exp(scores - new_max[:, None]), jnp.float32(0.0))
    row_sum = jnp.sum(weights, axis=1)
    running = jnp.dot(
        weights.astype(jnp.bfloat16), key_rows[:, :kv_rank], preferred_element_type=jnp.float32
    )
    row_max, row_sum, running = (new_max, row_sum, running)
    context_output = (
        (running / row_sum[:, None]).astype(jnp.bfloat16).reshape(tok_rows, heads_dev, kv_rank)
    )
    heads_out = (
        jnp.einsum(
            "euw,uwz->euz", context_output, head_value_up_weight, preferred_element_type=jnp.float32
        )
        .astype(jnp.bfloat16)
        .reshape(tok_rows, -1)
    )
    partial_value = jnp.dot(
        lax.all_gather(heads_out, "seq", axis=0, tiled=True),
        output_projection_weight,
        preferred_element_type=jnp.float32,
    )
    mixed = lax.psum_scatter(
        partial_value.astype(jnp.bfloat16), "head", scatter_dimension=0, tiled=True
    )
    return (merged_query_weight, mixed)


def flipped(n, bit):
    return [(i, i ^ bit) for i in range(n)]


def partners(n):
    return [b for b in range(2, n)] + [1]


def call(body, outs, args, hbm=(), scratch=(), alias=None, flops=0, moved=0):
    vmem = pl.BlockSpec(memory_space=pltpu.VMEM)
    far = pl.BlockSpec(memory_space=pl.ANY)
    args = [pltpu.with_memory_space_constraint(a, pltpu.HBM) if i in hbm else a for i, a in enumerate(args)]
    return pl.pallas_call(
        body,
        out_shape=outs,
        grid_spec=pltpu.PrefetchScalarGridSpec(
            num_scalar_prefetch=1,
            grid=(1,),
            in_specs=[far if i in hbm else vmem for i in range(1, len(args))],
            out_specs=jax.tree.map(lambda o: vmem, outs),
            scratch_shapes=list(scratch),
        ),
        input_output_aliases=alias or {},
        compiler_params=pltpu.CompilerParams(vmem_limit_bytes=VMEM_BYTES),
        cost_estimate=pl.CostEstimate(flops=flops, bytes_accessed=moved, transcendentals=0),
    )(*args)


def fetch(pairs, sems):
    copies = [pltpu.make_async_copy(a, b, sems.at[i]) for i, (a, b) in enumerate(pairs)]
    for copy in copies:
        copy.start()
    return copies


def three_terms(p):
    out = []
    for _ in range(3):
        t = p.astype(jnp.bfloat16).astype(jnp.float32)
        out.append(t)
        p = p - t
    return out


def pack_body(n, kq, vq, aq, wide, kvr, sc, x_ref, kv_ref, at_ref, pos_ref, w_ref, *rest):
    count = CHUNKS * (n - 1)
    parts, outs, (xs, kvs, ats, ps, turn, turned, sems) = rest[0], rest[1 : 1 + count], rest[1 + count :]
    s, g, h = sc[0], sc[1], sc[2]
    tok = x_ref.shape[0]
    rope = kv_ref.shape[1] - kvr
    half = outs[-1].shape[0]
    small = [
        (x_ref.at[:, pl.ds(pl.multiple_of(h * kq, 128), kq)], xs),
        (kv_ref, kvs),
        (at_ref.at[pl.ds(pl.multiple_of(h * aq, 16), aq), :], ats),
        (pos_ref, ps),
    ]
    mine = pl.ds(pl.multiple_of(g * half, 16), half)
    large = []
    for c in range(CHUNKS):
        for k, bits in enumerate(partners(n)):
            chunk = (s ^ bits) * CHUNKS + c
            columns = pl.ds(pl.multiple_of(chunk * wide, 128), wide)
            large.append((w_ref.at[mine, columns], outs[c * (n - 1) + k]))
    copies = fetch(small + large, sems)
    turn[...] = jnp.zeros_like(turn)
    for copy in copies[: len(small)]:
        copy.wait()
    turn[:tok, :rope] = kvs[:, kvr:].astype(jnp.float32)
    start = ps[0:1, 0:1].astype(jnp.float32)
    for i, t in enumerate(three_terms(start)):
        turn[tok + i : tok + i + 1, :] = jnp.broadcast_to(t, (1, turn.shape[1]))
    turned[...] = turn[...].T
    keys = kvs[:, pl.ds(pl.multiple_of(h * vq, 128), vq)]
    ropes = turned[pl.ds(pl.multiple_of(h * aq, 16), aq), :].astype(jnp.bfloat16)
    third = (tok + aq) // 3
    tail = jnp.concatenate([keys, ropes], axis=0)
    parts[:tok, :] = xs[...]
    parts[tok : tok + aq, :] = ats[...]
    for i in range(3):
        parts[tok + aq :, i * vq : (i + 1) * vq] = tail[i * third : (i + 1) * third]
    for copy in copies[len(small) :]:
        copy.wait()


def join_body(sc, *refs):
    outs = [ref for ref in refs if len(ref.shape) == 3]
    count = (len(refs) - len(outs)) // len(outs)
    for i, out in enumerate(outs):
        for k in range(count):
            out[k] = refs[i * count + k][...]


def unpack(n, nh, kq, vq, aq, sc, own, packs, stacks, outs, turn):
    (x_ref, kv_ref, at_ref, pos_ref), (xo, kvo, ao, bias) = own, outs
    s, h = sc[0], sc[2]
    tok, depth = x_ref.shape[0], at_ref.shape[1]
    kvr = vq * nh
    rope = kv_ref.shape[1] - kvr
    third = (tok + aq) // 3
    tokens = bias.shape[0]
    row = pl.multiple_of(s * tok, 16)
    xo[pl.ds(row, tok), :] = x_ref[...]
    kvo[pl.ds(row, tok), :] = kv_ref[...]
    ao[:, pl.ds(pl.multiple_of(s * depth, 128), depth)] = at_ref[...]
    starts = [(s, pos_ref[0:1, 0:1].astype(jnp.float32))]
    turn[...] = jnp.zeros_like(turn)
    for k, bits in enumerate(partners(n)):
        src = s ^ bits
        rows = pl.ds(pl.multiple_of(src * tok, 16), tok)
        for j in range(nh):
            hh = h ^ j
            got = stacks[j - 1].at[k] if j else packs[k]
            xo[rows, pl.ds(pl.multiple_of(hh * kq, 128), kq)] = got[:tok, :]
            arow = pl.ds(pl.multiple_of(hh * aq, 16), aq)
            ao[arow, pl.ds(pl.multiple_of(src * depth, 128), depth)] = got[tok : tok + aq, :]
            tail = jnp.concatenate([got[tok + aq :, i * vq : (i + 1) * vq] for i in range(3)], axis=0)
            kvo[rows, pl.ds(pl.multiple_of(hh * vq, 128), vq)] = tail[:tok]
            turn[arow, :] = tail[tok:].astype(jnp.float32)
        turned = turn[...].T
        kvo[rows, kvr:] = turned[:tok, :rope].astype(jnp.bfloat16)
        terms = [turned[tok + i : tok + i + 1, :1] for i in range(3)]
        starts.append((src, terms[0] + terms[1] + terms[2]))

    def places(shape, dim):
        index = lax.broadcasted_iota(jnp.int32, shape, dim)
        block = index // tok
        out = (index - block * tok).astype(jnp.float32)
        for src, start in starts:
            out = out + jnp.where(block == src, start, 0.0)
        return out

    seen = places((1, tokens), 1) <= places((tokens, 1), 0)
    bias[...] = jnp.where(seen, 0.0, -1e30)


def own_weights(sc, c, weights, outs):
    b_ref, w_ref, ku_ref, vu_ref = weights
    b, w, ku, vu = outs
    wide, heads = w.shape[1], ku.shape[0]
    chunk = sc[0] * CHUNKS + c
    columns = pl.ds(pl.multiple_of(chunk * wide, 128), wide)
    return [
        (b_ref.at[:, columns], b),
        (w_ref.at[:, columns], w),
        (ku_ref.at[pl.ds(chunk * heads, heads)], ku),
        (vu_ref.at[pl.ds(chunk * heads, heads)], vu),
    ]


def attend(n, nope, scale, sc, shared, units, ys, weights, out, raw, before=None, copies=()):
    x_ref, kv_ref, at_ref, bias_ref = shared
    b_own, w_own, ku, vu = weights
    s, g = sc[0], sc[1]
    depth, wide = w_own.shape
    half = depth // 2
    heads, kvr, vdim = vu.shape
    if before is not None:
        before()
    for k, bits in enumerate(partners(n)):
        src = s ^ bits
        raw[pl.ds(pl.multiple_of(src * depth + g * half, 16), half), :] = units[k][:half]
        raw[pl.ds(pl.multiple_of(src * depth + (1 - g) * half, 16), half), :] = ys[k][...]
    for copy in copies[:2]:
        copy.wait()
    raw[pl.ds(pl.multiple_of(s * depth, 16), depth), :] = w_own[...]

    def merge(rows):
        add = lax.dot_general(
            at_ref[:, rows], b_own[...], (((0,), (0,)), ((), ())), preferred_element_type=jnp.float32
        )
        raw[rows, :] = (raw[rows, :].astype(jnp.float32) + add).astype(jnp.bfloat16)

    for src in range(n):
        merge(slice(src * depth, (src + 1) * depth))
    q = jnp.dot(x_ref[...], raw[...], preferred_element_type=jnp.float32)
    for copy in copies[2:]:
        copy.wait()
    width = wide // heads
    lat, rope_key = kv_ref[:, :kvr], kv_ref[:, kvr:]
    bias = bias_ref[...]
    nt = (((1,), (1,)), ((), ()))
    for j in range(heads):
        qn = q[:, j * width : j * width + nope].astype(jnp.bfloat16)
        qr = q[:, j * width + nope : (j + 1) * width].astype(jnp.bfloat16)
        absorbed = jnp.dot(qn, ku[j], preferred_element_type=jnp.float32).astype(jnp.bfloat16)
        scores = lax.dot_general(absorbed, lat, nt, preferred_element_type=jnp.float32)
        scores = scores + lax.dot_general(qr, rope_key, nt, preferred_element_type=jnp.float32)
        scores = scores * scale + bias
        top = jnp.max(scores, axis=1, keepdims=True)
        e = jnp.exp(scores - top)
        total = jnp.sum(e, axis=1, keepdims=True)
        ctx = jnp.dot(e.astype(jnp.bfloat16), lat, preferred_element_type=jnp.float32)
        ctx = (ctx / total).astype(jnp.bfloat16)
        ho = jnp.dot(ctx, vu[j], preferred_element_type=jnp.float32)
        out[:, j * vdim : (j + 1) * vdim] = ho.astype(jnp.bfloat16)


def pick_body(sc, *refs):
    far, outs, sems = refs[:4], refs[4:8], refs[8]
    for copy in fetch(own_weights(sc, 0, far, outs), sems):
        copy.wait()


def attend_first(n, nh, kq, vq, aq, nope, scale, sc, *refs):
    own, units, y_ref, stacks = refs[:4], refs[4 : 3 + n], refs[3 + n], refs[4 + n : 3 + n + nh]
    packs, refs = refs[3 + n + nh : 2 + 2 * n + nh], refs[2 + 2 * n + nh :]
    weights, far, out, shared, later = refs[:4], refs[4:8], refs[8], refs[9:13], refs[13:17]
    turn, raw, sems = refs[17:]
    copies = fetch(own_weights(sc, CHUNKS - 1, far, later), sems)

    def before():
        unpack(n, nh, kq, vq, aq, sc, own, packs, stacks, shared, turn)

    ys = [y_ref.at[k] for k in range(n - 1)]
    attend(n, nope, scale, sc, shared, units, ys, weights, out, raw, before)
    for copy in copies:
        copy.wait()


def attend_next(n, nope, scale, sc, *refs):
    shared, units, ys, refs = refs[:4], refs[4 : 3 + n], refs[3 + n : 2 + 2 * n], refs[2 + 2 * n :]
    attend(n, nope, scale, sc, shared, units, ys, refs[:4], refs[4], refs[5])


def gather_line(x, *held):
    two = lax.ppermute(x, "seq", flipped(4, 2))
    one = lax.ppermute(x, "seq", flipped(4, 1))
    two, one, *held = lax.optimization_barrier((two, one) + held)
    return [x, one, two, lax.ppermute(two, "seq", flipped(4, 1))] + held


EARLY = ((0, 0), (1, 0), (2, 0), (0, 1))
MIDDLE = ((3, 0), (1, 1), (2, 1))
LATE = ((3, 1),)


def place(slots, lhs):
    for i, ref in enumerate(slots):
        width = ref.shape[1]
        lhs[:, i * width : (i + 1) * width] = ref[...]


def slabs(sc, w_ref, pieces, columns, out):
    return [(w_ref.at[sc[0] ^ bits, c, :, columns], out.at[i]) for i, (bits, c) in enumerate(pieces)]


def columns_dot(lhs, w, begin, end, put):
    for at in range(begin, end, TILE):
        stop = min(at + TILE, end)
        tile = w[:, :, at:stop]
        tile = tile.reshape(-1, tile.shape[-1])
        put(slice(at, stop), jnp.dot(lhs[...], tile, preferred_element_type=jnp.float32))


def early_body(sc, *refs):
    count = len(EARLY)
    slots, (w_ref, acc, token, middle, late, lhs, w, sems) = refs[:count], refs[count:]
    copies = fetch(
        slabs(sc, w_ref, EARLY, slice(None), w)
        + slabs(sc, w_ref, MIDDLE, slice(None), middle)
        + slabs(sc, w_ref, LATE, slice(None), late),
        sems,
    )
    place(slots, lhs)
    token[...] = jnp.zeros_like(token)
    for copy in copies[:count]:
        copy.wait()

    def put(band, value):
        acc[:, band] = value

    columns_dot(lhs, w, 0, acc.shape[1], put)
    for copy in copies[count:]:
        copy.wait()


def middle_body(sc, *refs):
    count = len(MIDDLE)
    slots, (w, before, token, acc, lhs) = refs[:count], refs[count:]
    del before, token
    place(slots, lhs)

    def add(band, value):
        acc[:, band] += value

    columns_dot(lhs, w, 0, acc.shape[1], add)


def last_body(nh, tok, sc, *refs):
    slots, (w, acc, keep, send, lhs, tot) = refs[: len(LATE)], refs[len(LATE) :]
    place(slots, lhs)

    def put(band, value):
        tot[:, band] = acc[:, band] + value

    columns_dot(lhs, w, 0, keep.shape[1], put)
    core = sc[2] % 2
    for i in range(nh // 2):
        mine = pl.ds(pl.multiple_of((2 * i + core) * tok, 16), tok)
        theirs = pl.ds(pl.multiple_of((2 * i + 1 - core) * tok, 16), tok)
        keep[i * tok : (i + 1) * tok, :] = tot[mine, :]
        send[i * tok : (i + 1) * tok, :] = tot[theirs, :].astype(jnp.bfloat16)


def by_heads(x, kv, pos, wq, down, up, ku, vu, wo):
    n, nh = lax.axis_size("seq"), lax.axis_size("head")
    s, g, h = lax.axis_index("seq"), lax.axis_index("groups"), lax.axis_index("head")
    sc = jnp.stack([s, g, h]).astype(jnp.int32)
    bf, f32 = jnp.bfloat16, jnp.float32
    tok, depth = x.shape
    heads, nope, kvr = ku.shape
    vdim = vu.shape[2]
    rope = kv.shape[1] - kvr
    rank = down.shape[1]
    rows, cols = wq.shape
    half = rows // 2
    tokens = n * tok
    per = heads // n // CHUNKS
    wide = per * (cols // heads)
    kq, vq, aq = depth // nh, kvr // nh, rank // nh
    extra = tok + aq + (tok + aq) // 3
    at = down.T
    pos2 = pos[None, :]

    def like(*shape, dtype=bf):
        return jax.ShapeDtypeStruct(shape, dtype)

    parts, *units = call(
        functools.partial(pack_body, n, kq, vq, aq, wide, kvr),
        (like(extra, wide), *[like(half, wide)] * (n - 1) * CHUNKS),
        [sc, x, kv, at, pos2, wq],
        hbm=range(1, 6),
        scratch=[
            pltpu.VMEM((tok, kq), bf),
            pltpu.VMEM(kv.shape, bf),
            pltpu.VMEM((aq, rows), bf),
            pltpu.VMEM(pos2.shape, jnp.int32),
            pltpu.VMEM((128, 128), f32),
            pltpu.VMEM((128, 128), f32),
            pltpu.SemaphoreType.DMA((4 + (n - 1) * CHUNKS,)),
        ],
        moved=4 * half * cols,
    )
    def exchange(parts):
        return [lax.ppermute(p, "seq", flipped(n, bits)) for p, bits in zip(parts, partners(n))]

    def join(*groups):
        outs = tuple(like(n - 1, *group[0].shape) for group in groups)
        args = [a for group in groups for a in group]
        return call(join_body, outs, [sc] + args, moved=4 * sum(a.size for a in args))

    merged = (wq.astype(f32) + jnp.dot(down, up, preferred_element_type=f32)).astype(bf)
    _, one, two, three = gather_line(parts)
    packs = [two, three, one]
    moved = [exchange(units[: n - 1])]
    held = lax.optimization_barrier((*moved[0], *packs, merged))
    moved[0], packs, merged = list(held[: n - 1]), list(held[n - 1 : -1]), held[-1]
    moved.append(exchange(units[n - 1 :]))
    share, stack = join(moved[0], packs)
    passed = [[lax.ppermute(share, "groups", flipped(2, 1))]]
    across = lax.ppermute(stack, "head", flipped(nh, 2))
    shapes = ((rank, wide), (rows, wide), (per, nope, kvr), (per, kvr, vdim))
    picked = call(
        pick_body,
        tuple(like(*shape) for shape in shapes),
        [sc, up, wq, ku, vu],
        hbm=range(1, 5),
        scratch=[pltpu.SemaphoreType.DMA((4,))],
        moved=4 * sum(math.prod(shape) for shape in shapes),
    )
    across, *rest = lax.optimization_barrier((across, *moved[1], *picked))
    moved[1], picked = rest[: n - 1], rest[n - 1 :]
    stacks = [
        lax.ppermute(stack, "head", flipped(nh, 1)),
        across,
        lax.ppermute(across, "head", flipped(nh, 1)),
    ]
    passed.append([lax.ppermute(p, "groups", flipped(2, 1)) for p in moved[1]])

    scale = 1.0 / math.sqrt(nope + rope)
    raw = pltpu.VMEM((n * rows, wide), bf)
    cost = dict(
        flops=2 * tokens * per * (depth * wide // per + 2 * nope * kvr + 2 * tokens * kvr),
        moved=4 * n * rows * wide,
    )
    ho, *kept = call(
        functools.partial(attend_first, n, nh, kq, vq, aq, nope, scale),
        (
            like(tokens, per * vdim),
            like(tokens, depth),
            like(tokens, kvr + rope),
            like(rank, n * rows),
            like(tokens, tokens, dtype=f32),
            *(like(*shape) for shape in shapes),
        ),
        [sc, x, kv, at, pos2] + moved[0] + passed[0] + stacks + packs + picked + [up, wq, ku, vu],
        hbm=range(7 + 2 * n + nh, 11 + 2 * n + nh),
        scratch=[pltpu.VMEM((128, 128), f32), raw]
        + [pltpu.SemaphoreType.DMA((4,))],
        **cost,
    )
    slots = [gather_line(ho)]
    ho = call(
        functools.partial(attend_next, n, nope, scale),
        like(tokens, per * vdim),
        [sc] + kept[:4] + moved[1] + passed[1] + kept[4:],
        scratch=[raw],
        **cost,
    )
    w4 = wo.reshape(n, CHUNKS, per * vdim, wo.shape[1])
    total = wo.shape[1]
    width = per * vdim

    def room(pieces):
        return [
            pltpu.VMEM((tokens, len(pieces) * width), bf),
            pltpu.VMEM((len(pieces), width, total), bf),
        ]

    def work(pieces):
        rows = len(pieces) * width
        return dict(flops=2 * tokens * rows * total, moved=2 * rows * total)

    def pick(pieces):
        return [slots[c][bits] for bits, c in pieces]

    slots.append([ho])
    acc, token, w_middle, w_late = call(
        early_body,
        (
            like(tokens, total, dtype=f32),
            like(8, 128, dtype=f32),
            like(len(MIDDLE), width, total),
            like(len(LATE), width, total),
        ),
        [sc] + pick(EARLY) + [w4],
        hbm=(1 + len(EARLY),),
        scratch=room(EARLY) + [pltpu.SemaphoreType.DMA((len(EARLY + MIDDLE + LATE),))],
        **work(EARLY),
    )
    *slots[1], token = gather_line(ho, token)
    late = pick(LATE)
    acc = call(
        middle_body,
        like(tokens, total, dtype=f32),
        [sc] + pick(MIDDLE) + [w_middle, acc, token],
        scratch=room(MIDDLE)[:1],
        alias={2 + len(MIDDLE): 0},
        **work(MIDDLE),
    )
    keep, send = call(
        functools.partial(last_body, nh, tok),
        (like(nh // 2 * tok, total, dtype=f32), like(nh // 2 * tok, total)),
        [sc] + late + [w_late, acc],
        scratch=[room(LATE)[0], pltpu.VMEM((tokens, total), f32)],
        **work(LATE),
    )
    got = lax.ppermute(send, "head", flipped(nh, 1))
    pair = (keep + got.astype(f32)).reshape(nh // 2, tok, total)
    side = h // 2
    out = lax.dynamic_index_in_dim(pair, side, 0, keepdims=False)
    away = lax.dynamic_index_in_dim(pair, 1 - side, 0, keepdims=False).astype(bf)
    out = out + lax.ppermute(away, "head", flipped(nh, 2)).astype(f32)
    return merged, out.astype(bf)


def fits(mesh, shapes):
    n, nh = mesh.shape["seq"], mesh.shape["head"]
    x, kv, _, wq, down, _, ku, vu, wo = shapes
    tok, kvr, rank = x[0], ku[2], down[1]
    if mesh.shape["groups"] != 2 or n != 4 or nh != 4 or CHUNKS != 2 or ku[0] % (n * CHUNKS):
        return False
    wide = wq[1] // n // CHUNKS
    return (
        (tok + rank // nh) % 48 == 0
        and tok % 16 == 0
        and tok + 3 <= 128
        and rank <= 128
        and rank // nh % 16 == 0
        and kv[1] - kvr == rank
        and kvr // nh == 128
        and x[1] // nh == wide
        and down[0] == wide
        and wide == 3 * 128
        and wo[1] % 128 == 0
    )


def solution(mesh):
    placed = (
        P(("groups", "seq"), None),
        P(("groups", "seq"), None),
        P(("groups", "seq")),
        P("seq", "head"),
        P(("groups", "seq"), None),
        P("groups", "head"),
        P("head", None, None),
        P("head", None, None),
        P("head", "seq"),
    )

    def local(*args):
        chosen = by_heads if fits(mesh, [a.shape for a in args]) else on_device
        return chosen(*args)

    return jax.shard_map(
        local,
        mesh=mesh,
        in_specs=placed,
        out_specs=(P(("groups", "seq"), "head"), P(("groups", "head"), "seq")),
        check_vma=False,
    )
```

```python
import functools
import math

import jax
import jax.numpy as jnp
from jax import lax
from jax.experimental import pallas as pl
from jax.experimental.pallas import tpu as pltpu
from jax.sharding import PartitionSpec as P

CHUNKS = 2
VMEM_BYTES = 20 * 1024 * 1024
TILE = 512
W_PARTS = 4
HEAD_PARTS = 2
PACK_PARTS = 4


def on_device(
    query_latent_rows,
    key_value_latents,
    positions,
    query_up_weight,
    adapter_down_factor,
    adapter_up_factor,
    head_key_up_weight,
    head_value_up_weight,
    output_projection_weight,
):
    merged_query_weight = (
        query_up_weight.astype(jnp.float32)
        + jnp.dot(adapter_down_factor, adapter_up_factor, preferred_element_type=jnp.float32)
    ).astype(jnp.bfloat16)
    tok_rows = query_latent_rows.shape[0]
    queries = jnp.dot(
        query_latent_rows,
        lax.all_gather(merged_query_weight, "seq", axis=0, tiled=True),
        preferred_element_type=jnp.float32,
    )
    heads_dev = head_key_up_weight.shape[0]
    nope_dim = head_key_up_weight.shape[1]
    kv_rank = head_key_up_weight.shape[2]
    lat_width = key_value_latents.shape[1]
    score_scale = 1.0 / math.sqrt(nope_dim + lat_width - kv_rank)
    queries = queries.astype(jnp.bfloat16).reshape(tok_rows, heads_dev, -1)
    absorbed = jnp.einsum(
        "thn,hnk->thk",
        queries[:, :, :nope_dim],
        head_key_up_weight,
        preferred_element_type=jnp.float32,
    ).astype(jnp.bfloat16)
    full_query = jnp.concatenate([absorbed, queries[:, :, nope_dim:]], axis=2).reshape(
        tok_rows * heads_dev, lat_width
    )
    query_pos = jnp.repeat(positions, heads_dev)
    q_count = tok_rows * heads_dev
    row_max = jnp.full((q_count,), -1e30, jnp.float32)
    key_rows = lax.all_gather(key_value_latents, "seq", axis=0, tiled=True)
    key_pos = lax.all_gather(positions, "seq", axis=0, tiled=True)
    visible = key_pos[None, :] <= query_pos[:, None]
    scores = (
        lax.dot_general(
            full_query, key_rows, (((1,), (1,)), ((), ())), preferred_element_type=jnp.float32
        )
        * score_scale
    )
    scores = jnp.where(visible, scores, jnp.float32(-1e30))
    new_max = jnp.maximum(row_max, jnp.max(scores, axis=1))
    weights = jnp.where(visible, jnp.exp(scores - new_max[:, None]), jnp.float32(0.0))
    row_sum = jnp.sum(weights, axis=1)
    running = jnp.dot(
        weights.astype(jnp.bfloat16), key_rows[:, :kv_rank], preferred_element_type=jnp.float32
    )
    row_max, row_sum, running = (new_max, row_sum, running)
    context_output = (
        (running / row_sum[:, None]).astype(jnp.bfloat16).reshape(tok_rows, heads_dev, kv_rank)
    )
    heads_out = (
        jnp.einsum(
            "euw,uwz->euz", context_output, head_value_up_weight, preferred_element_type=jnp.float32
        )
        .astype(jnp.bfloat16)
        .reshape(tok_rows, -1)
    )
    partial_value = jnp.dot(
        lax.all_gather(heads_out, "seq", axis=0, tiled=True),
        output_projection_weight,
        preferred_element_type=jnp.float32,
    )
    mixed = lax.psum_scatter(
        partial_value.astype(jnp.bfloat16), "head", scatter_dimension=0, tiled=True
    )
    return (merged_query_weight, mixed)


def flipped(n, bit):
    return [(i, i ^ bit) for i in range(n)]


def partners(n):
    return [1, 3, 2]


def call(body, outs, args, hbm=(), scratch=(), alias=None, flops=0, moved=0):
    vmem = pl.BlockSpec(memory_space=pltpu.VMEM)
    far = pl.BlockSpec(memory_space=pl.ANY)
    args = [pltpu.with_memory_space_constraint(a, pltpu.HBM) if i in hbm else a for i, a in enumerate(args)]
    return pl.pallas_call(
        body,
        out_shape=outs,
        grid_spec=pltpu.PrefetchScalarGridSpec(
            num_scalar_prefetch=1,
            grid=(1,),
            in_specs=[far if i in hbm else vmem for i in range(1, len(args))],
            out_specs=jax.tree.map(lambda o: vmem, outs),
            scratch_shapes=list(scratch),
        ),
        input_output_aliases=alias or {},
        compiler_params=pltpu.CompilerParams(vmem_limit_bytes=VMEM_BYTES),
        cost_estimate=pl.CostEstimate(flops=flops, bytes_accessed=moved, transcendentals=0),
    )(*args)


def fetch(pairs, sems):
    copies = [pltpu.make_async_copy(a, b, sems.at[i]) for i, (a, b) in enumerate(pairs)]
    for copy in copies:
        copy.start()
    return copies


def three_terms(p):
    out = []
    for _ in range(3):
        t = p.astype(jnp.bfloat16).astype(jnp.float32)
        out.append(t)
        p = p - t
    return out


def pack_body(n, kq, vq, aq, wide, kvr, sc, x_ref, kv_ref, at_ref, pos_ref, w_ref, *rest):
    count = CHUNKS * (n - 1)
    parts, outs, (xs, kvs, ats, ps, turn, turned, sems) = rest[0], rest[1 : 1 + count], rest[1 + count :]
    s, g, h = sc[0], sc[1], sc[2]
    tok = x_ref.shape[0]
    rope = kv_ref.shape[1] - kvr
    half = outs[-1].shape[0]
    small = [
        (x_ref.at[:, pl.ds(pl.multiple_of(h * kq, 128), kq)], xs),
        (kv_ref, kvs),
        (at_ref.at[pl.ds(pl.multiple_of(h * aq, 16), aq), :], ats),
        (pos_ref, ps),
    ]
    mine = pl.ds(pl.multiple_of(g * half, 16), half)
    large = []
    for c in range(CHUNKS):
        for k, bits in enumerate(partners(n)):
            chunk = (s ^ bits) * CHUNKS + c
            columns = pl.ds(pl.multiple_of(chunk * wide, 128), wide)
            large.append((w_ref.at[mine, columns], outs[c * (n - 1) + k]))
    copies = fetch(small + large, sems)
    turn[...] = jnp.zeros_like(turn)
    for copy in copies[: len(small)]:
        copy.wait()
    turn[:tok, :rope] = kvs[:, kvr:].astype(jnp.float32)
    start = ps[0:1, 0:1].astype(jnp.float32)
    for i, t in enumerate(three_terms(start)):
        turn[tok + i : tok + i + 1, :] = jnp.broadcast_to(t, (1, turn.shape[1]))
    turned[...] = turn[...].T
    keys = kvs[:, pl.ds(pl.multiple_of(h * vq, 128), vq)]
    ropes = turned[pl.ds(pl.multiple_of(h * aq, 16), aq), :].astype(jnp.bfloat16)
    third = (tok + aq) // 3
    tail = jnp.concatenate([keys, ropes], axis=0)
    parts[:tok, :] = xs[...]
    parts[tok : tok + aq, :] = ats[...]
    for i in range(3):
        parts[tok + aq :, i * vq : (i + 1) * vq] = tail[i * third : (i + 1) * third]
    for copy in copies[len(small) :]:
        copy.wait()


def join_body(sc, *refs):
    outs = [ref for ref in refs if len(ref.shape) == 3]
    count = (len(refs) - len(outs)) // len(outs)
    for i, out in enumerate(outs):
        for k in range(count):
            out[k] = refs[i * count + k][...]


def unpack(n, nh, kq, vq, aq, sc, own, packs, stacks, outs, turn):
    (x_ref, kv_ref, at_ref, pos_ref), (xo, kvo, ao, bias) = own, outs
    s, h = sc[0], sc[2]
    tok, depth = x_ref.shape[0], at_ref.shape[1]
    kvr = vq * nh
    rope = kv_ref.shape[1] - kvr
    third = (tok + aq) // 3
    tokens = bias.shape[0]
    row = pl.multiple_of(s * tok, 16)
    xo[pl.ds(row, tok), :] = x_ref[...]
    kvo[pl.ds(row, tok), :] = kv_ref[...]
    ao[:, pl.ds(pl.multiple_of(s * depth, 128), depth)] = at_ref[...]
    starts = [(s, pos_ref[0:1, 0:1].astype(jnp.float32))]
    turn[...] = jnp.zeros_like(turn)
    for k, bits in enumerate(partners(n)):
        src = s ^ bits
        rows = pl.ds(pl.multiple_of(src * tok, 16), tok)
        for j in range(nh):
            hh = h ^ j
            got = stacks[j - 1].at[k] if j else packs[k]
            xo[rows, pl.ds(pl.multiple_of(hh * kq, 128), kq)] = got[:tok, :]
            arow = pl.ds(pl.multiple_of(hh * aq, 16), aq)
            ao[arow, pl.ds(pl.multiple_of(src * depth, 128), depth)] = got[tok : tok + aq, :]
            tail = jnp.concatenate([got[tok + aq :, i * vq : (i + 1) * vq] for i in range(3)], axis=0)
            kvo[rows, pl.ds(pl.multiple_of(hh * vq, 128), vq)] = tail[:tok]
            turn[arow, :] = tail[tok:].astype(jnp.float32)
        turned = turn[...].T
        kvo[rows, kvr:] = turned[:tok, :rope].astype(jnp.bfloat16)
        terms = [turned[tok + i : tok + i + 1, :1] for i in range(3)]
        starts.append((src, terms[0] + terms[1] + terms[2]))

    def places(shape, dim):
        index = lax.broadcasted_iota(jnp.int32, shape, dim)
        block = index // tok
        out = (index - block * tok).astype(jnp.float32)
        for src, start in starts:
            out = out + jnp.where(block == src, start, 0.0)
        return out

    seen = places((1, tokens), 1) <= places((tokens, 1), 0)
    bias[...] = jnp.where(seen, 0.0, -1e30)


def own_weights(sc, c, weights, outs):
    b_ref, w_ref, ku_ref, vu_ref = weights
    b, w, ku, vu = outs
    wide, heads = w.shape[1], ku.shape[0]
    chunk = sc[0] * CHUNKS + c
    columns = pl.ds(pl.multiple_of(chunk * wide, 128), wide)
    return [
        (b_ref.at[:, columns], b),
        (w_ref.at[:, columns], w),
        (ku_ref.at[pl.ds(chunk * heads, heads)], ku),
        (vu_ref.at[pl.ds(chunk * heads, heads)], vu),
    ]


def attend(n, nope, scale, sc, shared, units, ys, weights, out, raw, before=None, copies=()):
    x_ref, kv_ref, at_ref, bias_ref = shared
    b_own, w_own, ku, vu = weights
    s, g = sc[0], sc[1]
    depth, wide = w_own.shape
    half = depth // 2
    heads, kvr, vdim = vu.shape
    if before is not None:
        before()
    for k, bits in enumerate(partners(n)):
        src = s ^ bits
        raw[pl.ds(pl.multiple_of(src * depth + g * half, 16), half), :] = units[k][:half]
        raw[pl.ds(pl.multiple_of(src * depth + (1 - g) * half, 16), half), :] = ys[k][...]
    for copy in copies[:2]:
        copy.wait()
    raw[pl.ds(pl.multiple_of(s * depth, 16), depth), :] = w_own[...]

    def merge(rows):
        add = lax.dot_general(
            at_ref[:, rows], b_own[...], (((0,), (0,)), ((), ())), preferred_element_type=jnp.float32
        )
        raw[rows, :] = (raw[rows, :].astype(jnp.float32) + add).astype(jnp.bfloat16)

    for src in range(n):
        merge(slice(src * depth, (src + 1) * depth))
    q = jnp.dot(x_ref[...], raw[...], preferred_element_type=jnp.float32)
    for copy in copies[2:]:
        copy.wait()
    width = wide // heads
    lat, rope_key = kv_ref[:, :kvr], kv_ref[:, kvr:]
    bias = bias_ref[...]
    nt = (((1,), (1,)), ((), ()))
    for j in range(heads):
        qn = q[:, j * width : j * width + nope].astype(jnp.bfloat16)
        qr = q[:, j * width + nope : (j + 1) * width].astype(jnp.bfloat16)
        absorbed = jnp.dot(qn, ku[j], preferred_element_type=jnp.float32).astype(jnp.bfloat16)
        scores = lax.dot_general(absorbed, lat, nt, preferred_element_type=jnp.float32)
        scores = scores + lax.dot_general(qr, rope_key, nt, preferred_element_type=jnp.float32)
        scores = scores * scale + bias
        top = jnp.max(scores, axis=1, keepdims=True)
        e = jnp.exp(scores - top)
        total = jnp.sum(e, axis=1, keepdims=True)
        ctx = jnp.dot(e.astype(jnp.bfloat16), lat, preferred_element_type=jnp.float32)
        ctx = (ctx / total).astype(jnp.bfloat16)
        ho = jnp.dot(ctx, vu[j], preferred_element_type=jnp.float32)
        out[:, j * vdim : (j + 1) * vdim] = ho.astype(jnp.bfloat16)


def pick_body(sc, *refs):
    far, outs, sems = refs[:4], refs[4:8], refs[8]
    for copy in fetch(own_weights(sc, 0, far, outs), sems):
        copy.wait()


def attend_first(n, nh, kq, vq, aq, nope, scale, sc, *refs):
    own, units, y_ref, stacks = refs[:4], refs[4 : 3 + n], refs[3 + n], refs[4 + n : 3 + n + nh]
    packs, refs = refs[3 + n + nh : 2 + 2 * n + nh], refs[2 + 2 * n + nh :]
    weights, far, out, shared, later = refs[:4], refs[4:8], refs[8], refs[9:13], refs[13:17]
    turn, raw, sems = refs[17:]
    copies = fetch(own_weights(sc, CHUNKS - 1, far, later), sems)

    def before():
        unpack(n, nh, kq, vq, aq, sc, own, packs, stacks, shared, turn)

    ys = [y_ref.at[k] for k in range(n - 1)]
    attend(n, nope, scale, sc, shared, units, ys, weights, out, raw, before)
    for copy in copies:
        copy.wait()


def attend_next(n, nope, scale, sc, *refs):
    shared, units, ys, refs = refs[:4], refs[4 : 3 + n], refs[3 + n : 2 + 2 * n], refs[2 + 2 * n :]
    attend(n, nope, scale, sc, shared, units, ys, refs[:4], refs[4], refs[5])


def gather_line(x, *held):
    two = lax.ppermute(x, "seq", flipped(4, 2))
    one = lax.ppermute(x, "seq", flipped(4, 1))
    two, one, *held = lax.optimization_barrier((two, one) + held)
    return [x, one, two, lax.ppermute(two, "seq", flipped(4, 1))] + held


EARLY = ((0, 0), (1, 0), (2, 0), (0, 1))
MIDDLE = ((3, 0), (1, 1), (2, 1))
LATE = ((3, 1),)


def place(slots, lhs):
    for i, ref in enumerate(slots):
        width = ref.shape[1]
        lhs[:, i * width : (i + 1) * width] = ref[...]


def slabs(sc, w_ref, pieces, columns, out):
    return [(w_ref.at[sc[0] ^ bits, c, :, columns], out.at[i]) for i, (bits, c) in enumerate(pieces)]


def columns_dot(lhs, w, begin, end, put):
    for at in range(begin, end, TILE):
        stop = min(at + TILE, end)
        tile = w[:, :, at:stop]
        tile = tile.reshape(-1, tile.shape[-1])
        put(slice(at, stop), jnp.dot(lhs[...], tile, preferred_element_type=jnp.float32))


def early_body(sc, *refs):
    count = len(EARLY)
    slots, (w_ref, acc, token, middle, late, lhs, w, sems) = refs[:count], refs[count:]
    copies = fetch(
        slabs(sc, w_ref, EARLY, slice(None), w)
        + slabs(sc, w_ref, MIDDLE, slice(None), middle)
        + slabs(sc, w_ref, LATE, slice(None), late),
        sems,
    )
    place(slots, lhs)
    token[...] = jnp.zeros_like(token)
    for copy in copies[:count]:
        copy.wait()

    def put(band, value):
        acc[:, band] = value

    columns_dot(lhs, w, 0, acc.shape[1], put)
    for copy in copies[count:]:
        copy.wait()


def middle_body(sc, *refs):
    count = len(MIDDLE)
    slots, (w, before, token, acc, lhs) = refs[:count], refs[count:]
    del before, token
    place(slots, lhs)

    def add(band, value):
        acc[:, band] += value

    columns_dot(lhs, w, 0, acc.shape[1], add)


def last_body(nh, tok, sc, *refs):
    slots, (w, acc, keep, send) = refs[: len(LATE)], refs[len(LATE) :]
    core = sc[2] % 2
    total = acc.shape[1]
    for which, out in ((core, keep), (1 - core, send)):
        rows = [pl.ds(pl.multiple_of((2 * i + which) * tok, 16), tok) for i in range(nh // 2)]
        lhs = jnp.concatenate([slots[0][row, :] for row in rows], axis=0)
        for at in range(0, total, TILE):
            band = slice(at, min(at + TILE, total))
            more = jnp.dot(lhs, w[0, :, band], preferred_element_type=jnp.float32)
            for i, row in enumerate(rows):
                part = acc[row, band] + more[i * tok : (i + 1) * tok]
                out[i * tok : (i + 1) * tok, band] = part.astype(out.dtype)


def by_heads(x, kv, pos, wq, down, up, ku, vu, wo):
    n, nh = lax.axis_size("seq"), lax.axis_size("head")
    s, g, h = lax.axis_index("seq"), lax.axis_index("groups"), lax.axis_index("head")
    sc = jnp.stack([s, g, h]).astype(jnp.int32)
    bf, f32 = jnp.bfloat16, jnp.float32
    tok, depth = x.shape
    heads, nope, kvr = ku.shape
    vdim = vu.shape[2]
    rope = kv.shape[1] - kvr
    rank = down.shape[1]
    rows, cols = wq.shape
    half = rows // 2
    tokens = n * tok
    per = heads // n // CHUNKS
    wide = per * (cols // heads)
    kq, vq, aq = depth // nh, kvr // nh, rank // nh
    extra = tok + aq + (tok + aq) // 3
    at = down.T
    pos2 = pos[None, :]

    def like(*shape, dtype=bf):
        return jax.ShapeDtypeStruct(shape, dtype)

    parts, *units = call(
        functools.partial(pack_body, n, kq, vq, aq, wide, kvr),
        (like(extra, wide), *[like(half, wide)] * (n - 1) * CHUNKS),
        [sc, x, kv, at, pos2, wq],
        hbm=range(1, 6),
        scratch=[
            pltpu.VMEM((tok, kq), bf),
            pltpu.VMEM(kv.shape, bf),
            pltpu.VMEM((aq, rows), bf),
            pltpu.VMEM(pos2.shape, jnp.int32),
            pltpu.VMEM((128, 128), f32),
            pltpu.VMEM((128, 128), f32),
            pltpu.SemaphoreType.DMA((4 + (n - 1) * CHUNKS,)),
        ],
        moved=4 * half * cols,
    )
    def exchange(parts):
        return [lax.ppermute(p, "seq", flipped(n, bits)) for p, bits in zip(parts, partners(n))]

    def join(*groups):
        outs = tuple(like(n - 1, *group[0].shape) for group in groups)
        args = [a for group in groups for a in group]
        return call(join_body, outs, [sc] + args, moved=4 * sum(a.size for a in args))

    merged = (wq.astype(f32) + jnp.dot(down, up, preferred_element_type=f32)).astype(bf)
    _, one, two, three = gather_line(parts)
    by_bits = {1: one, 2: two, 3: three}
    packs = [by_bits[b] for b in partners(n)]
    moved = [exchange(units[: n - 1])]
    held = lax.optimization_barrier((*moved[0], *packs, merged))
    moved[0], packs, merged = list(held[: n - 1]), list(held[n - 1 : -1]), held[-1]
    moved.append(exchange(units[n - 1 :]))
    share, stack = join(moved[0], packs)
    passed = [[lax.ppermute(share, "groups", flipped(2, 1))]]
    across = lax.ppermute(stack, "head", flipped(nh, 2))
    shapes = ((rank, wide), (rows, wide), (per, nope, kvr), (per, kvr, vdim))
    picked = call(
        pick_body,
        tuple(like(*shape) for shape in shapes),
        [sc, up, wq, ku, vu],
        hbm=range(1, 5),
        scratch=[pltpu.SemaphoreType.DMA((4,))],
        moved=4 * sum(math.prod(shape) for shape in shapes),
    )
    across, *rest = lax.optimization_barrier((across, *moved[1], *picked))
    moved[1], picked = rest[: n - 1], rest[n - 1 :]
    stacks = [
        lax.ppermute(stack, "head", flipped(nh, 1)),
        across,
        lax.ppermute(across, "head", flipped(nh, 1)),
    ]
    passed.append([lax.ppermute(p, "groups", flipped(2, 1)) for p in moved[1]])

    scale = 1.0 / math.sqrt(nope + rope)
    raw = pltpu.VMEM((n * rows, wide), bf)
    cost = dict(
        flops=2 * tokens * per * (depth * wide // per + 2 * nope * kvr + 2 * tokens * kvr),
        moved=4 * n * rows * wide,
    )
    ho, *kept = call(
        functools.partial(attend_first, n, nh, kq, vq, aq, nope, scale),
        (
            like(tokens, per * vdim),
            like(tokens, depth),
            like(tokens, kvr + rope),
            like(rank, n * rows),
            like(tokens, tokens, dtype=f32),
            *(like(*shape) for shape in shapes),
        ),
        [sc, x, kv, at, pos2] + moved[0] + passed[0] + stacks + packs + picked + [up, wq, ku, vu],
        hbm=range(7 + 2 * n + nh, 11 + 2 * n + nh),
        scratch=[pltpu.VMEM((128, 128), f32), raw]
        + [pltpu.SemaphoreType.DMA((4,))],
        **cost,
    )
    slots = [gather_line(ho)]
    ho = call(
        functools.partial(attend_next, n, nope, scale),
        like(tokens, per * vdim),
        [sc] + kept[:4] + moved[1] + passed[1] + kept[4:],
        scratch=[raw],
        **cost,
    )
    w4 = wo.reshape(n, CHUNKS, per * vdim, wo.shape[1])
    total = wo.shape[1]
    width = per * vdim

    def room(pieces):
        return [
            pltpu.VMEM((tokens, len(pieces) * width), bf),
            pltpu.VMEM((len(pieces), width, total), bf),
        ]

    def work(pieces):
        rows = len(pieces) * width
        return dict(flops=2 * tokens * rows * total, moved=2 * rows * total)

    def pick(pieces):
        return [slots[c][bits] for bits, c in pieces]

    slots.append([ho])
    acc, token, w_middle, w_late = call(
        early_body,
        (
            like(tokens, total, dtype=f32),
            like(8, 128, dtype=f32),
            like(len(MIDDLE), width, total),
            like(len(LATE), width, total),
        ),
        [sc] + pick(EARLY) + [w4],
        hbm=(1 + len(EARLY),),
        scratch=room(EARLY) + [pltpu.SemaphoreType.DMA((len(EARLY + MIDDLE + LATE),))],
        **work(EARLY),
    )
    *slots[1], token = gather_line(ho, token)
    late = pick(LATE)
    acc = call(
        middle_body,
        like(tokens, total, dtype=f32),
        [sc] + pick(MIDDLE) + [w_middle, acc, token],
        scratch=room(MIDDLE)[:1],
        alias={2 + len(MIDDLE): 0},
        **work(MIDDLE),
    )
    keep, send = call(
        functools.partial(last_body, nh, tok),
        (like(nh // 2 * tok, total, dtype=f32), like(nh // 2 * tok, total)),
        [sc] + late + [w_late, acc],
        **work(LATE),
    )
    got = lax.ppermute(send, "head", flipped(nh, 1))
    pair = (keep + got.astype(f32)).reshape(nh // 2, tok, total)
    side = h // 2
    out = lax.dynamic_index_in_dim(pair, side, 0, keepdims=False)
    away = lax.dynamic_index_in_dim(pair, 1 - side, 0, keepdims=False).astype(bf)
    out = out + lax.ppermute(away, "head", flipped(nh, 2)).astype(f32)
    return merged, out.astype(bf)


def fits(mesh, shapes):
    n, nh = mesh.shape["seq"], mesh.shape["head"]
    x, kv, _, wq, down, _, ku, vu, wo = shapes
    tok, kvr, rank = x[0], ku[2], down[1]
    if mesh.shape["groups"] != 2 or n != 4 or nh != 4 or CHUNKS != 2 or ku[0] % (n * CHUNKS):
        return False
    wide = wq[1] // n // CHUNKS
    return (
        (tok + rank // nh) % 48 == 0
        and tok % 16 == 0
        and tok + 3 <= 128
        and rank <= 128
        and rank // nh % 16 == 0
        and kv[1] - kvr == rank
        and kvr // nh == 128
        and x[1] // nh == wide
        and down[0] == wide
        and wide == 3 * 128
        and wo[1] % 128 == 0
    )


def solution(mesh):
    placed = (
        P(("groups", "seq"), None),
        P(("groups", "seq"), None),
        P(("groups", "seq")),
        P("seq", "head"),
        P(("groups", "seq"), None),
        P("groups", "head"),
        P("head", None, None),
        P("head", None, None),
        P("head", "seq"),
    )

    def local(*args):
        chosen = by_heads if fits(mesh, [a.shape for a in args]) else on_device
        return chosen(*args)

    return jax.shard_map(
        local,
        mesh=mesh,
        in_specs=placed,
        out_specs=(P(("groups", "seq"), "head"), P(("groups", "head"), "seq")),
        check_vma=False,
    )
```

```python
import functools
import math

import jax
import jax.numpy as jnp
from jax import lax
from jax.experimental import pallas as pl
from jax.experimental.pallas import tpu as pltpu
from jax.sharding import PartitionSpec as P

CHUNKS = 2
VMEM_BYTES = 20 * 1024 * 1024
TILE = 512
W_PARTS = 4
HEAD_PARTS = 2
PACK_PARTS = 4


def on_device(
    query_latent_rows,
    key_value_latents,
    positions,
    query_up_weight,
    adapter_down_factor,
    adapter_up_factor,
    head_key_up_weight,
    head_value_up_weight,
    output_projection_weight,
):
    merged_query_weight = (
        query_up_weight.astype(jnp.float32)
        + jnp.dot(adapter_down_factor, adapter_up_factor, preferred_element_type=jnp.float32)
    ).astype(jnp.bfloat16)
    tok_rows = query_latent_rows.shape[0]
    queries = jnp.dot(
        query_latent_rows,
        lax.all_gather(merged_query_weight, "seq", axis=0, tiled=True),
        preferred_element_type=jnp.float32,
    )
    heads_dev = head_key_up_weight.shape[0]
    nope_dim = head_key_up_weight.shape[1]
    kv_rank = head_key_up_weight.shape[2]
    lat_width = key_value_latents.shape[1]
    score_scale = 1.0 / math.sqrt(nope_dim + lat_width - kv_rank)
    queries = queries.astype(jnp.bfloat16).reshape(tok_rows, heads_dev, -1)
    absorbed = jnp.einsum(
        "thn,hnk->thk",
        queries[:, :, :nope_dim],
        head_key_up_weight,
        preferred_element_type=jnp.float32,
    ).astype(jnp.bfloat16)
    full_query = jnp.concatenate([absorbed, queries[:, :, nope_dim:]], axis=2).reshape(
        tok_rows * heads_dev, lat_width
    )
    query_pos = jnp.repeat(positions, heads_dev)
    q_count = tok_rows * heads_dev
    row_max = jnp.full((q_count,), -1e30, jnp.float32)
    key_rows = lax.all_gather(key_value_latents, "seq", axis=0, tiled=True)
    key_pos = lax.all_gather(positions, "seq", axis=0, tiled=True)
    visible = key_pos[None, :] <= query_pos[:, None]
    scores = (
        lax.dot_general(
            full_query, key_rows, (((1,), (1,)), ((), ())), preferred_element_type=jnp.float32
        )
        * score_scale
    )
    scores = jnp.where(visible, scores, jnp.float32(-1e30))
    new_max = jnp.maximum(row_max, jnp.max(scores, axis=1))
    weights = jnp.where(visible, jnp.exp(scores - new_max[:, None]), jnp.float32(0.0))
    row_sum = jnp.sum(weights, axis=1)
    running = jnp.dot(
        weights.astype(jnp.bfloat16), key_rows[:, :kv_rank], preferred_element_type=jnp.float32
    )
    row_max, row_sum, running = (new_max, row_sum, running)
    context_output = (
        (running / row_sum[:, None]).astype(jnp.bfloat16).reshape(tok_rows, heads_dev, kv_rank)
    )
    heads_out = (
        jnp.einsum(
            "euw,uwz->euz", context_output, head_value_up_weight, preferred_element_type=jnp.float32
        )
        .astype(jnp.bfloat16)
        .reshape(tok_rows, -1)
    )
    partial_value = jnp.dot(
        lax.all_gather(heads_out, "seq", axis=0, tiled=True),
        output_projection_weight,
        preferred_element_type=jnp.float32,
    )
    mixed = lax.psum_scatter(
        partial_value.astype(jnp.bfloat16), "head", scatter_dimension=0, tiled=True
    )
    return (merged_query_weight, mixed)


def flipped(n, bit):
    return [(i, i ^ bit) for i in range(n)]


def partners(n):
    return [2, 3, 1]


def call(body, outs, args, hbm=(), scratch=(), alias=None, flops=0, moved=0):
    vmem = pl.BlockSpec(memory_space=pltpu.VMEM)
    far = pl.BlockSpec(memory_space=pl.ANY)
    args = [pltpu.with_memory_space_constraint(a, pltpu.HBM) if i in hbm else a for i, a in enumerate(args)]
    return pl.pallas_call(
        body,
        out_shape=outs,
        grid_spec=pltpu.PrefetchScalarGridSpec(
            num_scalar_prefetch=1,
            grid=(1,),
            in_specs=[far if i in hbm else vmem for i in range(1, len(args))],
            out_specs=jax.tree.map(lambda o: vmem, outs),
            scratch_shapes=list(scratch),
        ),
        input_output_aliases=alias or {},
        compiler_params=pltpu.CompilerParams(vmem_limit_bytes=VMEM_BYTES),
        cost_estimate=pl.CostEstimate(flops=flops, bytes_accessed=moved, transcendentals=0),
    )(*args)


def fetch(pairs, sems):
    copies = [pltpu.make_async_copy(a, b, sems.at[i]) for i, (a, b) in enumerate(pairs)]
    for copy in copies:
        copy.start()
    return copies


def three_terms(p):
    out = []
    for _ in range(3):
        t = p.astype(jnp.bfloat16).astype(jnp.float32)
        out.append(t)
        p = p - t
    return out


def pack_body(n, kq, vq, aq, wide, kvr, sc, x_ref, kv_ref, at_ref, pos_ref, w_ref, *rest):
    count = CHUNKS * (n - 1)
    parts, outs, (xs, kvs, ats, ps, turn, turned, sems) = rest[0], rest[1 : 1 + count], rest[1 + count :]
    s, g, h = sc[0], sc[1], sc[2]
    tok = x_ref.shape[0]
    rope = kv_ref.shape[1] - kvr
    half = outs[-1].shape[0]
    small = [
        (x_ref.at[:, pl.ds(pl.multiple_of(h * kq, 128), kq)], xs),
        (kv_ref, kvs),
        (at_ref.at[pl.ds(pl.multiple_of(h * aq, 16), aq), :], ats),
        (pos_ref, ps),
    ]
    mine = pl.ds(pl.multiple_of(g * half, 16), half)
    large = []
    for c in range(CHUNKS):
        for k, bits in enumerate(partners(n)):
            chunk = (s ^ bits) * CHUNKS + c
            columns = pl.ds(pl.multiple_of(chunk * wide, 128), wide)
            large.append((w_ref.at[mine, columns], outs[c * (n - 1) + k]))
    copies = fetch(small + large, sems)
    turn[...] = jnp.zeros_like(turn)
    for copy in copies[: len(small)]:
        copy.wait()
    turn[:tok, :rope] = kvs[:, kvr:].astype(jnp.float32)
    start = ps[0:1, 0:1].astype(jnp.float32)
    for i, t in enumerate(three_terms(start)):
        turn[tok + i : tok + i + 1, :] = jnp.broadcast_to(t, (1, turn.shape[1]))
    turned[...] = turn[...].T
    keys = kvs[:, pl.ds(pl.multiple_of(h * vq, 128), vq)]
    ropes = turned[pl.ds(pl.multiple_of(h * aq, 16), aq), :].astype(jnp.bfloat16)
    third = (tok + aq) // 3
    tail = jnp.concatenate([keys, ropes], axis=0)
    parts[:tok, :] = xs[...]
    parts[tok : tok + aq, :] = ats[...]
    for i in range(3):
        parts[tok + aq :, i * vq : (i + 1) * vq] = tail[i * third : (i + 1) * third]
    for copy in copies[len(small) :]:
        copy.wait()


def join_body(sc, *refs):
    outs = [ref for ref in refs if len(ref.shape) == 3]
    count = (len(refs) - len(outs)) // len(outs)
    for i, out in enumerate(outs):
        for k in range(count):
            out[k] = refs[i * count + k][...]


def unpack(n, nh, kq, vq, aq, sc, own, packs, stacks, outs, turn):
    (x_ref, kv_ref, at_ref, pos_ref), (xo, kvo, ao, bias) = own, outs
    s, h = sc[0], sc[2]
    tok, depth = x_ref.shape[0], at_ref.shape[1]
    kvr = vq * nh
    rope = kv_ref.shape[1] - kvr
    third = (tok + aq) // 3
    tokens = bias.shape[0]
    row = pl.multiple_of(s * tok, 16)
    xo[pl.ds(row, tok), :] = x_ref[...]
    kvo[pl.ds(row, tok), :] = kv_ref[...]
    ao[:, pl.ds(pl.multiple_of(s * depth, 128), depth)] = at_ref[...]
    starts = [(s, pos_ref[0:1, 0:1].astype(jnp.float32))]
    turn[...] = jnp.zeros_like(turn)
    for k, bits in enumerate(partners(n)):
        src = s ^ bits
        rows = pl.ds(pl.multiple_of(src * tok, 16), tok)
        for j in range(nh):
            hh = h ^ j
            got = stacks[j - 1].at[k] if j else packs[k]
            xo[rows, pl.ds(pl.multiple_of(hh * kq, 128), kq)] = got[:tok, :]
            arow = pl.ds(pl.multiple_of(hh * aq, 16), aq)
            ao[arow, pl.ds(pl.multiple_of(src * depth, 128), depth)] = got[tok : tok + aq, :]
            tail = jnp.concatenate([got[tok + aq :, i * vq : (i + 1) * vq] for i in range(3)], axis=0)
            kvo[rows, pl.ds(pl.multiple_of(hh * vq, 128), vq)] = tail[:tok]
            turn[arow, :] = tail[tok:].astype(jnp.float32)
        turned = turn[...].T
        kvo[rows, kvr:] = turned[:tok, :rope].astype(jnp.bfloat16)
        terms = [turned[tok + i : tok + i + 1, :1] for i in range(3)]
        starts.append((src, terms[0] + terms[1] + terms[2]))

    def places(shape, dim):
        index = lax.broadcasted_iota(jnp.int32, shape, dim)
        block = index // tok
        out = (index - block * tok).astype(jnp.float32)
        for src, start in starts:
            out = out + jnp.where(block == src, start, 0.0)
        return out

    seen = places((1, tokens), 1) <= places((tokens, 1), 0)
    bias[...] = jnp.where(seen, 0.0, -1e30)


def own_weights(sc, c, weights, outs):
    b_ref, w_ref, ku_ref, vu_ref = weights
    b, w, ku, vu = outs
    wide, heads = w.shape[1], ku.shape[0]
    chunk = sc[0] * CHUNKS + c
    columns = pl.ds(pl.multiple_of(chunk * wide, 128), wide)
    return [
        (b_ref.at[:, columns], b),
        (w_ref.at[:, columns], w),
        (ku_ref.at[pl.ds(chunk * heads, heads)], ku),
        (vu_ref.at[pl.ds(chunk * heads, heads)], vu),
    ]


def attend(n, nope, scale, sc, shared, units, ys, weights, out, raw, before=None, copies=()):
    x_ref, kv_ref, at_ref, bias_ref = shared
    b_own, w_own, ku, vu = weights
    s, g = sc[0], sc[1]
    depth, wide = w_own.shape
    half = depth // 2
    heads, kvr, vdim = vu.shape
    if before is not None:
        before()
    for k, bits in enumerate(partners(n)):
        src = s ^ bits
        raw[pl.ds(pl.multiple_of(src * depth + g * half, 16), half), :] = units[k][:half]
        raw[pl.ds(pl.multiple_of(src * depth + (1 - g) * half, 16), half), :] = ys[k][...]
    for copy in copies[:2]:
        copy.wait()
    raw[pl.ds(pl.multiple_of(s * depth, 16), depth), :] = w_own[...]

    def merge(rows):
        add = lax.dot_general(
            at_ref[:, rows], b_own[...], (((0,), (0,)), ((), ())), preferred_element_type=jnp.float32
        )
        raw[rows, :] = (raw[rows, :].astype(jnp.float32) + add).astype(jnp.bfloat16)

    for src in range(n):
        merge(slice(src * depth, (src + 1) * depth))
    q = jnp.dot(x_ref[...], raw[...], preferred_element_type=jnp.float32)
    for copy in copies[2:]:
        copy.wait()
    width = wide // heads
    lat, rope_key = kv_ref[:, :kvr], kv_ref[:, kvr:]
    bias = bias_ref[...]
    nt = (((1,), (1,)), ((), ()))
    for j in range(heads):
        qn = q[:, j * width : j * width + nope].astype(jnp.bfloat16)
        qr = q[:, j * width + nope : (j + 1) * width].astype(jnp.bfloat16)
        absorbed = jnp.dot(qn, ku[j], preferred_element_type=jnp.float32).astype(jnp.bfloat16)
        scores = lax.dot_general(absorbed, lat, nt, preferred_element_type=jnp.float32)
        scores = scores + lax.dot_general(qr, rope_key, nt, preferred_element_type=jnp.float32)
        scores = scores * scale + bias
        top = jnp.max(scores, axis=1, keepdims=True)
        e = jnp.exp(scores - top)
        total = jnp.sum(e, axis=1, keepdims=True)
        ctx = jnp.dot(e.astype(jnp.bfloat16), lat, preferred_element_type=jnp.float32)
        ctx = (ctx / total).astype(jnp.bfloat16)
        ho = jnp.dot(ctx, vu[j], preferred_element_type=jnp.float32)
        out[:, j * vdim : (j + 1) * vdim] = ho.astype(jnp.bfloat16)


def pick_body(sc, *refs):
    far, outs, sems = refs[:4], refs[4:8], refs[8]
    for copy in fetch(own_weights(sc, 0, far, outs), sems):
        copy.wait()


def attend_first(n, nh, kq, vq, aq, nope, scale, sc, *refs):
    own, units, y_ref, stacks = refs[:4], refs[4 : 3 + n], refs[3 + n], refs[4 + n : 3 + n + nh]
    packs, refs = refs[3 + n + nh : 2 + 2 * n + nh], refs[2 + 2 * n + nh :]
    weights, far, out, shared, later = refs[:4], refs[4:8], refs[8], refs[9:13], refs[13:17]
    turn, raw, sems = refs[17:]
    copies = fetch(own_weights(sc, CHUNKS - 1, far, later), sems)

    def before():
        unpack(n, nh, kq, vq, aq, sc, own, packs, stacks, shared, turn)

    ys = [y_ref.at[k] for k in range(n - 1)]
    attend(n, nope, scale, sc, shared, units, ys, weights, out, raw, before)
    for copy in copies:
        copy.wait()


def attend_next(n, nope, scale, sc, *refs):
    shared, units, ys, refs = refs[:4], refs[4 : 3 + n], refs[3 + n : 2 + 2 * n], refs[2 + 2 * n :]
    attend(n, nope, scale, sc, shared, units, ys, refs[:4], refs[4], refs[5])


def gather_line(x, *held):
    two = lax.ppermute(x, "seq", flipped(4, 2))
    one = lax.ppermute(x, "seq", flipped(4, 1))
    two, one, *held = lax.optimization_barrier((two, one) + held)
    return [x, one, two, lax.ppermute(two, "seq", flipped(4, 1))] + held


EARLY = ((0, 0), (1, 0), (2, 0), (0, 1))
MIDDLE = ((3, 0), (1, 1), (2, 1))
LATE = ((3, 1),)


def place(slots, lhs):
    for i, ref in enumerate(slots):
        width = ref.shape[1]
        lhs[:, i * width : (i + 1) * width] = ref[...]


def slabs(sc, w_ref, pieces, columns, out):
    return [(w_ref.at[sc[0] ^ bits, c, :, columns], out.at[i]) for i, (bits, c) in enumerate(pieces)]


def columns_dot(lhs, w, begin, end, put):
    for at in range(begin, end, TILE):
        stop = min(at + TILE, end)
        tile = w[:, :, at:stop]
        tile = tile.reshape(-1, tile.shape[-1])
        put(slice(at, stop), jnp.dot(lhs[...], tile, preferred_element_type=jnp.float32))


def early_body(sc, *refs):
    count = len(EARLY)
    slots, (w_ref, acc, token, middle, late, lhs, w, sems) = refs[:count], refs[count:]
    copies = fetch(
        slabs(sc, w_ref, EARLY, slice(None), w)
        + slabs(sc, w_ref, MIDDLE, slice(None), middle)
        + slabs(sc, w_ref, LATE, slice(None), late),
        sems,
    )
    place(slots, lhs)
    token[...] = jnp.zeros_like(token)
    for copy in copies[:count]:
        copy.wait()

    def put(band, value):
        acc[:, band] = value

    columns_dot(lhs, w, 0, acc.shape[1], put)
    for copy in copies[count:]:
        copy.wait()


def middle_body(sc, *refs):
    count = len(MIDDLE)
    slots, (w, before, token, acc, lhs) = refs[:count], refs[count:]
    del before, token
    place(slots, lhs)

    def add(band, value):
        acc[:, band] += value

    columns_dot(lhs, w, 0, acc.shape[1], add)


def last_body(tok, wanted, sc, *refs):
    slots, (w, acc, *outs) = refs[: len(LATE)], refs[len(LATE) :]
    outs = outs[-len(wanted) :]
    total = acc.shape[1]
    rows = [pl.ds(pl.multiple_of((sc[2] ^ bits) * tok, 16), tok) for bits in wanted]
    lhs = jnp.concatenate([slots[0][row, :] for row in rows], axis=0)
    for at in range(0, total, TILE):
        band = slice(at, min(at + TILE, total))
        more = jnp.dot(lhs, w[0, :, band], preferred_element_type=jnp.float32)
        for i, (row, out) in enumerate(zip(rows, outs)):
            part = acc[row, band] + more[i * tok : (i + 1) * tok]
            out[:, band] = part.astype(out.dtype)


def by_heads(x, kv, pos, wq, down, up, ku, vu, wo):
    n, nh = lax.axis_size("seq"), lax.axis_size("head")
    s, g, h = lax.axis_index("seq"), lax.axis_index("groups"), lax.axis_index("head")
    sc = jnp.stack([s, g, h]).astype(jnp.int32)
    bf, f32 = jnp.bfloat16, jnp.float32
    tok, depth = x.shape
    heads, nope, kvr = ku.shape
    vdim = vu.shape[2]
    rope = kv.shape[1] - kvr
    rank = down.shape[1]
    rows, cols = wq.shape
    half = rows // 2
    tokens = n * tok
    per = heads // n // CHUNKS
    wide = per * (cols // heads)
    kq, vq, aq = depth // nh, kvr // nh, rank // nh
    extra = tok + aq + (tok + aq) // 3
    at = down.T
    pos2 = pos[None, :]

    def like(*shape, dtype=bf):
        return jax.ShapeDtypeStruct(shape, dtype)

    parts, *units = call(
        functools.partial(pack_body, n, kq, vq, aq, wide, kvr),
        (like(extra, wide), *[like(half, wide)] * (n - 1) * CHUNKS),
        [sc, x, kv, at, pos2, wq],
        hbm=range(1, 6),
        scratch=[
            pltpu.VMEM((tok, kq), bf),
            pltpu.VMEM(kv.shape, bf),
            pltpu.VMEM((aq, rows), bf),
            pltpu.VMEM(pos2.shape, jnp.int32),
            pltpu.VMEM((128, 128), f32),
            pltpu.VMEM((128, 128), f32),
            pltpu.SemaphoreType.DMA((4 + (n - 1) * CHUNKS,)),
        ],
        moved=4 * half * cols,
    )
    def exchange(parts):
        return [lax.ppermute(p, "seq", flipped(n, bits)) for p, bits in zip(parts, partners(n))]

    def join(*groups):
        outs = tuple(like(n - 1, *group[0].shape) for group in groups)
        args = [a for group in groups for a in group]
        return call(join_body, outs, [sc] + args, moved=4 * sum(a.size for a in args))

    merged = (wq.astype(f32) + jnp.dot(down, up, preferred_element_type=f32)).astype(bf)
    _, one, two, three = gather_line(parts)
    by_bits = {1: one, 2: two, 3: three}
    packs = [by_bits[b] for b in partners(n)]
    moved = [exchange(units[: n - 1])]
    held = lax.optimization_barrier((*moved[0], *packs, merged))
    moved[0], packs, merged = list(held[: n - 1]), list(held[n - 1 : -1]), held[-1]
    moved.append(exchange(units[n - 1 :]))
    share, stack = join(moved[0], packs)
    passed = [[lax.ppermute(share, "groups", flipped(2, 1))]]
    across = lax.ppermute(stack, "head", flipped(nh, 2))
    shapes = ((rank, wide), (rows, wide), (per, nope, kvr), (per, kvr, vdim))
    picked = call(
        pick_body,
        tuple(like(*shape) for shape in shapes),
        [sc, up, wq, ku, vu],
        hbm=range(1, 5),
        scratch=[pltpu.SemaphoreType.DMA((4,))],
        moved=4 * sum(math.prod(shape) for shape in shapes),
    )
    across, *rest = lax.optimization_barrier((across, *moved[1], *picked))
    moved[1], picked = rest[: n - 1], rest[n - 1 :]
    stacks = [
        lax.ppermute(stack, "head", flipped(nh, 1)),
        across,
        lax.ppermute(across, "head", flipped(nh, 1)),
    ]
    passed.append([lax.ppermute(p, "groups", flipped(2, 1)) for p in moved[1][:-1]])

    scale = 1.0 / math.sqrt(nope + rope)
    raw = pltpu.VMEM((n * rows, wide), bf)
    cost = dict(
        flops=2 * tokens * per * (depth * wide // per + 2 * nope * kvr + 2 * tokens * kvr),
        moved=4 * n * rows * wide,
    )
    ho, *kept = call(
        functools.partial(attend_first, n, nh, kq, vq, aq, nope, scale),
        (
            like(tokens, per * vdim),
            like(tokens, depth),
            like(tokens, kvr + rope),
            like(rank, n * rows),
            like(tokens, tokens, dtype=f32),
            *(like(*shape) for shape in shapes),
        ),
        [sc, x, kv, at, pos2] + moved[0] + passed[0] + stacks + packs + picked + [up, wq, ku, vu],
        hbm=range(7 + 2 * n + nh, 11 + 2 * n + nh),
        scratch=[pltpu.VMEM((128, 128), f32), raw]
        + [pltpu.SemaphoreType.DMA((4,))],
        **cost,
    )
    moved[1][-1], ho = lax.optimization_barrier((moved[1][-1], ho))
    passed[1].append(lax.ppermute(moved[1][-1], "groups", flipped(2, 1)))
    slots = [gather_line(ho)]
    ho = call(
        functools.partial(attend_next, n, nope, scale),
        like(tokens, per * vdim),
        [sc] + kept[:4] + moved[1] + passed[1] + kept[4:],
        scratch=[raw],
        **cost,
    )
    w4 = wo.reshape(n, CHUNKS, per * vdim, wo.shape[1])
    total = wo.shape[1]
    width = per * vdim

    def room(pieces):
        return [
            pltpu.VMEM((tokens, len(pieces) * width), bf),
            pltpu.VMEM((len(pieces), width, total), bf),
        ]

    def work(pieces):
        rows = len(pieces) * width
        return dict(flops=2 * tokens * rows * total, moved=2 * rows * total)

    def pick(pieces):
        return [slots[c][bits] for bits, c in pieces]

    slots.append([ho])
    acc, token, w_middle, w_late = call(
        early_body,
        (
            like(tokens, total, dtype=f32),
            like(8, 128, dtype=f32),
            like(len(MIDDLE), width, total),
            like(len(LATE), width, total),
        ),
        [sc] + pick(EARLY) + [w4],
        hbm=(1 + len(EARLY),),
        scratch=room(EARLY) + [pltpu.SemaphoreType.DMA((len(EARLY + MIDDLE + LATE),))],
        **work(EARLY),
    )
    *slots[1], token = gather_line(ho, token)
    late = pick(LATE)
    acc = call(
        middle_body,
        like(tokens, total, dtype=f32),
        [sc] + pick(MIDDLE) + [w_middle, acc, token],
        scratch=room(MIDDLE)[:1],
        alias={2 + len(MIDDLE): 0},
        **work(MIDDLE),
    )
    def last(*wanted, after=()):
        return call(
            functools.partial(last_body, tok, [bits for bits, _ in wanted]),
            tuple(like(tok, total, dtype=kind) for _, kind in wanted),
            [sc] + late + [w_late, acc, *after],
            flops=2 * len(wanted) * tok * width * total,
            moved=8 * len(wanted) * tok * total,
        )

    (send_away,) = last((3, bf))
    keep_away, send_home, keep_home = last((2, f32), (1, bf), (0, f32), after=[send_away])
    away = keep_away + lax.ppermute(send_away, "head", flipped(nh, 1)).astype(f32)
    got = lax.ppermute(away.astype(bf), "head", flipped(nh, 2))
    home = keep_home + lax.ppermute(send_home, "head", flipped(nh, 1)).astype(f32)
    return merged, (home + got.astype(f32)).astype(bf)


def fits(mesh, shapes):
    n, nh = mesh.shape["seq"], mesh.shape["head"]
    x, kv, _, wq, down, _, ku, vu, wo = shapes
    tok, kvr, rank = x[0], ku[2], down[1]
    if mesh.shape["groups"] != 2 or n != 4 or nh != 4 or CHUNKS != 2 or ku[0] % (n * CHUNKS):
        return False
    wide = wq[1] // n // CHUNKS
    return (
        (tok + rank // nh) % 48 == 0
        and tok % 16 == 0
        and tok + 3 <= 128
        and rank <= 128
        and rank // nh % 16 == 0
        and kv[1] - kvr == rank
        and kvr // nh == 128
        and x[1] // nh == wide
        and down[0] == wide
        and wide == 3 * 128
        and wo[1] % 128 == 0
    )


def solution(mesh):
    placed = (
        P(("groups", "seq"), None),
        P(("groups", "seq"), None),
        P(("groups", "seq")),
        P("seq", "head"),
        P(("groups", "seq"), None),
        P("groups", "head"),
        P("head", None, None),
        P("head", None, None),
        P("head", "seq"),
    )

    def local(*args):
        chosen = by_heads if fits(mesh, [a.shape for a in args]) else on_device
        return chosen(*args)

    return jax.shard_map(
        local,
        mesh=mesh,
        in_specs=placed,
        out_specs=(P(("groups", "seq"), "head"), P(("groups", "head"), "seq")),
        check_vma=False,
    )
```

```python
import functools
import math

import jax
import jax.numpy as jnp
from jax import lax
from jax.experimental import pallas as pl
from jax.experimental.pallas import tpu as pltpu
from jax.sharding import PartitionSpec as P

CHUNKS = 2
VMEM_BYTES = 20 * 1024 * 1024
TILE = 512
W_PARTS = 4
HEAD_PARTS = 2
PACK_PARTS = 4


def on_device(
    query_latent_rows,
    key_value_latents,
    positions,
    query_up_weight,
    adapter_down_factor,
    adapter_up_factor,
    head_key_up_weight,
    head_value_up_weight,
    output_projection_weight,
):
    merged_query_weight = (
        query_up_weight.astype(jnp.float32)
        + jnp.dot(adapter_down_factor, adapter_up_factor, preferred_element_type=jnp.float32)
    ).astype(jnp.bfloat16)
    tok_rows = query_latent_rows.shape[0]
    queries = jnp.dot(
        query_latent_rows,
        lax.all_gather(merged_query_weight, "seq", axis=0, tiled=True),
        preferred_element_type=jnp.float32,
    )
    heads_dev = head_key_up_weight.shape[0]
    nope_dim = head_key_up_weight.shape[1]
    kv_rank = head_key_up_weight.shape[2]
    lat_width = key_value_latents.shape[1]
    score_scale = 1.0 / math.sqrt(nope_dim + lat_width - kv_rank)
    queries = queries.astype(jnp.bfloat16).reshape(tok_rows, heads_dev, -1)
    absorbed = jnp.einsum(
        "thn,hnk->thk",
        queries[:, :, :nope_dim],
        head_key_up_weight,
        preferred_element_type=jnp.float32,
    ).astype(jnp.bfloat16)
    full_query = jnp.concatenate([absorbed, queries[:, :, nope_dim:]], axis=2).reshape(
        tok_rows * heads_dev, lat_width
    )
    query_pos = jnp.repeat(positions, heads_dev)
    q_count = tok_rows * heads_dev
    row_max = jnp.full((q_count,), -1e30, jnp.float32)
    key_rows = lax.all_gather(key_value_latents, "seq", axis=0, tiled=True)
    key_pos = lax.all_gather(positions, "seq", axis=0, tiled=True)
    visible = key_pos[None, :] <= query_pos[:, None]
    scores = (
        lax.dot_general(
            full_query, key_rows, (((1,), (1,)), ((), ())), preferred_element_type=jnp.float32
        )
        * score_scale
    )
    scores = jnp.where(visible, scores, jnp.float32(-1e30))
    new_max = jnp.maximum(row_max, jnp.max(scores, axis=1))
    weights = jnp.where(visible, jnp.exp(scores - new_max[:, None]), jnp.float32(0.0))
    row_sum = jnp.sum(weights, axis=1)
    running = jnp.dot(
        weights.astype(jnp.bfloat16), key_rows[:, :kv_rank], preferred_element_type=jnp.float32
    )
    row_max, row_sum, running = (new_max, row_sum, running)
    context_output = (
        (running / row_sum[:, None]).astype(jnp.bfloat16).reshape(tok_rows, heads_dev, kv_rank)
    )
    heads_out = (
        jnp.einsum(
            "euw,uwz->euz", context_output, head_value_up_weight, preferred_element_type=jnp.float32
        )
        .astype(jnp.bfloat16)
        .reshape(tok_rows, -1)
    )
    partial_value = jnp.dot(
        lax.all_gather(heads_out, "seq", axis=0, tiled=True),
        output_projection_weight,
        preferred_element_type=jnp.float32,
    )
    mixed = lax.psum_scatter(
        partial_value.astype(jnp.bfloat16), "head", scatter_dimension=0, tiled=True
    )
    return (merged_query_weight, mixed)


def flipped(n, bit):
    return [(i, i ^ bit) for i in range(n)]


def partners(n):
    return [2, 3, 1]


def call(body, outs, args, hbm=(), scratch=(), alias=None, flops=0, moved=0):
    vmem = pl.BlockSpec(memory_space=pltpu.VMEM)
    far = pl.BlockSpec(memory_space=pl.ANY)
    args = [pltpu.with_memory_space_constraint(a, pltpu.HBM) if i in hbm else a for i, a in enumerate(args)]
    return pl.pallas_call(
        body,
        out_shape=outs,
        grid_spec=pltpu.PrefetchScalarGridSpec(
            num_scalar_prefetch=1,
            grid=(1,),
            in_specs=[far if i in hbm else vmem for i in range(1, len(args))],
            out_specs=jax.tree.map(lambda o: vmem, outs),
            scratch_shapes=list(scratch),
        ),
        input_output_aliases=alias or {},
        compiler_params=pltpu.CompilerParams(vmem_limit_bytes=VMEM_BYTES),
        cost_estimate=pl.CostEstimate(flops=flops, bytes_accessed=moved, transcendentals=0),
    )(*args)


def fetch(pairs, sems):
    copies = [pltpu.make_async_copy(a, b, sems.at[i]) for i, (a, b) in enumerate(pairs)]
    for copy in copies:
        copy.start()
    return copies


def three_terms(p):
    out = []
    for _ in range(3):
        t = p.astype(jnp.bfloat16).astype(jnp.float32)
        out.append(t)
        p = p - t
    return out


def pack_body(n, kq, vq, aq, wide, kvr, sc, x_ref, kv_ref, at_ref, pos_ref, w_ref, *rest):
    count = CHUNKS * (n - 1)
    parts, outs, (xs, kvs, ats, ps, turn, turned, sems) = rest[0], rest[1 : 1 + count], rest[1 + count :]
    s, g, h = sc[0], sc[1], sc[2]
    tok = x_ref.shape[0]
    rope = kv_ref.shape[1] - kvr
    half = outs[-1].shape[0]
    small = [
        (x_ref.at[:, pl.ds(pl.multiple_of(h * kq, 128), kq)], xs),
        (kv_ref, kvs),
        (at_ref.at[pl.ds(pl.multiple_of(h * aq, 16), aq), :], ats),
        (pos_ref, ps),
    ]
    mine = pl.ds(pl.multiple_of(g * half, 16), half)
    large = []
    for c in range(CHUNKS):
        for k, bits in enumerate(partners(n)):
            chunk = (s ^ bits) * CHUNKS + c
            columns = pl.ds(pl.multiple_of(chunk * wide, 128), wide)
            large.append((w_ref.at[mine, columns], outs[c * (n - 1) + k]))
    copies = fetch(small + large, sems)
    turn[...] = jnp.zeros_like(turn)
    for copy in copies[: len(small)]:
        copy.wait()
    turn[:tok, :rope] = kvs[:, kvr:].astype(jnp.float32)
    start = ps[0:1, 0:1].astype(jnp.float32)
    for i, t in enumerate(three_terms(start)):
        turn[tok + i : tok + i + 1, :] = jnp.broadcast_to(t, (1, turn.shape[1]))
    turned[...] = turn[...].T
    keys = kvs[:, pl.ds(pl.multiple_of(h * vq, 128), vq)]
    ropes = turned[pl.ds(pl.multiple_of(h * aq, 16), aq), :].astype(jnp.bfloat16)
    third = (tok + aq) // 3
    tail = jnp.concatenate([keys, ropes], axis=0)
    parts[:tok, :] = xs[...]
    parts[tok : tok + aq, :] = ats[...]
    for i in range(3):
        parts[tok + aq :, i * vq : (i + 1) * vq] = tail[i * third : (i + 1) * third]
    for copy in copies[len(small) :]:
        copy.wait()


def join_body(sc, *refs):
    outs = [ref for ref in refs if len(ref.shape) == 3]
    count = (len(refs) - len(outs)) // len(outs)
    for i, out in enumerate(outs):
        for k in range(count):
            out[k] = refs[i * count + k][...]


def unpack(n, nh, kq, vq, aq, sc, own, packs, stacks, outs, turn):
    (x_ref, kv_ref, at_ref, pos_ref), (xo, kvo, ao, bias) = own, outs
    s, h = sc[0], sc[2]
    tok, depth = x_ref.shape[0], at_ref.shape[1]
    kvr = vq * nh
    rope = kv_ref.shape[1] - kvr
    third = (tok + aq) // 3
    tokens = bias.shape[0]
    row = pl.multiple_of(s * tok, 16)
    xo[pl.ds(row, tok), :] = x_ref[...]
    kvo[pl.ds(row, tok), :] = kv_ref[...]
    ao[:, pl.ds(pl.multiple_of(s * depth, 128), depth)] = at_ref[...]
    starts = [(s, pos_ref[0:1, 0:1].astype(jnp.float32))]
    turn[...] = jnp.zeros_like(turn)
    for k, bits in enumerate(partners(n)):
        src = s ^ bits
        rows = pl.ds(pl.multiple_of(src * tok, 16), tok)
        for j in range(nh):
            hh = h ^ j
            got = stacks[j - 1].at[k] if j else packs[k]
            xo[rows, pl.ds(pl.multiple_of(hh * kq, 128), kq)] = got[:tok, :]
            arow = pl.ds(pl.multiple_of(hh * aq, 16), aq)
            ao[arow, pl.ds(pl.multiple_of(src * depth, 128), depth)] = got[tok : tok + aq, :]
            tail = jnp.concatenate([got[tok + aq :, i * vq : (i + 1) * vq] for i in range(3)], axis=0)
            kvo[rows, pl.ds(pl.multiple_of(hh * vq, 128), vq)] = tail[:tok]
            turn[arow, :] = tail[tok:].astype(jnp.float32)
        turned = turn[...].T
        kvo[rows, kvr:] = turned[:tok, :rope].astype(jnp.bfloat16)
        terms = [turned[tok + i : tok + i + 1, :1] for i in range(3)]
        starts.append((src, terms[0] + terms[1] + terms[2]))

    def places(shape, dim):
        index = lax.broadcasted_iota(jnp.int32, shape, dim)
        block = index // tok
        out = (index - block * tok).astype(jnp.float32)
        for src, start in starts:
            out = out + jnp.where(block == src, start, 0.0)
        return out

    seen = places((1, tokens), 1) <= places((tokens, 1), 0)
    bias[...] = jnp.where(seen, 0.0, -1e30)


def own_weights(sc, c, weights, outs):
    b_ref, w_ref, ku_ref, vu_ref = weights
    b, w, ku, vu = outs
    wide, heads = w.shape[1], ku.shape[0]
    chunk = sc[0] * CHUNKS + c
    columns = pl.ds(pl.multiple_of(chunk * wide, 128), wide)
    return [
        (b_ref.at[:, columns], b),
        (w_ref.at[:, columns], w),
        (ku_ref.at[pl.ds(chunk * heads, heads)], ku),
        (vu_ref.at[pl.ds(chunk * heads, heads)], vu),
    ]


def attend(n, nope, scale, sc, shared, units, ys, weights, out, raw, before=None, copies=()):
    x_ref, kv_ref, at_ref, bias_ref = shared
    b_own, w_own, ku, vu = weights
    s, g = sc[0], sc[1]
    depth, wide = w_own.shape
    half = depth // 2
    heads, kvr, vdim = vu.shape
    if before is not None:
        before()
    for k, bits in enumerate(partners(n)):
        src = s ^ bits
        raw[pl.ds(pl.multiple_of(src * depth + g * half, 16), half), :] = units[k][:half]
        raw[pl.ds(pl.multiple_of(src * depth + (1 - g) * half, 16), half), :] = ys[k][...]
    for copy in copies[:2]:
        copy.wait()
    raw[pl.ds(pl.multiple_of(s * depth, 16), depth), :] = w_own[...]

    def merge(rows):
        add = lax.dot_general(
            at_ref[:, rows], b_own[...], (((0,), (0,)), ((), ())), preferred_element_type=jnp.float32
        )
        raw[rows, :] = (raw[rows, :].astype(jnp.float32) + add).astype(jnp.bfloat16)

    for src in range(n):
        merge(slice(src * depth, (src + 1) * depth))
    q = jnp.dot(x_ref[...], raw[...], preferred_element_type=jnp.float32)
    for copy in copies[2:]:
        copy.wait()
    width = wide // heads
    lat, rope_key = kv_ref[:, :kvr], kv_ref[:, kvr:]
    bias = bias_ref[...]
    nt = (((1,), (1,)), ((), ()))
    for j in range(heads):
        qn = q[:, j * width : j * width + nope].astype(jnp.bfloat16)
        qr = q[:, j * width + nope : (j + 1) * width].astype(jnp.bfloat16)
        absorbed = jnp.dot(qn, ku[j], preferred_element_type=jnp.float32).astype(jnp.bfloat16)
        scores = lax.dot_general(absorbed, lat, nt, preferred_element_type=jnp.float32)
        scores = scores + lax.dot_general(qr, rope_key, nt, preferred_element_type=jnp.float32)
        scores = scores * scale + bias
        top = jnp.max(scores, axis=1, keepdims=True)
        e = jnp.exp(scores - top)
        total = jnp.sum(e, axis=1, keepdims=True)
        ctx = jnp.dot(e.astype(jnp.bfloat16), lat, preferred_element_type=jnp.float32)
        ctx = (ctx / total).astype(jnp.bfloat16)
        ho = jnp.dot(ctx, vu[j], preferred_element_type=jnp.float32)
        out[:, j * vdim : (j + 1) * vdim] = ho.astype(jnp.bfloat16)


def pick_body(sc, *refs):
    far, outs, sems = refs[:4], refs[4:8], refs[8]
    for copy in fetch(own_weights(sc, 0, far, outs), sems):
        copy.wait()


def attend_first(n, nh, kq, vq, aq, nope, scale, sc, *refs):
    own, units, y_ref, stacks = refs[:4], refs[4 : 3 + n], refs[3 + n], refs[4 + n : 3 + n + nh]
    packs, refs = refs[3 + n + nh : 2 + 2 * n + nh], refs[2 + 2 * n + nh :]
    weights, far, out, shared, later = refs[:4], refs[4:8], refs[8], refs[9:13], refs[13:17]
    turn, raw, sems = refs[17:]
    copies = fetch(own_weights(sc, CHUNKS - 1, far, later), sems)

    def before():
        unpack(n, nh, kq, vq, aq, sc, own, packs, stacks, shared, turn)

    ys = [y_ref.at[k] for k in range(n - 1)]
    attend(n, nope, scale, sc, shared, units, ys, weights, out, raw, before)
    for copy in copies:
        copy.wait()


def attend_next(n, nope, scale, sc, *refs):
    shared, units, ys, refs = refs[:4], refs[4 : 3 + n], refs[3 + n : 2 + 2 * n], refs[2 + 2 * n :]
    attend(n, nope, scale, sc, shared, units, ys, refs[:4], refs[4], refs[5])


def gather_line(x, *held):
    two = lax.ppermute(x, "seq", flipped(4, 2))
    one = lax.ppermute(x, "seq", flipped(4, 1))
    two, one, *held = lax.optimization_barrier((two, one) + held)
    return [x, one, two, lax.ppermute(two, "seq", flipped(4, 1))] + held


EARLY = ((0, 0), (1, 0), (2, 0), (0, 1))
MIDDLE = ((3, 0), (1, 1), (2, 1))
LATE = ((3, 1),)


def place(slots, lhs):
    for i, ref in enumerate(slots):
        width = ref.shape[1]
        lhs[:, i * width : (i + 1) * width] = ref[...]


def slabs(sc, w_ref, pieces, columns, out):
    return [(w_ref.at[sc[0] ^ bits, c, :, columns], out.at[i]) for i, (bits, c) in enumerate(pieces)]


def columns_dot(lhs, w, begin, end, put):
    for at in range(begin, end, TILE):
        stop = min(at + TILE, end)
        tile = w[:, :, at:stop]
        tile = tile.reshape(-1, tile.shape[-1])
        put(slice(at, stop), jnp.dot(lhs[...], tile, preferred_element_type=jnp.float32))


def early_body(sc, *refs):
    count = len(EARLY)
    slots, (w_ref, acc, token, middle, late, lhs, w, sems) = refs[:count], refs[count:]
    copies = fetch(
        slabs(sc, w_ref, EARLY, slice(None), w)
        + slabs(sc, w_ref, MIDDLE, slice(None), middle)
        + slabs(sc, w_ref, LATE, slice(None), late),
        sems,
    )
    place(slots, lhs)
    token[...] = jnp.zeros_like(token)
    for copy in copies[:count]:
        copy.wait()

    def put(band, value):
        acc[:, band] = value

    columns_dot(lhs, w, 0, acc.shape[1], put)
    for copy in copies[count:]:
        copy.wait()


def middle_body(sc, *refs):
    count = len(MIDDLE)
    slots, (w, before, token, acc, lhs) = refs[:count], refs[count:]
    del before, token
    place(slots, lhs)

    def add(band, value):
        acc[:, band] += value

    columns_dot(lhs, w, 0, acc.shape[1], add)


def last_body(tok, wanted, sc, *refs):
    slots, (w, acc, *outs) = refs[: len(LATE)], refs[len(LATE) :]
    outs = outs[-len(wanted) :]
    total = acc.shape[1]
    rows = [pl.ds(pl.multiple_of((sc[2] ^ bits) * tok, 16), tok) for bits in wanted]
    lhs = jnp.concatenate([slots[0][row, :] for row in rows], axis=0)
    for at in range(0, total, TILE):
        band = slice(at, min(at + TILE, total))
        more = jnp.dot(lhs, w[0, :, band], preferred_element_type=jnp.float32)
        for i, (row, out) in enumerate(zip(rows, outs)):
            part = acc[row, band] + more[i * tok : (i + 1) * tok]
            out[:, band] = part.astype(out.dtype)


def by_heads(x, kv, pos, wq, down, up, ku, vu, wo):
    n, nh = lax.axis_size("seq"), lax.axis_size("head")
    s, g, h = lax.axis_index("seq"), lax.axis_index("groups"), lax.axis_index("head")
    sc = jnp.stack([s, g, h]).astype(jnp.int32)
    bf, f32 = jnp.bfloat16, jnp.float32
    tok, depth = x.shape
    heads, nope, kvr = ku.shape
    vdim = vu.shape[2]
    rope = kv.shape[1] - kvr
    rank = down.shape[1]
    rows, cols = wq.shape
    half = rows // 2
    tokens = n * tok
    per = heads // n // CHUNKS
    wide = per * (cols // heads)
    kq, vq, aq = depth // nh, kvr // nh, rank // nh
    extra = tok + aq + (tok + aq) // 3
    at = down.T
    pos2 = pos[None, :]

    def like(*shape, dtype=bf):
        return jax.ShapeDtypeStruct(shape, dtype)

    parts, *units = call(
        functools.partial(pack_body, n, kq, vq, aq, wide, kvr),
        (like(extra, wide), *[like(half, wide)] * (n - 1) * CHUNKS),
        [sc, x, kv, at, pos2, wq],
        hbm=range(1, 6),
        scratch=[
            pltpu.VMEM((tok, kq), bf),
            pltpu.VMEM(kv.shape, bf),
            pltpu.VMEM((aq, rows), bf),
            pltpu.VMEM(pos2.shape, jnp.int32),
            pltpu.VMEM((128, 128), f32),
            pltpu.VMEM((128, 128), f32),
            pltpu.SemaphoreType.DMA((4 + (n - 1) * CHUNKS,)),
        ],
        moved=4 * half * cols,
    )
    def exchange(parts):
        return [lax.ppermute(p, "seq", flipped(n, bits)) for p, bits in zip(parts, partners(n))]

    def join(*groups):
        outs = tuple(like(n - 1, *group[0].shape) for group in groups)
        args = [a for group in groups for a in group]
        return call(join_body, outs, [sc] + args, moved=4 * sum(a.size for a in args))

    merged = (wq.astype(f32) + jnp.dot(down, up, preferred_element_type=f32)).astype(bf)
    _, one, two, three = gather_line(parts)
    by_bits = {1: one, 2: two, 3: three}
    packs = [by_bits[b] for b in partners(n)]
    moved = [exchange(units[: n - 1])]
    held = lax.optimization_barrier((*moved[0], *packs, merged))
    moved[0], packs, merged = list(held[: n - 1]), list(held[n - 1 : -1]), held[-1]
    later = dict(zip(partners(n), units[n - 1 :]))
    later = {b: lax.ppermute(later[b], "seq", flipped(n, b)) for b in (3, 2, 1)}
    moved.append([later[b] for b in partners(n)])
    share, stack = join(moved[0], packs)
    passed = [[lax.ppermute(share, "groups", flipped(2, 1))]]
    across = lax.ppermute(stack, "head", flipped(nh, 2))
    shapes = ((rank, wide), (rows, wide), (per, nope, kvr), (per, kvr, vdim))
    picked = call(
        pick_body,
        tuple(like(*shape) for shape in shapes),
        [sc, up, wq, ku, vu],
        hbm=range(1, 5),
        scratch=[pltpu.SemaphoreType.DMA((4,))],
        moved=4 * sum(math.prod(shape) for shape in shapes),
    )
    across, *rest = lax.optimization_barrier((across, *moved[1], *picked))
    moved[1], picked = rest[: n - 1], rest[n - 1 :]
    stacks = [
        lax.ppermute(stack, "head", flipped(nh, 1)),
        across,
        lax.ppermute(across, "head", flipped(nh, 1)),
    ]
    passed.append([lax.ppermute(p, "groups", flipped(2, 1)) for p in moved[1][:-1]])

    scale = 1.0 / math.sqrt(nope + rope)
    raw = pltpu.VMEM((n * rows, wide), bf)
    cost = dict(
        flops=2 * tokens * per * (depth * wide // per + 2 * nope * kvr + 2 * tokens * kvr),
        moved=4 * n * rows * wide,
    )
    ho, *kept = call(
        functools.partial(attend_first, n, nh, kq, vq, aq, nope, scale),
        (
            like(tokens, per * vdim),
            like(tokens, depth),
            like(tokens, kvr + rope),
            like(rank, n * rows),
            like(tokens, tokens, dtype=f32),
            *(like(*shape) for shape in shapes),
        ),
        [sc, x, kv, at, pos2] + moved[0] + passed[0] + stacks + packs + picked + [up, wq, ku, vu],
        hbm=range(7 + 2 * n + nh, 11 + 2 * n + nh),
        scratch=[pltpu.VMEM((128, 128), f32), raw]
        + [pltpu.SemaphoreType.DMA((4,))],
        **cost,
    )
    moved[1][-1], ho = lax.optimization_barrier((moved[1][-1], ho))
    passed[1].append(lax.ppermute(moved[1][-1], "groups", flipped(2, 1)))
    slots = [gather_line(ho)]
    ho = call(
        functools.partial(attend_next, n, nope, scale),
        like(tokens, per * vdim),
        [sc] + kept[:4] + moved[1] + passed[1] + kept[4:],
        scratch=[raw],
        **cost,
    )
    w4 = wo.reshape(n, CHUNKS, per * vdim, wo.shape[1])
    total = wo.shape[1]
    width = per * vdim

    def room(pieces):
        return [
            pltpu.VMEM((tokens, len(pieces) * width), bf),
            pltpu.VMEM((len(pieces), width, total), bf),
        ]

    def work(pieces):
        rows = len(pieces) * width
        return dict(flops=2 * tokens * rows * total, moved=2 * rows * total)

    def pick(pieces):
        return [slots[c][bits] for bits, c in pieces]

    slots.append([ho])
    acc, token, w_middle, w_late = call(
        early_body,
        (
            like(tokens, total, dtype=f32),
            like(8, 128, dtype=f32),
            like(len(MIDDLE), width, total),
            like(len(LATE), width, total),
        ),
        [sc] + pick(EARLY) + [w4],
        hbm=(1 + len(EARLY),),
        scratch=room(EARLY) + [pltpu.SemaphoreType.DMA((len(EARLY + MIDDLE + LATE),))],
        **work(EARLY),
    )
    *slots[1], token = gather_line(ho, token)
    late = pick(LATE)
    acc = call(
        middle_body,
        like(tokens, total, dtype=f32),
        [sc] + pick(MIDDLE) + [w_middle, acc, token],
        scratch=room(MIDDLE)[:1],
        alias={2 + len(MIDDLE): 0},
        **work(MIDDLE),
    )
    def last(*wanted, after=()):
        return call(
            functools.partial(last_body, tok, [bits for bits, _ in wanted]),
            tuple(like(tok, total, dtype=kind) for _, kind in wanted),
            [sc] + late + [w_late, acc, *after],
            flops=2 * len(wanted) * tok * width * total,
            moved=8 * len(wanted) * tok * total,
        )

    (send_away,) = last((3, bf))
    keep_away, send_home, keep_home = last((2, f32), (1, bf), (0, f32), after=[send_away])
    away = keep_away + lax.ppermute(send_away, "head", flipped(nh, 1)).astype(f32)
    got = lax.ppermute(away.astype(bf), "head", flipped(nh, 2))
    home = keep_home + lax.ppermute(send_home, "head", flipped(nh, 1)).astype(f32)
    return merged, (home + got.astype(f32)).astype(bf)


def fits(mesh, shapes):
    n, nh = mesh.shape["seq"], mesh.shape["head"]
    x, kv, _, wq, down, _, ku, vu, wo = shapes
    tok, kvr, rank = x[0], ku[2], down[1]
    if mesh.shape["groups"] != 2 or n != 4 or nh != 4 or CHUNKS != 2 or ku[0] % (n * CHUNKS):
        return False
    wide = wq[1] // n // CHUNKS
    return (
        (tok + rank // nh) % 48 == 0
        and tok % 16 == 0
        and tok + 3 <= 128
        and rank <= 128
        and rank // nh % 16 == 0
        and kv[1] - kvr == rank
        and kvr // nh == 128
        and x[1] // nh == wide
        and down[0] == wide
        and wide == 3 * 128
        and wo[1] % 128 == 0
    )


def solution(mesh):
    placed = (
        P(("groups", "seq"), None),
        P(("groups", "seq"), None),
        P(("groups", "seq")),
        P("seq", "head"),
        P(("groups", "seq"), None),
        P("groups", "head"),
        P("head", None, None),
        P("head", None, None),
        P("head", "seq"),
    )

    def local(*args):
        chosen = by_heads if fits(mesh, [a.shape for a in args]) else on_device
        return chosen(*args)

    return jax.shard_map(
        local,
        mesh=mesh,
        in_specs=placed,
        out_specs=(P(("groups", "seq"), "head"), P(("groups", "head"), "seq")),
        check_vma=False,
    )
```
